32 devices in a mesh: groups: 2 (over y), adapter: 8 (over z, x), tensor: 2 (over core).
Axes of the slice: x: 2, y: 2, z: 4, core: 2. Of those that a mesh axis runs over, the one named last changes fastest.
Arguments:
- layer_input: bfloat16 [256, 8192], P(('groups', 'adapter')), parts along dimension 0, may hold values from -6 to 6
- input_norm_gain: float32 [8192], replicated, may hold values from 0.5 to 1.5
- query_projection: bfloat16 [8192, 512], P(None, 'tensor'), may hold values from -0.0625 to 0.0625
- key_projection: bfloat16 [8192, 128], P(None, 'tensor'), may hold values from -0.0625 to 0.0625
- value_projection: bfloat16 [8192, 128], P(None, 'tensor'), may hold values from -0.0625 to 0.0625
- output_projection: bfloat16 [512, 8192], P('tensor'), may hold values from -1 to 1
- cached_key_rows: bfloat16 [256, 32, 128], P(('groups', 'adapter')), parts along dimension 0, may hold values from -120 to 120
- cached_value_rows: bfloat16 [256, 32, 128], P(('groups', 'adapter')), parts along dimension 0, may hold values from -6 to 6
- request_adapter: int32 [256, 1], P(('groups', 'adapter')), parts along dimension 0, may hold values from 0 to 7; in each aligned block of 16 rows (0 to 15, 16 to 31, ...) at most 4 rows name the same one
- adapter_row_table: int32 [8], replicated, may hold values from 0 to 7, each once
- cached_length: int32 [256], P(('groups', 'adapter')), parts along dimension 0, may hold values from 1 to 32, as said below
- projection_adapter_down: bfloat16 [8, 8192, 192], P('adapter', 'tensor'), may hold values from -0.0625 to 0.0625
- query_adapter_up: bfloat16 [8, 64, 512], P('adapter', None, 'tensor'), may hold values from -0.75 to 0.75
- key_value_adapter_up: bfloat16 [8, 2, 64, 128], P('adapter', None, None, 'tensor'), may hold values from -0.75 to 0.75
- output_adapter_down: bfloat16 [8, 512, 64], P('adapter', 'tensor'), may hold values from -1 to 1
- output_adapter_up: bfloat16 [8, 64, 8192], P('adapter', None, 'tensor'), may hold values from -0.75 to 0.75
Outputs:
- block_out: bfloat16 [256, 8192], P(('groups', 'adapter'), 'tensor'), parts along dimension 0
The draws below stay inside these ranges and needn't reach their ends.
There are 2 independent parts, one for each index of `groups`. The reference program is written for one: setup_inputs(seed, part) draws one part's arguments, and reference() takes and returns one part's arrays. A program takes and returns all parts, laid end to end along the dimension named above; an argument that names none is the same for every part. Nothing has to cross between parts.
Inputs may be any that keep to these rules, and one draw needn't show every extreme that they name: `request_adapter`: among the requests of one device (aligned blocks of 16 rows) no adapter is named more than 4 times, a bound that some block reaches. A permutation: adapter j's weights are row adapter_row_table[j] of the adapter arrays. `cached_length`: the requests of every device include one whose cache holds exactly 32 positions.
All inputs are finite; a program needn't handle non-finite values.
Results may differ from the reference program's by a relative error of at most 0.012.
The reference program's roundings to bfloat16 on the way count: a program that leaves them out, or rounds other values in their place, can miss the bound.
Values may be sent and summed in bfloat16 or wider, within the bound.
No kernel may reach another device: no remote copies, remote signals or barrier semaphores. Data moves between devices by JAX's collectives and lax.ppermute only.
A program may use at most 64 MiB of HBM per device.

```python
import math
import jax
import jax.numpy as jnp
import numpy as np
from jax import lax

MODEL_WIDTH = 8192
HEAD_SIZE = 128
QUERY_HEADS = 4
ADAPTER_RANK = 64
R_DEV = 16
L = 32
ADAPTER_COUNT = 8
REQUESTS = 128
CAP = 4


def draw_cached_key_rows(key, part):
    key = jax.random.fold_in(key, 11)
    first_key, second_key = jax.random.split(key)
    spread = math.log(3.0)
    scales = jnp.exp(jax.random.uniform(second_key, (REQUESTS, L, 1), jnp.float32) * spread)
    entries = jax.random.truncated_normal(first_key, -4.0, 4.0, (REQUESTS, L, HEAD_SIZE), jnp.float32)
    return (entries * scales).astype(jnp.bfloat16)


def draw_cached_length(key, part):
    key = jax.random.fold_in(key, 23)
    first_key, second_key = jax.random.split(key)
    drawn = jax.random.randint(first_key, (REQUESTS,), 1, L + 1, dtype=jnp.int32)
    chosen = jax.random.randint(second_key, (REQUESTS // R_DEV,), 0, R_DEV, dtype=jnp.int32)
    places = jnp.arange(REQUESTS, dtype=jnp.int32)
    filled = places % R_DEV == jnp.repeat(chosen, R_DEV)
    return jnp.where(filled, L, drawn).astype(jnp.int32)


def block_levels(stream_key, extent, shards, smallest, largest):
    gain = 1.0
    for position, parts in shards:
        draws = jax.random.uniform(jax.random.fold_in(jax.random.fold_in(stream_key, 6), position), (parts,), jnp.float32, smallest / len(shards), largest / len(shards))
        gain = gain * jnp.repeat(jnp.exp(draws), extent[position] // parts).reshape((-1,) + (1,) * (len(extent) - 1 - position))
    return gain


def assign_block(own_key, own, number, rows, number_of, top, bound, lean):
    order = jax.random.permutation(own_key, number_of)
    packed, common = load_shares(number_of, rows * top, bound, lean, True), load_shares(number_of, rows * top, bound, lean, False)
    places = jnp.arange(number_of)

    def named(tallies, turn):
        used = int((tallies > 0).sum())
        fixed = max(1, used // 4)
        shifted = fixed + (places - fixed + turn * (used - fixed)) % max(1, number_of - fixed)
        return jnp.zeros((number_of,), jnp.int32).at[order[jnp.where(places < fixed, places, shifted)]].set(jnp.asarray(tallies, jnp.int32))

    tallies = jnp.where(number % 4 == 0, named(packed, number // 4), named(common, number - number // 4 - 1))
    mixed = jax.random.permutation(jax.random.fold_in(own, 3), number_of)
    giver, taker = mixed[0:number_of // 2 * 2:2], mixed[1:number_of // 2 * 2:2]
    slack = jnp.minimum(tallies[giver] - 1, bound - tallies[taker]) // 2
    slack = jnp.where((giver == order[0]) | (taker == order[0]) | (tallies[taker] == 0), 0, jnp.maximum(slack, 0))
    shifted = jax.random.randint(jax.random.fold_in(own, 4), (number_of // 2,), 0, 1 << 20) % (slack + 1)
    tallies = tallies.at[giver].add(-shifted).at[taker].add(shifted)
    items = jnp.searchsorted(jnp.cumsum(tallies), jnp.arange(rows * top), side="right").astype(jnp.int32)
    grid = items.reshape(top, rows).T
    grid = grid[jax.random.permutation(jax.random.fold_in(own, 1), rows)]
    turn = jax.random.randint(jax.random.fold_in(own, 2), (rows, 1), 0, top)
    return jnp.take_along_axis(grid, (jnp.arange(top)[None, :] + turn) % top, axis=1)


def load_shares(count, total, most, lean, full):
    weights = [(1 << 20) // math.isqrt(grade ** lean) + 1 for grade in range(1, count + 1)]
    largest = most if full else min(most, max(-(-total // count), total * weights[0] // sum(weights)))
    least = 1 if total - largest >= count - 1 else 0
    holding, rest = [largest] + [least] * (count - 1), total - largest - least * (count - 1)
    while rest > 0:
        candidates = [i for i in range(1, count) if holding[i] < largest] or [i for i in range(1, count) if holding[i] < most]
        pool, left = sum([weights[i] for i in candidates]), rest
        for i in candidates:
            addition = min(most - holding[i], max(1, left * weights[i] // pool), rest)
            holding[i] = holding[i] + addition
            rest = rest - addition
    return np.array(holding)


def bell_draw(stream_key, shape, width, limit, shards=(), kind=jnp.bfloat16):
    result = width * jax.random.normal(stream_key, shape, jnp.float32)
    if shards:
        result = result * block_levels(stream_key, shape, shards, -0.22, 0.18)
    return jnp.clip(result, -limit, limit).astype(kind)


def setup_inputs(seed: int = 0, part: int = 0) -> dict:
    seeds = jax.random.split(jax.random.key(seed), 17)
    part_splits = jax.random.split(jax.random.fold_in(seeds[16], part), 17)
    layer_input = bell_draw(part_splits[0], (REQUESTS, MODEL_WIDTH), 1.0, 6.0, ((0, 8),))
    input_norm_gain = jnp.clip(1.0 + 0.1 * jax.random.normal(seeds[1], (MODEL_WIDTH,), jnp.float32), 0.5, 1.5)
    query_projection = bell_draw(seeds[2], (MODEL_WIDTH, QUERY_HEADS * HEAD_SIZE), MODEL_WIDTH ** -0.5, 0.0625, ((1, 2),))
    key_projection = bell_draw(seeds[3], (MODEL_WIDTH, HEAD_SIZE), MODEL_WIDTH ** -0.5, 0.0625, ((1, 2),))
    value_projection = bell_draw(seeds[4], (MODEL_WIDTH, HEAD_SIZE), MODEL_WIDTH ** -0.5, 0.0625, ((1, 2),))
    output_projection = bell_draw(seeds[5], (QUERY_HEADS * HEAD_SIZE, MODEL_WIDTH), (QUERY_HEADS * HEAD_SIZE // 16) ** -0.5, 1.0, ((0, 2),))
    cached_key_rows = draw_cached_key_rows(jax.random.fold_in(jax.random.fold_in(seeds[16], part), 71), part)
    cached_value_rows = bell_draw(part_splits[7], (REQUESTS, L, HEAD_SIZE), 1.0, 6.0, ((0, 8),))
    request_adapter_keys = jax.random.split(jax.random.fold_in(part_splits[8], 1), REQUESTS // R_DEV)
    request_adapter_turns = jax.random.permutation(jax.random.fold_in(part_splits[8], 3), REQUESTS // R_DEV)
    request_adapter = jax.vmap(lambda own, number: assign_block(jax.random.fold_in(part_splits[8], 2), own, number, R_DEV, ADAPTER_COUNT, 1, CAP, 2))(request_adapter_keys, request_adapter_turns).reshape((REQUESTS, 1))
    adapter_row_table = jax.random.permutation(seeds[9], ADAPTER_COUNT).astype(jnp.int32)
    cached_length = draw_cached_length(jax.random.fold_in(jax.random.fold_in(seeds[16], part), 71), part)
    projection_adapter_down = bell_draw(seeds[11], (ADAPTER_COUNT, MODEL_WIDTH, 3 * ADAPTER_RANK), MODEL_WIDTH ** -0.5, 0.0625, ((0, 8), (1, 2)))
    query_adapter_up = bell_draw(seeds[12], (ADAPTER_COUNT, ADAPTER_RANK, QUERY_HEADS * HEAD_SIZE), ADAPTER_RANK ** -0.5, 0.75, ((0, 8), (2, 2)))
    key_value_adapter_up = bell_draw(seeds[13], (ADAPTER_COUNT, 2, ADAPTER_RANK, HEAD_SIZE), ADAPTER_RANK ** -0.5, 0.75, ((0, 8), (3, 2)))
    output_adapter_down = bell_draw(seeds[14], (ADAPTER_COUNT, QUERY_HEADS * HEAD_SIZE, ADAPTER_RANK), (QUERY_HEADS * HEAD_SIZE // 16) ** -0.5, 1.0, ((0, 8), (1, 2)))
    output_adapter_up = bell_draw(seeds[15], (ADAPTER_COUNT, ADAPTER_RANK, MODEL_WIDTH), ADAPTER_RANK ** -0.5, 0.75, ((0, 8), (2, 2)))
    return dict(layer_input=layer_input, input_norm_gain=input_norm_gain, query_projection=query_projection, key_projection=key_projection, value_projection=value_projection, output_projection=output_projection, cached_key_rows=cached_key_rows, cached_value_rows=cached_value_rows, request_adapter=request_adapter, adapter_row_table=adapter_row_table, cached_length=cached_length, projection_adapter_down=projection_adapter_down, query_adapter_up=query_adapter_up, key_value_adapter_up=key_value_adapter_up, output_adapter_down=output_adapter_down, output_adapter_up=output_adapter_up)


EPSILON = 1e-05
THETA = 500000.0

def rotary(input_batch, positions):
    halfway = input_batch.shape[-1] // 2
    frequency = THETA ** (-jnp.arange(halfway, dtype=jnp.float32) / halfway)
    angles = positions.astype(jnp.float32)[:, None, None] * frequency[None, None, :]
    cosine = jnp.cos(angles)
    sine = jnp.sin(angles)
    leading = input_batch[..., :halfway]
    trailing = input_batch[..., halfway:]
    return jnp.concatenate([leading * cosine - trailing * sine, trailing * cosine + leading * sine], axis=-1)

def rms_normed(layer_input, input_norm_gain):
    floats = layer_input.astype(jnp.float32)
    mean_square = lax.optimization_barrier(jnp.mean(floats * floats, axis=1, keepdims=True))
    return (floats * lax.rsqrt(mean_square + EPSILON) * input_norm_gain[None, :]).astype(jnp.bfloat16)

def blockwise(input_batch, adapter_slots, one_request):

    def one_block(pair):
        return jax.vmap(one_request)(pair[0], pair[1])
    requests = input_batch.shape[0]
    blocked = (input_batch.reshape(requests // R_DEV, R_DEV, input_batch.shape[1]), adapter_slots.reshape(requests // R_DEV, R_DEV))
    outcome = lax.map(one_block, blocked)
    return outcome.reshape(requests, -1)

def projection_adapter_result(input_batch, adapter_slots, projection_adapter_down, query_adapter_up, key_value_adapter_up):

    def one_request(single_input, adapter_slot):
        rank_activations = jnp.dot(single_input, projection_adapter_down[adapter_slot], preferred_element_type=jnp.float32).astype(jnp.bfloat16).astype(jnp.float32)
        query_update = jnp.dot(rank_activations[:ADAPTER_RANK], query_adapter_up[adapter_slot].astype(jnp.float32))
        key_value_update = jnp.einsum('pq,pqf->pf', rank_activations[ADAPTER_RANK:].reshape(2, ADAPTER_RANK), key_value_adapter_up[adapter_slot].astype(jnp.float32))
        return jnp.concatenate([query_update, key_value_update.reshape(-1)]).astype(jnp.bfloat16)
    return blockwise(input_batch, adapter_slots, one_request)

def output_adapter_result(input_batch, adapter_slots, first, second):

    def one_request(single_input, adapter_slot):
        rank_activations = jnp.dot(single_input, first[adapter_slot], preferred_element_type=jnp.float32).astype(jnp.bfloat16)
        return jnp.dot(rank_activations, second[adapter_slot], preferred_element_type=jnp.float32).astype(jnp.bfloat16)
    return blockwise(input_batch, adapter_slots, one_request)

def reference(layer_input, input_norm_gain, query_projection, key_projection, value_projection, output_projection, cached_key_rows, cached_value_rows, request_adapter, adapter_row_table, cached_length, projection_adapter_down, query_adapter_up, key_value_adapter_up, output_adapter_down, output_adapter_up):
    requests = layer_input.shape[0]
    qcols = QUERY_HEADS * HEAD_SIZE
    normalized_input = rms_normed(layer_input, input_norm_gain)
    adapter_slots = adapter_row_table[request_adapter[:, 0]].astype(jnp.int32)
    projected = jnp.dot(normalized_input, jnp.concatenate([query_projection, key_projection, value_projection], axis=1), preferred_element_type=jnp.float32)
    projection_updates = projection_adapter_result(normalized_input, adapter_slots, projection_adapter_down, query_adapter_up, key_value_adapter_up).astype(jnp.float32)
    combined = projected + projection_updates
    queries = rotary(combined[:, :qcols].reshape(requests, QUERY_HEADS, HEAD_SIZE), cached_length).astype(jnp.bfloat16)
    own_keys = rotary(combined[:, qcols:qcols + HEAD_SIZE].reshape(requests, 1, HEAD_SIZE), cached_length)[:, 0].astype(jnp.bfloat16)
    own_values = combined[:, qcols + HEAD_SIZE:].astype(jnp.bfloat16)
    key_table = jnp.concatenate([cached_key_rows, own_keys[:, None]], axis=1).astype(jnp.float32)
    value_table = jnp.concatenate([cached_value_rows, own_values[:, None]], axis=1).astype(jnp.float32)
    scores = jnp.einsum('nhd,nld->nhl', queries.astype(jnp.float32), key_table) / math.sqrt(HEAD_SIZE)
    places = jnp.arange(L + 1, dtype=jnp.int32)
    visible = (places[None, :] < cached_length[:, None]) | (places[None, :] == L)
    scores = jnp.where(visible[:, None, :], scores, -jnp.inf)
    highest = lax.optimization_barrier(jnp.max(scores, axis=2, keepdims=True))
    raised = jnp.exp(scores - highest)
    weights = (raised / lax.optimization_barrier(jnp.sum(raised, axis=2, keepdims=True))).astype(jnp.bfloat16)
    attention_output = jnp.einsum('nhl,nld->nhd', weights.astype(jnp.float32), value_table)
    attention_output = attention_output.reshape(requests, qcols).astype(jnp.bfloat16)
    output_updates = output_adapter_result(attention_output, adapter_slots, output_adapter_down, output_adapter_up).astype(jnp.float32)
    projected_out = jnp.dot(attention_output, output_projection, preferred_element_type=jnp.float32)
    return (projected_out + output_updates).astype(jnp.bfloat16)
```

```python
import functools
import math

import jax
import jax.numpy as jnp
from jax import lax
from jax.experimental import pallas as pl
from jax.experimental.pallas import tpu as pltpu
from jax.sharding import PartitionSpec as P

HEAD_SIZE = 128
LANES = 128
EPSILON = 1e-05
THETA = 500000.0
BF16 = jnp.bfloat16
F32 = jnp.float32
SWAP = [(0, 1), (1, 0)]
VMEM_LIMIT = 40 * 1024 * 1024


def nn(a, b):
    return lax.dot_general(a, b, (((1,), (0,)), ((), ())), preferred_element_type=F32)


def nt(a, b):
    return lax.dot_general(a, b, (((1,), (1,)), ((), ())), preferred_element_type=F32)


def iota(shape, dim):
    return lax.broadcasted_iota(jnp.int32, shape, dim)


def ones_where(condition):
    return jnp.where(condition, 1.0, 0.0).astype(BF16)


def owner_and_standing(named, table):
    requests, adapters = named.shape[1], table.shape[1]
    table_column = jnp.sum(
        jnp.where(iota((adapters, adapters), 0) == iota((adapters, adapters), 1), table, 0),
        axis=1,
        keepdims=True,
    )
    owner = jnp.sum(
        jnp.where(iota((adapters, requests), 0) == named, table_column, 0), axis=0, keepdims=True
    )
    square = (requests, requests)
    owner_column = jnp.sum(
        jnp.where(iota(square, 0) == iota(square, 1), owner, 0), axis=1, keepdims=True
    )
    earlier = (owner_column == owner) & (iota(square, 0) < iota(square, 1))
    standing = jnp.sum(jnp.where(earlier, 1, 0), axis=0, keepdims=True)
    return owner, standing


def pack_kernel(capacity, x_ref, gain_ref, k_ref, v_ref, named_ref, table_ref, length_ref, out_ref, flat_ref, spread_ref):
    core = lax.axis_index("tensor")
    requests, width = x_ref.shape
    half = width // 2
    positions = k_ref.shape[0] // requests
    per_owner = 2 * capacity
    rows = out_ref.shape[0]
    owner, standing = owner_and_standing(named_ref[...], table_ref[...])
    own_slot = standing % 2 == core
    place = owner * per_owner + standing // 2
    x_row = place + jnp.where(own_slot, 0, capacity // 2)
    k_row = jnp.where(own_slot, owner * per_owner + capacity + 2 * (standing // 2), -2)
    order = iota((rows, requests), 0)
    put_x = ones_where(order == x_row)
    put_k = ones_where(order == k_row)
    put_v = ones_where(order == k_row + 1)

    floats = x_ref[...].astype(F32)
    scale = lax.rsqrt(jnp.mean(floats * floats, axis=1, keepdims=True) + EPSILON)
    mine = pl.ds(pl.multiple_of(core * half, half), half)
    flat_ref[0:requests, :] = (x_ref[:, mine].astype(F32) * scale * gain_ref[:, mine]).astype(BF16)
    for first, source in ((requests, k_ref), (2 * requests, v_ref)):
        spread_ref[...] = source[...].astype(F32)
        for p in range(positions):
            flat_ref[first : first + requests, p * LANES : (p + 1) * LANES] = spread_ref[
                pl.ds(p, requests, stride=positions), :
            ].astype(BF16)
    put = jnp.concatenate([put_x, put_k, put_v], axis=1)
    step = 512
    for c in range(0, half, step):
        out_ref[:, c : c + step] = nn(put, flat_ref[:, c : c + step]).astype(BF16)
    square = (requests, requests)
    length_column = jnp.sum(
        jnp.where(iota(square, 0) == iota(square, 1), length_ref[...], 0), axis=1, keepdims=True
    )
    lengths = jnp.broadcast_to(length_column.astype(F32), (requests, LANES)).astype(BF16)
    out_ref[:, half:] = nn(put_x, lengths).astype(BF16)


def project_kernel(capacity, owners, buf_ref, wq_ref, wq_other_ref, kv_ref, kv_other_ref, down_ref, mine_ref, theirs_ref, sums_ref):
    core = lax.axis_index("tensor")
    half = wq_other_ref.shape[0]
    per_owner = 2 * capacity
    here = capacity // 2
    buf = buf_ref[:, :half]
    rows = pl.ds(pl.multiple_of(core * half, half), half)
    ranks = nt(buf, down_ref[...])
    spare = jnp.zeros((buf.shape[0], -ranks.shape[1] % LANES), F32)
    parts = [
        nn(buf, wq_ref[rows, :]),
        nn(buf, wq_other_ref[...]),
        nt(buf, kv_ref[:, rows]),
        nt(buf, kv_other_ref[...]),
        jnp.concatenate([ranks, spare], axis=1),
    ]
    tile = 0
    for part in parts:
        for c in range(0, part.shape[1], LANES):
            sums_ref[...] = part[:, c : c + LANES]
            columns = slice(tile * LANES, (tile + 1) * LANES)
            for i in range(here):
                to = slice(i * owners, (i + 1) * owners)
                mine_ref[to, columns] = sums_ref[pl.ds(i, owners, stride=per_owner), :]
                theirs_ref[to, columns] = sums_ref[pl.ds(here + i, owners, stride=per_owner), :]
            tile += 1


def unpack_kernel(capacity, owners, buf_ref, k_ref, v_ref, length_ref, cosine_ref, sine_ref):
    rows = buf_ref.shape[0]
    slots = owners * capacity // 2
    positions = k_ref.shape[0] // slots
    half = positions * LANES
    per_owner = 2 * capacity
    slot = iota((slots, rows), 0)
    base = (slot % owners) * per_owner
    order = iota((slots, rows), 1)
    pick_x = ones_where(order == base + slot // owners)
    pick_k = ones_where(order == base + capacity + 2 * (slot // owners))
    pick_v = ones_where(order == base + capacity + 2 * (slot // owners) + 1)
    pick = jnp.concatenate([pick_k, pick_v], axis=0)
    step = 512
    for c in range(0, half, step):
        both = nn(pick, buf_ref[:, c : c + step]).astype(BF16)
        for j in range(step // LANES):
            p = c // LANES + j
            tile = both[:, j * LANES : (j + 1) * LANES]
            k_ref[p * slots : (p + 1) * slots, :] = tile[:slots]
            v_ref[p * slots : (p + 1) * slots, :] = tile[slots:]
    length = nn(pick_x, buf_ref[:, half:])
    length_ref[...] = length
    halfway = HEAD_SIZE // 2
    lane = iota((slots, LANES), 1)
    exponent = (lane % halfway).astype(F32) * (-math.log(THETA) / halfway)
    angle = length * jnp.exp(exponent)
    cosine_ref[...] = jnp.cos(angle)
    sine = jnp.sin(angle)
    sine_ref[...] = jnp.where(lane < halfway, -sine, sine)


def attend_kernel(mine_ref, theirs_ref, up_ref, k_ref, v_ref, length_ref, cosine_ref, sine_ref, out_ref):
    core = lax.axis_index("tensor")
    slots = mine_ref.shape[0]
    ucols = up_ref.shape[1]
    kvcols = LANES
    qcols = (ucols - 2 * kvcols) // 2
    heads = 2 * qcols // HEAD_SIZE
    halfway = HEAD_SIZE // 2
    mine = mine_ref[...]
    theirs = theirs_ref[...]
    swapped = jnp.concatenate(
        [
            theirs[:, qcols : 2 * qcols],
            theirs[:, :qcols],
            theirs[:, 2 * qcols + kvcols : ucols],
            theirs[:, 2 * qcols : 2 * qcols + kvcols],
            theirs[:, ucols:],
        ],
        axis=1,
    )
    sums = mine + swapped
    ranks = sums[:, ucols : ucols + up_ref.shape[0]].astype(BF16)
    deltas = nn(ranks, up_ref[...]).astype(BF16).astype(F32)
    combined = sums[:, :ucols] + deltas
    cosine, sine = cosine_ref[...], sine_ref[...]

    def rotate(part):
        return part * cosine + pltpu.roll(part, halfway, 1) * sine

    queries = jnp.concatenate(
        [rotate(combined[:, h * HEAD_SIZE : (h + 1) * HEAD_SIZE]) for h in range(heads)], axis=0
    ).astype(BF16)
    kv_mine = combined[:, 2 * qcols : 2 * qcols + kvcols]
    kv_theirs = combined[:, 2 * qcols + kvcols :]
    leading = jnp.where(core == 0, kv_mine, kv_theirs)
    trailing = jnp.where(core == 0, kv_theirs, kv_mine)
    first = iota((slots, LANES), 1) < halfway
    own_key = rotate(jnp.where(first, leading, pltpu.roll(trailing, halfway, 1))).astype(BF16)
    own_value = jnp.where(first, pltpu.roll(leading, halfway, 1), trailing).astype(BF16)

    cached = k_ref.shape[0]
    rows = heads * slots
    shrink = math.sqrt(HEAD_SIZE)
    length = jnp.concatenate([length_ref[:, 0:1]] * heads, axis=0).astype(jnp.int32)
    column = iota((rows, cached), 1)
    visible = (column % slots == iota((rows, cached), 0) % slots) & (column // slots < length)
    own = iota((rows, slots), 1) == iota((rows, slots), 0) % slots
    scores = jnp.where(visible, nt(queries, k_ref[...]) / shrink, -jnp.inf)
    own_scores = jnp.where(own, nt(queries, own_key) / shrink, -jnp.inf)
    highest = jnp.maximum(
        jnp.max(scores, axis=1, keepdims=True), jnp.max(own_scores, axis=1, keepdims=True)
    )
    raised = jnp.exp(scores - highest)
    own_raised = jnp.exp(own_scores - highest)
    total = jnp.sum(raised, axis=1, keepdims=True) + jnp.sum(own_raised, axis=1, keepdims=True)
    weights = (raised / total).astype(BF16)
    own_weights = (own_raised / total).astype(BF16)
    attended = (nn(weights, v_ref[...]) + nn(own_weights, own_value)).astype(BF16)
    for h in range(heads):
        out_ref[:, h * HEAD_SIZE : (h + 1) * HEAD_SIZE] = attended[h * slots : (h + 1) * slots]


def output_kernel(capacity, owners, mine_ref, theirs_ref, wo_ref, wo_other_ref, down_ref, down_other_ref, up_ref, out_ref):
    core = lax.axis_index("tensor")
    slots, cols = mine_ref.shape
    hcols = cols // 2
    half = out_ref.shape[1]
    rows = owners * capacity
    theirs = theirs_ref[...]
    rows_in = jnp.concatenate(
        [mine_ref[...], jnp.concatenate([theirs[:, hcols:], theirs[:, :hcols]], axis=1)], axis=0
    )
    out_row = iota((rows, 2 * slots), 0)
    standing = out_row % capacity
    source = (
        jnp.where(standing % 2 == core, 0, slots) + (standing // 2) * owners + out_row // capacity
    )
    arrange = ones_where(iota((rows, 2 * slots), 1) == source)
    attended = nn(arrange, rows_in).astype(BF16)
    left, right = attended[:, :hcols], attended[:, hcols:]
    ranks = (nt(left, down_ref[...]) + nt(right, down_other_ref[...])).astype(BF16)
    step = 512
    for c in range(0, half, step):
        columns = pl.ds(pl.multiple_of(core * half + c, step), step)
        delta = nn(ranks, up_ref[:, c : c + step]).astype(BF16).astype(F32)
        terms = nn(left, wo_ref[:, columns]) + nn(right, wo_other_ref[:, c : c + step])
        out_ref[:, c : c + step] = (terms + delta).astype(BF16)


def pick_kernel(capacity, back_ref, named_ref, table_ref, out_ref):
    rows, half = back_ref.shape
    requests = out_ref.shape[0]
    owner, standing = owner_and_standing(named_ref[...], table_ref[...])
    place = ones_where(iota((rows, requests), 0) == owner * capacity + standing)
    step = 512
    for c in range(0, half, step):
        out_ref[:, c : c + step] = lax.dot_general(
            place,
            back_ref[:, c : c + step],
            (((0,), (0,)), ((), ())),
            preferred_element_type=F32,
        ).astype(BF16)


def call(kernel, outs, scratch=(), flops=0, moved=0):
    many = isinstance(outs, (list, tuple))
    spec = pl.BlockSpec(memory_space=pltpu.VMEM)
    return lambda *args: pl.pallas_call(
        kernel,
        out_shape=outs,
        in_specs=[spec] * len(args),
        out_specs=[spec] * len(outs) if many else spec,
        scratch_shapes=list(scratch),
        compiler_params=pltpu.CompilerParams(vmem_limit_bytes=VMEM_LIMIT),
        cost_estimate=pl.CostEstimate(flops=flops, bytes_accessed=moved, transcendentals=0),
    )(*args)


def body(
    layer_input,
    input_norm_gain,
    query_projection,
    key_projection,
    value_projection,
    output_projection,
    cached_key_rows,
    cached_value_rows,
    request_adapter,
    adapter_row_table,
    cached_length,
    projection_adapter_down,
    query_adapter_up,
    key_value_adapter_up,
    output_adapter_down,
    output_adapter_up,
):
    requests, width = layer_input.shape
    owners = lax.axis_size("adapter")
    adapters = adapter_row_table.shape[0]
    positions = cached_key_rows.shape[1]
    half = width // 2
    capacity = max(2, 2 * ((requests + adapters - 1) // adapters))
    rows = owners * 2 * capacity
    slots = owners * capacity // 2
    core = lax.axis_index("tensor")
    named = request_adapter.reshape(1, requests)
    table = adapter_row_table.reshape(1, adapters)
    shape = jax.ShapeDtypeStruct

    packed = call(
        functools.partial(pack_kernel, capacity),
        shape((rows, half + LANES), BF16),
        [pltpu.VMEM((3 * requests, half), BF16), pltpu.VMEM((positions * requests, LANES), F32)],
    )(
        layer_input,
        input_norm_gain.reshape(1, width),
        cached_key_rows.reshape(requests * positions, HEAD_SIZE),
        cached_value_rows.reshape(requests * positions, HEAD_SIZE),
        named,
        table,
        cached_length.reshape(1, requests),
    )
    arrived = lax.all_to_all(
        packed.reshape(owners, 2 * capacity, half + LANES),
        "adapter",
        split_axis=0,
        concat_axis=0,
        tiled=True,
    ).reshape(rows, half + LANES)

    other = (1 - core) * half
    qcols = query_projection.shape[1]
    kv = jnp.concatenate([key_projection.T, value_projection.T], axis=0)
    kvcols = kv.shape[0]
    wq_other = lax.ppermute(
        lax.dynamic_slice(query_projection, (other, 0), (half, qcols)), "tensor", SWAP
    )
    kv_other = lax.ppermute(lax.dynamic_slice(kv, (0, other), (kvcols, half)), "tensor", SWAP)
    wo_other = lax.ppermute(
        lax.dynamic_slice(output_projection, (0, other), (output_projection.shape[0], half)),
        "tensor",
        SWAP,
    )
    query_up = query_adapter_up[0]
    rank = query_up.shape[0]
    kv_up = key_value_adapter_up[0]
    hcols = kv_up.shape[2]
    out_down = output_adapter_down[0].T
    small = jnp.concatenate([query_up, kv_up[0], kv_up[1], out_down], axis=1)
    small_other = lax.ppermute(small, "tensor", SWAP)
    out_down_other = small_other[:, qcols + 2 * hcols :]

    def zeros(columns):
        return jnp.zeros((rank, columns), BF16)

    def kv_rows(which):
        blocks = []
        for source in (small, small_other):
            for one in range(2):
                first = qcols + one * hcols
                blocks.append(source[:, first : first + hcols] if one == which else zeros(hcols))
        return jnp.concatenate([zeros(2 * qcols)] + blocks, axis=1)

    up = jnp.concatenate(
        [
            jnp.concatenate(
                [small[:, :qcols], small_other[:, :qcols], zeros(4 * hcols)], axis=1
            ),
            kv_rows(0),
            kv_rows(1),
        ],
        axis=0,
    )
    down = projection_adapter_down[0].T
    ucols = 2 * qcols + 2 * kvcols
    pcols = ucols + (down.shape[0] + LANES - 1) // LANES * LANES

    mine, theirs = call(
        functools.partial(project_kernel, capacity, owners),
        [shape((slots, pcols), F32), shape((slots, pcols), F32)],
        [pltpu.VMEM((rows, LANES), F32)],
    )(arrived, query_projection, wq_other, kv, kv_other, down)
    theirs = lax.ppermute(theirs, "tensor", SWAP)
    keys, values, lengths, cosine, sine = call(
        functools.partial(unpack_kernel, capacity, owners),
        [shape((slots * positions, HEAD_SIZE), BF16)] * 2 + [shape((slots, LANES), F32)] * 3,
    )(arrived)
    attended = call(attend_kernel, shape((slots, 2 * qcols), BF16))(
        mine, theirs, up, keys, values, lengths, cosine, sine
    )
    attended_other = lax.ppermute(attended, "tensor", SWAP)
    finished = call(
        functools.partial(output_kernel, capacity, owners),
        shape((owners * capacity, half), BF16),
    )(
        attended,
        attended_other,
        output_projection,
        wo_other,
        out_down,
        out_down_other,
        output_adapter_up[0],
    )
    back = lax.all_to_all(
        finished.reshape(owners, capacity, half), "adapter", split_axis=0, concat_axis=0, tiled=True
    ).reshape(owners * capacity, half)
    return call(functools.partial(pick_kernel, capacity), shape((requests, half), BF16))(
        back, named, table
    )


def solution(mesh):
    placed = (
        P(("groups", "adapter"), None),
        P(),
        P(None, "tensor"),
        P(None, "tensor"),
        P(None, "tensor"),
        P("tensor", None),
        P(("groups", "adapter"), None, None),
        P(("groups", "adapter"), None, None),
        P(("groups", "adapter"), None),
        P(),
        P(("groups", "adapter")),
        P("adapter", "tensor", None),
        P("adapter", None, "tensor"),
        P("adapter", None, None, "tensor"),
        P("adapter", "tensor", None),
        P("adapter", None, "tensor"),
    )
    return jax.shard_map(
        body,
        mesh=mesh,
        in_specs=placed,
        out_specs=P(("groups", "adapter"), "tensor"),
        check_vma=False,
    )
```

```python
import functools
import math

import jax
import jax.numpy as jnp
from jax import lax
from jax.experimental import pallas as pl
from jax.experimental.pallas import tpu as pltpu
from jax.sharding import PartitionSpec as P

HEAD_SIZE = 128
LANES = 128
EPSILON = 1e-05
THETA = 500000.0
BF16 = jnp.bfloat16
F32 = jnp.float32
SWAP = [(0, 1), (1, 0)]
STEPS = 4
MIB = 1024 * 1024


def nn(a, b):
    return lax.dot_general(a, b, (((1,), (0,)), ((), ())), preferred_element_type=F32)


def nt(a, b):
    return lax.dot_general(a, b, (((1,), (1,)), ((), ())), preferred_element_type=F32)


def iota(shape, dim):
    return lax.broadcasted_iota(jnp.int32, shape, dim)


def ones_where(condition):
    return jnp.where(condition, 1.0, 0.0).astype(BF16)


def owner_and_standing(named, table):
    requests, adapters = named.shape[1], table.shape[1]
    table_column = jnp.sum(
        jnp.where(iota((adapters, adapters), 0) == iota((adapters, adapters), 1), table, 0),
        axis=1,
        keepdims=True,
    )
    owner = jnp.sum(
        jnp.where(iota((adapters, requests), 0) == named, table_column, 0), axis=0, keepdims=True
    )
    square = (requests, requests)
    owner_column = jnp.sum(
        jnp.where(iota(square, 0) == iota(square, 1), owner, 0), axis=1, keepdims=True
    )
    earlier = (owner_column == owner) & (iota(square, 0) < iota(square, 1))
    standing = jnp.sum(jnp.where(earlier, 1, 0), axis=0, keepdims=True)
    return owner, standing


def copy_all(pairs, sems):
    copies = [pltpu.make_async_copy(a, b, sems.at[i]) for i, (a, b) in enumerate(pairs)]
    for copy in copies:
        copy.start()
    return copies


def pack_kernel(capacity, x_hbm, gain_hbm, k_hbm, v_hbm, named_hbm, table_hbm, length_hbm, out_ref, x_ref, gain_ref, k_ref, v_ref, named_ref, table_ref, length_ref, flat_ref, spread_ref, sems):
    core = lax.axis_index("tensor")
    named_copy, table_copy, length_copy, x_copy, gain_copy, k_copy, v_copy = copy_all(
        [
            (named_hbm, named_ref),
            (table_hbm, table_ref),
            (length_hbm, length_ref),
            (x_hbm, x_ref),
            (gain_hbm, gain_ref),
            (k_hbm, k_ref),
            (v_hbm, v_ref),
        ],
        sems,
    )
    named_copy.wait()
    table_copy.wait()
    length_copy.wait()
    requests, width = x_ref.shape
    half = width // 2
    positions = k_ref.shape[0] // requests
    per_owner = 2 * capacity
    rows = out_ref.shape[0]
    owner, standing = owner_and_standing(named_ref[...], table_ref[...])
    own_slot = standing % 2 == core
    place = owner * per_owner + standing // 2
    x_row = place + jnp.where(own_slot, 0, capacity // 2)
    k_row = jnp.where(own_slot, owner * per_owner + capacity + 2 * (standing // 2), -2)
    order = iota((rows, requests), 0)
    put_x = ones_where(order == x_row)
    put_k = ones_where(order == k_row)
    put_v = ones_where(order == k_row + 1)

    x_copy.wait()
    gain_copy.wait()
    floats = x_ref[...].astype(F32)
    scale = lax.rsqrt(jnp.mean(floats * floats, axis=1, keepdims=True) + EPSILON)
    mine = pl.ds(pl.multiple_of(core * half, half), half)
    flat_ref[0:requests, :] = (x_ref[:, mine].astype(F32) * scale * gain_ref[:, mine]).astype(BF16)
    for first, source, copy in ((requests, k_ref, k_copy), (2 * requests, v_ref, v_copy)):
        copy.wait()
        spread_ref[...] = source[...].astype(F32)
        for p in range(positions):
            flat_ref[first : first + requests, p * LANES : (p + 1) * LANES] = spread_ref[
                pl.ds(p, requests, stride=positions), :
            ].astype(BF16)
    put = jnp.concatenate([put_x, put_k, put_v], axis=1)
    step = 512
    for c in range(0, half, step):
        out_ref[:, c : c + step] = nn(put, flat_ref[:, c : c + step]).astype(BF16)
    square = (requests, requests)
    length_column = jnp.sum(
        jnp.where(iota(square, 0) == iota(square, 1), length_ref[...], 0), axis=1, keepdims=True
    )
    lengths = jnp.broadcast_to(length_column.astype(F32), (requests, LANES)).astype(BF16)
    out_ref[:, half:] = nn(put_x, lengths).astype(BF16)


def project_kernel(capacity, owners, buf_ref, wq_hbm, wk_hbm, wv_hbm, down_hbm, *rest):
    wq_other_hbm, kv_other_hbm = rest[:STEPS], rest[STEPS : 2 * STEPS]
    mine_ref, theirs_ref, q_ref, narrow_ref, sums_ref, sems = rest[2 * STEPS :]
    half, qcols = q_ref.shape[0], wq_hbm.shape[1]
    hcols = wk_hbm.shape[0]
    kvcols = 2 * hcols
    per_owner = 2 * capacity
    here = capacity // 2
    rows = buf_ref.shape[0]
    start = lax.axis_index("tensor") * half
    step = half // STEPS
    waiting = []
    for n in range(STEPS):
        part = pl.ds(n * step, step)
        span = pl.ds(pl.multiple_of(start + n * step, step), step)
        pairs = [
            (wq_hbm.at[span, :], q_ref.at[part, 0:qcols]),
            (wq_other_hbm[n], q_ref.at[part, qcols : 2 * qcols]),
            (wk_hbm.at[:, span], narrow_ref.at[0:hcols, part]),
            (wv_hbm.at[:, span], narrow_ref.at[hcols:kvcols, part]),
            (kv_other_hbm[n], narrow_ref.at[kvcols : 2 * kvcols, part]),
            (down_hbm.at[:, part], narrow_ref.at[2 * kvcols :, part]),
        ]
        waiting.append(copy_all(pairs, sems.at[n]))
    wide = jnp.zeros((rows, 2 * qcols), F32)
    narrow = jnp.zeros((rows, narrow_ref.shape[0]), F32)
    for n in range(STEPS):
        for copy in waiting[n]:
            copy.wait()
        part = slice(n * step, (n + 1) * step)
        buf = buf_ref[:, part]
        wide += nn(buf, q_ref[part, :])
        narrow += nt(buf, narrow_ref[:, part])
    spare = jnp.zeros((rows, -narrow.shape[1] % LANES), F32)
    tile = 0
    for part in (wide, jnp.concatenate([narrow, spare], axis=1)):
        for c in range(0, part.shape[1], LANES):
            sums_ref[tile] = part[:, c : c + LANES]
            columns = slice(tile * LANES, (tile + 1) * LANES)
            for i in range(here):
                to = slice(i * owners, (i + 1) * owners)
                mine_ref[to, columns] = sums_ref[tile, pl.ds(i, owners, stride=per_owner), :]
                theirs_ref[to, columns] = sums_ref[
                    tile, pl.ds(here + i, owners, stride=per_owner), :
                ]
            tile += 1


def unpack_kernel(capacity, owners, buf_ref, wo_hbm, k_ref, v_ref, length_ref, cosine_ref, sine_ref, wo_ref, sems):
    columns = wo_ref.shape[1]
    span = pl.ds(pl.multiple_of(lax.axis_index("tensor") * columns, columns), columns)
    copies = copy_all([(wo_hbm.at[:, span], wo_ref)], sems)
    rows = buf_ref.shape[0]
    slots = owners * capacity // 2
    positions = k_ref.shape[0] // slots
    half = positions * LANES
    per_owner = 2 * capacity
    slot = iota((slots, rows), 0)
    base = (slot % owners) * per_owner
    order = iota((slots, rows), 1)
    pick_x = ones_where(order == base + slot // owners)
    pick_k = ones_where(order == base + capacity + 2 * (slot // owners))
    pick_v = ones_where(order == base + capacity + 2 * (slot // owners) + 1)
    pick = jnp.concatenate([pick_k, pick_v], axis=0)
    step = 512
    for c in range(0, half, step):
        both = nn(pick, buf_ref[:, c : c + step]).astype(BF16)
        for j in range(step // LANES):
            p = c // LANES + j
            tile = both[:, j * LANES : (j + 1) * LANES]
            k_ref[p * slots : (p + 1) * slots, :] = tile[:slots]
            v_ref[p * slots : (p + 1) * slots, :] = tile[slots:]
    length = nn(pick_x, buf_ref[:, half:])
    length_ref[...] = length
    halfway = HEAD_SIZE // 2
    lane = iota((slots, LANES), 1)
    exponent = (lane % halfway).astype(F32) * (-math.log(THETA) / halfway)
    angle = length * jnp.exp(exponent)
    cosine_ref[...] = jnp.cos(angle)
    sine = jnp.sin(angle)
    sine_ref[...] = jnp.where(lane < halfway, -sine, sine)
    for copy in copies:
        copy.wait()


def attend_kernel(mine_ref, theirs_ref, up_ref, k_ref, v_ref, length_ref, cosine_ref, sine_ref, out_up_hbm, *rest):
    wo_other_hbm = rest[:STEPS]
    out_ref, wo_other_ref, out_up_ref, sems = rest[STEPS:]
    step = wo_other_ref.shape[1] // STEPS
    copies = copy_all(
        [(out_up_hbm, out_up_ref)]
        + [
            (wo_other_hbm[n], wo_other_ref.at[:, n * step : (n + 1) * step]) for n in range(STEPS)
        ],
        sems,
    )
    core = lax.axis_index("tensor")
    slots = mine_ref.shape[0]
    ucols = up_ref.shape[1]
    kvcols = LANES
    qcols = (ucols - 2 * kvcols) // 2
    heads = 2 * qcols // HEAD_SIZE
    halfway = HEAD_SIZE // 2
    mine = mine_ref[...]
    theirs = theirs_ref[...]
    swapped = jnp.concatenate(
        [
            theirs[:, qcols : 2 * qcols],
            theirs[:, :qcols],
            theirs[:, 2 * qcols + kvcols : ucols],
            theirs[:, 2 * qcols : 2 * qcols + kvcols],
            theirs[:, ucols:],
        ],
        axis=1,
    )
    sums = mine + swapped
    ranks = sums[:, ucols : ucols + up_ref.shape[0]].astype(BF16)
    deltas = nn(ranks, up_ref[...]).astype(BF16).astype(F32)
    combined = sums[:, :ucols] + deltas
    cosine, sine = cosine_ref[...], sine_ref[...]

    def rotate(part):
        return part * cosine + pltpu.roll(part, halfway, 1) * sine

    queries = jnp.concatenate(
        [rotate(combined[:, h * HEAD_SIZE : (h + 1) * HEAD_SIZE]) for h in range(heads)], axis=0
    ).astype(BF16)
    kv_mine = combined[:, 2 * qcols : 2 * qcols + kvcols]
    kv_theirs = combined[:, 2 * qcols + kvcols :]
    leading = jnp.where(core == 0, kv_mine, kv_theirs)
    trailing = jnp.where(core == 0, kv_theirs, kv_mine)
    first = iota((slots, LANES), 1) < halfway
    own_key = rotate(jnp.where(first, leading, pltpu.roll(trailing, halfway, 1))).astype(BF16)
    own_value = jnp.where(first, pltpu.roll(leading, halfway, 1), trailing).astype(BF16)

    cached = k_ref.shape[0]
    rows = heads * slots
    shrink = math.sqrt(HEAD_SIZE)
    length = jnp.concatenate([length_ref[:, 0:1]] * heads, axis=0).astype(jnp.int32)
    column = iota((rows, cached), 1)
    visible = (column % slots == iota((rows, cached), 0) % slots) & (column // slots < length)
    own = iota((rows, slots), 1) == iota((rows, slots), 0) % slots
    scores = jnp.where(visible, nt(queries, k_ref[...]) / shrink, -jnp.inf)
    own_scores = jnp.where(own, nt(queries, own_key) / shrink, -jnp.inf)
    highest = jnp.maximum(
        jnp.max(scores, axis=1, keepdims=True), jnp.max(own_scores, axis=1, keepdims=True)
    )
    raised = jnp.exp(scores - highest)
    own_raised = jnp.exp(own_scores - highest)
    total = jnp.sum(raised, axis=1, keepdims=True) + jnp.sum(own_raised, axis=1, keepdims=True)
    weights = (raised / total).astype(BF16)
    own_weights = (own_raised / total).astype(BF16)
    attended = (nn(weights, v_ref[...]) + nn(own_weights, own_value)).astype(BF16)
    for h in range(heads):
        out_ref[:, h * HEAD_SIZE : (h + 1) * HEAD_SIZE] = attended[h * slots : (h + 1) * slots]
    for copy in copies:
        copy.wait()


def output_kernel(capacity, owners, mine_ref, theirs_ref, wo_ref, wo_other_ref, down_ref, down_other_ref, up_ref, out_ref):
    core = lax.axis_index("tensor")
    slots, cols = mine_ref.shape
    hcols = cols // 2
    half = out_ref.shape[1]
    rows = owners * capacity
    theirs = theirs_ref[...]
    rows_in = jnp.concatenate(
        [mine_ref[...], jnp.concatenate([theirs[:, hcols:], theirs[:, :hcols]], axis=1)], axis=0
    )
    out_row = iota((rows, 2 * slots), 0)
    standing = out_row % capacity
    source = (
        jnp.where(standing % 2 == core, 0, slots) + (standing // 2) * owners + out_row // capacity
    )
    arrange = ones_where(iota((rows, 2 * slots), 1) == source)
    attended = nn(arrange, rows_in).astype(BF16)
    left, right = attended[:, :hcols], attended[:, hcols:]
    ranks = (nt(left, down_ref[...]) + nt(right, down_other_ref[...])).astype(BF16)
    step = 512
    for c in range(0, half, step):
        delta = nn(ranks, up_ref[:, c : c + step]).astype(BF16).astype(F32)
        terms = nn(left, wo_ref[:, c : c + step]) + nn(right, wo_other_ref[:, c : c + step])
        out_ref[:, c : c + step] = (terms + delta).astype(BF16)


def pick_kernel(capacity, back_ref, named_ref, table_ref, out_ref):
    rows, half = back_ref.shape
    requests = out_ref.shape[0]
    owner, standing = owner_and_standing(named_ref[...], table_ref[...])
    place = ones_where(iota((rows, requests), 0) == owner * capacity + standing)
    step = 512
    for c in range(0, half, step):
        out_ref[:, c : c + step] = lax.dot_general(
            place,
            back_ref[:, c : c + step],
            (((0,), (0,)), ((), ())),
            preferred_element_type=F32,
        ).astype(BF16)


OUTSIDE = pl.BlockSpec(memory_space=pltpu.HBM)
INSIDE = pl.BlockSpec(memory_space=pltpu.VMEM)


def call(kernel, outs, scratch=(), vmem=8, outside=(), out_spec=INSIDE, moved=0):
    many = isinstance(outs, (list, tuple))
    return lambda *args: pl.pallas_call(
        kernel,
        out_shape=outs,
        in_specs=[OUTSIDE if i in outside else INSIDE for i in range(len(args))],
        out_specs=[out_spec] * len(outs) if many else out_spec,
        scratch_shapes=list(scratch),
        compiler_params=pltpu.CompilerParams(vmem_limit_bytes=vmem * MIB),
        cost_estimate=pl.CostEstimate(flops=0, bytes_accessed=moved, transcendentals=0),
    )(
        *[
            pltpu.with_memory_space_constraint(arg, pltpu.HBM) if i in outside else arg
            for i, arg in enumerate(args)
        ]
    )


def body(
    layer_input,
    input_norm_gain,
    query_projection,
    key_projection,
    value_projection,
    output_projection,
    cached_key_rows,
    cached_value_rows,
    request_adapter,
    adapter_row_table,
    cached_length,
    projection_adapter_down,
    query_adapter_up,
    key_value_adapter_up,
    output_adapter_down,
    output_adapter_up,
):
    requests, width = layer_input.shape
    owners = lax.axis_size("adapter")
    adapters = adapter_row_table.shape[0]
    positions = cached_key_rows.shape[1]
    half = width // 2
    capacity = max(2, 2 * ((requests + adapters - 1) // adapters))
    rows = owners * 2 * capacity
    slots = owners * capacity // 2
    named = request_adapter.reshape(1, requests)
    table = adapter_row_table.reshape(1, adapters)
    shape = jax.ShapeDtypeStruct

    packed = call(
        functools.partial(pack_kernel, capacity),
        shape((rows, half + LANES), BF16),
        [
            pltpu.VMEM((requests, width), BF16),
            pltpu.VMEM((1, width), F32),
            pltpu.VMEM((positions * requests, LANES), BF16),
            pltpu.VMEM((positions * requests, LANES), BF16),
            pltpu.VMEM((1, requests), jnp.int32),
            pltpu.VMEM((1, adapters), jnp.int32),
            pltpu.VMEM((1, requests), jnp.int32),
            pltpu.VMEM((3 * requests, half), BF16),
            pltpu.VMEM((positions * requests, LANES), F32),
            pltpu.SemaphoreType.DMA((7,)),
        ],
        outside=range(7),
    )(
        layer_input,
        input_norm_gain.reshape(1, width),
        cached_key_rows.reshape(requests * positions, HEAD_SIZE),
        cached_value_rows.reshape(requests * positions, HEAD_SIZE),
        named,
        table,
        cached_length.reshape(1, requests),
    )
    (
        packed,
        query_projection,
        key_projection,
        value_projection,
        output_projection,
        query_adapter_up,
        key_value_adapter_up,
        output_adapter_down,
    ) = lax.optimization_barrier(
        (
            packed,
            query_projection,
            key_projection,
            value_projection,
            output_projection,
            query_adapter_up,
            key_value_adapter_up,
            output_adapter_down,
        )
    )
    arrived = lax.all_to_all(
        packed.reshape(owners, 2 * capacity, half + LANES),
        "adapter",
        split_axis=0,
        concat_axis=0,
        tiled=True,
    ).reshape(rows, half + LANES)

    qcols = query_projection.shape[1]
    wk, wv = key_projection.T, value_projection.T
    kvcols = 2 * wk.shape[0]
    other = (1 - lax.axis_index("tensor")) * half
    hrows = output_projection.shape[0]
    step = half // STEPS
    wq_other = [
        lax.ppermute(
            lax.dynamic_slice(query_projection, (other + n * step, 0), (step, qcols)), "tensor", SWAP
        )
        for n in range(STEPS)
    ]
    kv_other = [
        lax.ppermute(
            jnp.concatenate(
                [
                    lax.dynamic_slice(w, (0, other + n * step), (kvcols // 2, step))
                    for w in (wk, wv)
                ],
                axis=0,
            ),
            "tensor",
            SWAP,
        )
        for n in range(STEPS)
    ]
    wo_other = [
        lax.ppermute(
            lax.dynamic_slice(output_projection, (0, other + n * step), (hrows, step)),
            "tensor",
            SWAP,
        )
        for n in range(STEPS)
    ]
    query_up = query_adapter_up[0]
    rank = query_up.shape[0]
    kv_up = key_value_adapter_up[0]
    hcols = kv_up.shape[2]
    out_down = output_adapter_down[0].T
    small = jnp.concatenate([query_up, kv_up[0], kv_up[1], out_down], axis=1)
    small_other = lax.ppermute(small, "tensor", SWAP)
    out_down_other = small_other[:, qcols + 2 * hcols :]

    def zeros(columns):
        return jnp.zeros((rank, columns), BF16)

    def kv_rows(which):
        blocks = []
        for source in (small, small_other):
            for one in range(2):
                first = qcols + one * hcols
                blocks.append(source[:, first : first + hcols] if one == which else zeros(hcols))
        return jnp.concatenate([zeros(2 * qcols)] + blocks, axis=1)

    up = jnp.concatenate(
        [
            jnp.concatenate(
                [small[:, :qcols], small_other[:, :qcols], zeros(4 * hcols)], axis=1
            ),
            kv_rows(0),
            kv_rows(1),
        ],
        axis=0,
    )
    down = projection_adapter_down[0].T
    ucols = 2 * qcols + 2 * kvcols
    pcols = ucols + (down.shape[0] + LANES - 1) // LANES * LANES

    narrow_rows = 2 * kvcols + down.shape[0]
    mine, theirs = call(
        functools.partial(project_kernel, capacity, owners),
        [shape((slots, pcols), F32), shape((slots, pcols), F32)],
        [
            pltpu.VMEM((half, 2 * qcols), BF16),
            pltpu.VMEM((narrow_rows, half), BF16),
            pltpu.VMEM((pcols // LANES, rows, LANES), F32),
            pltpu.SemaphoreType.DMA((STEPS, 6)),
        ],
        vmem=24,
        outside=range(1, 5 + 2 * STEPS),
    )(arrived, query_projection, wk, wv, down, *wq_other, *kv_other)
    theirs = lax.ppermute(theirs, "tensor", SWAP)
    keys, values, lengths, cosine, sine, wo_mine = call(
        functools.partial(unpack_kernel, capacity, owners),
        [shape((slots * positions, HEAD_SIZE), BF16)] * 2
        + [shape((slots, LANES), F32)] * 3
        + [shape((hrows, half), BF16)],
        [pltpu.SemaphoreType.DMA((1,))],
        outside=(1,),
    )(arrived, output_projection)
    attended, wo_other, out_up = call(
        attend_kernel,
        [
            shape((slots, 2 * qcols), BF16),
            shape((hrows, half), BF16),
            shape((rank, half), BF16),
        ],
        [pltpu.SemaphoreType.DMA((1 + STEPS,))],
        vmem=16,
        outside=range(8, 9 + STEPS),
    )(mine, theirs, up, keys, values, lengths, cosine, sine, output_adapter_up[0], *wo_other)
    attended_other = lax.ppermute(attended, "tensor", SWAP)
    finished = call(
        functools.partial(output_kernel, capacity, owners),
        shape((owners * capacity, half), BF16),
        vmem=16,
    )(
        attended,
        attended_other,
        wo_mine,
        wo_other,
        out_down,
        out_down_other,
        out_up,
    )
    back = lax.all_to_all(
        finished.reshape(owners, capacity, half), "adapter", split_axis=0, concat_axis=0, tiled=True
    ).reshape(owners * capacity, half)
    return call(functools.partial(pick_kernel, capacity), shape((requests, half), BF16))(
        back, named, table
    )


def solution(mesh):
    placed = (
        P(("groups", "adapter"), None),
        P(),
        P(None, "tensor"),
        P(None, "tensor"),
        P(None, "tensor"),
        P("tensor", None),
        P(("groups", "adapter"), None, None),
        P(("groups", "adapter"), None, None),
        P(("groups", "adapter"), None),
        P(),
        P(("groups", "adapter")),
        P("adapter", "tensor", None),
        P("adapter", None, "tensor"),
        P("adapter", None, None, "tensor"),
        P("adapter", "tensor", None),
        P("adapter", None, "tensor"),
    )
    return jax.shard_map(
        body,
        mesh=mesh,
        in_specs=placed,
        out_specs=P(("groups", "adapter"), "tensor"),
        check_vma=False,
    )
```

```python
import functools
import math

import jax
import jax.numpy as jnp
from jax import lax
from jax.experimental import pallas as pl
from jax.experimental.pallas import tpu as pltpu
from jax.sharding import PartitionSpec as P

HEAD_SIZE = 128
LANES = 128
EPSILON = 1e-05
THETA = 500000.0
BF16 = jnp.bfloat16
F32 = jnp.float32
SWAP = [(0, 1), (1, 0)]
GROUP = 16
MIB = 1024 * 1024


def nn(a, b):
    return lax.dot_general(a, b, (((1,), (0,)), ((), ())), preferred_element_type=F32)


def nt(a, b):
    return lax.dot_general(a, b, (((1,), (1,)), ((), ())), preferred_element_type=F32)


def iota(shape, dim):
    return lax.broadcasted_iota(jnp.int32, shape, dim)


def ones_where(condition):
    return jnp.where(condition, 1.0, 0.0).astype(BF16)


def owner_and_standing(named, table):
    requests, adapters = named.shape[1], table.shape[1]
    table_column = jnp.sum(
        jnp.where(iota((adapters, adapters), 0) == iota((adapters, adapters), 1), table, 0),
        axis=1,
        keepdims=True,
    )
    owner = jnp.sum(
        jnp.where(iota((adapters, requests), 0) == named, table_column, 0), axis=0, keepdims=True
    )
    square = (requests, requests)
    owner_column = jnp.sum(
        jnp.where(iota(square, 0) == iota(square, 1), owner, 0), axis=1, keepdims=True
    )
    earlier = (owner_column == owner) & (iota(square, 0) < iota(square, 1))
    standing = jnp.sum(jnp.where(earlier, 1, 0), axis=0, keepdims=True)
    return owner, standing


def copy_all(pairs, sems):
    copies = [pltpu.make_async_copy(a, b, sems.at[i]) for i, (a, b) in enumerate(pairs)]
    for copy in copies:
        copy.start()
    return copies


def pack_kernel(capacity, x_hbm, gain_hbm, k_hbm, v_hbm, named_hbm, table_hbm, length_hbm, up_hbm, kv_up_hbm, out_down_hbm, *rest):
    up_ref, kv_up_ref, out_down_ref = rest[-4:-1]
    rest = rest[:-4] + rest[-1:]
    small_ref, x_ref, gain_ref, k_ref, v_ref, named_ref, table_ref, length_ref, flat_ref, spread_ref, sems = rest[-11:]
    blocks = rest[:-11]
    count = len(blocks)
    owners = 2 * count
    named_copy, table_copy, length_copy, x_copy, gain_copy, k_copy, v_copy, *up_copies = copy_all(
        [
            (named_hbm, named_ref),
            (table_hbm, table_ref),
            (length_hbm, length_ref),
            (x_hbm, x_ref),
            (gain_hbm, gain_ref),
            (k_hbm, k_ref),
            (v_hbm, v_ref),
            (up_hbm, up_ref),
            (kv_up_hbm, kv_up_ref),
            (out_down_hbm, out_down_ref),
        ],
        sems,
    )
    requests, width = x_ref.shape
    positions = k_ref.shape[0] // requests
    per_block = blocks[0].shape[0]
    rows = per_block * count
    first = lax.axis_index("adapter") + lax.axis_index("tensor") * count
    named_copy.wait()
    table_copy.wait()
    length_copy.wait()
    owner, standing = owner_and_standing(named_ref[...], table_ref[...])
    ahead = owner - first
    ahead = jnp.where(ahead < -owners, ahead + 2 * owners, jnp.where(ahead < 0, ahead + owners, ahead))
    row = jnp.where(ahead < count, ahead * per_block + 2 * standing, -2)
    order = iota((rows, requests), 0)
    put_x = ones_where(order == row)
    put_kv = ones_where(order == row + 1)
    put = jnp.concatenate([put_x, put_kv], axis=1)

    x_copy.wait()
    gain_copy.wait()
    floats = x_ref[...].astype(F32)
    scale = lax.rsqrt(jnp.mean(floats * floats, axis=1, keepdims=True) + EPSILON)
    flat_ref[0:requests, :] = (floats * scale * gain_ref[...]).astype(BF16)
    for n, (source, copy) in enumerate(((k_ref, k_copy), (v_ref, v_copy))):
        copy.wait()
        spread_ref[...] = source[...].astype(F32)
        for p in range(positions):
            to = slice((n * positions + p) * LANES, (n * positions + p + 1) * LANES)
            flat_ref[requests : 2 * requests, to] = spread_ref[
                pl.ds(p, requests, stride=positions), :
            ].astype(BF16)
    step = 512
    for c in range(0, width, step):
        placed = nn(put, flat_ref[:, c : c + step]).astype(BF16)
        for j, block in enumerate(blocks):
            block[:, c : c + step] = placed[j * per_block : (j + 1) * per_block]
    square = (requests, requests)
    length_column = jnp.sum(
        jnp.where(iota(square, 0) == iota(square, 1), length_ref[...], 0), axis=1, keepdims=True
    )
    lengths = jnp.broadcast_to(length_column.astype(F32), (requests, LANES)).astype(BF16)
    placed = nn(put_x, lengths).astype(BF16)
    for j, block in enumerate(blocks):
        block[:, width:] = placed[j * per_block : (j + 1) * per_block]
    for copy in up_copies:
        copy.wait()
    small_ref[...] = jnp.concatenate(
        [up_ref[...], kv_up_ref[0], kv_up_ref[1], out_down_ref[...]], axis=1
    )


def stacked(blocks, columns):
    return jnp.concatenate([block[:, columns] for block in blocks], axis=0)


def stage_kernel(wq_hbm, wk_hbm, wv_hbm, down_hbm, wq_ref, kv_ref, down_ref, sems):
    width = wq_hbm.shape[0]
    hcols = wk_hbm.shape[0]
    ranks = down_hbm.shape[0]
    pieces = 4
    pairs = [(wk_hbm, kv_ref.at[0:hcols, :]), (wv_hbm, kv_ref.at[hcols:, :])]
    for n in range(pieces):
        rows = pl.ds(n * (width // pieces), width // pieces)
        pairs.append((wq_hbm.at[rows, :], wq_ref.at[rows, :]))
    for n in range(2):
        rows = pl.ds(n * (ranks // 2), ranks // 2)
        pairs.append((down_hbm.at[rows, :], down_ref.at[rows, :]))
    for copy in copy_all(pairs, sems):
        copy.wait()


def project_kernel(count, *refs):
    blocks = refs[: 2 * count]
    wq_ref, kv_ref, down_ref, mine_ref, theirs_ref, sums_ref = refs[2 * count :]
    width = wq_ref.shape[0]
    half = down_ref.shape[1]
    slots = mine_ref.shape[0]
    rows = sums_ref.shape[1]
    x_all = stacked(blocks, slice(0, width))
    halves = [x_all[:, :half], x_all[:, half:]]
    x_half = jnp.where(lax.axis_index("tensor") == 0, halves[0], halves[1])
    ranks = nt(x_half, down_ref[...])
    spare = jnp.zeros((rows, -ranks.shape[1] % LANES), F32)
    sums = [nn(x_all, wq_ref[...]), nt(x_all, kv_ref[...]), jnp.concatenate([ranks, spare], axis=1)]
    tile = 0
    for part in sums:
        for c in range(0, part.shape[1], LANES):
            sums_ref[tile] = part[:, c : c + LANES]
            columns = slice(tile * LANES, (tile + 1) * LANES)
            mine_ref[:, columns] = sums_ref[tile, pl.ds(0, slots, stride=2), :]
            theirs_ref[:, columns] = sums_ref[tile, pl.ds(rows // 2, slots, stride=2), :]
            tile += 1


def unpack_kernel(count, *refs):
    blocks = refs[:count]
    k_ref, v_ref, length_ref, cosine_ref, sine_ref = refs[count:]
    slots = length_ref.shape[0]
    per_block = blocks[0].shape[0]
    positions = k_ref.shape[0] // slots
    width = 2 * positions * LANES
    together = GROUP // (per_block // 2)
    pick = iota((GROUP, 2 * GROUP), 1) - 2 * iota((GROUP, 2 * GROUP), 0)
    pick_x, pick_kv = ones_where(pick == 0), ones_where(pick == 1)
    step = 512
    for g in range(slots // GROUP):
        members = blocks[g * together : (g + 1) * together]
        for c in range(0, width, step):
            picked = nn(pick_kv, stacked(members, slice(c, c + step))).astype(BF16)
            for j in range(step // LANES):
                p = c // LANES + j
                target, p = (k_ref, p) if p < positions else (v_ref, p - positions)
                first = (g * positions + p) * GROUP
                target[first : first + GROUP, :] = picked[:, j * LANES : (j + 1) * LANES]
        length_ref[g * GROUP : (g + 1) * GROUP, :] = nn(
            pick_x, stacked(members, slice(width, width + LANES))
        )
    halfway = HEAD_SIZE // 2
    lane = iota((slots, LANES), 1)
    exponent = (lane % halfway).astype(F32) * (-math.log(THETA) / halfway)
    angle = length_ref[...] * jnp.exp(exponent)
    cosine_ref[...] = jnp.cos(angle)
    sine = jnp.sin(angle)
    sine_ref[...] = jnp.where(lane < halfway, -sine, sine)


def attend_kernel(mine_ref, theirs_ref, small_ref, small_other_ref, k_ref, v_ref, length_ref, cosine_ref, sine_ref, out_ref):
    core = lax.axis_index("tensor")
    slots = mine_ref.shape[0]
    rank = small_ref.shape[0]
    kvcols = LANES
    qcols = out_ref.shape[1] // 2
    heads = 2 * qcols // HEAD_SIZE
    halfway = HEAD_SIZE // 2
    both = qcols + kvcols
    mine = mine_ref[...]
    theirs = theirs_ref[...]
    ranks = (mine + theirs)[:, both : both + 3 * rank].astype(BF16)
    ranks = [ranks[:, n * rank : (n + 1) * rank] for n in range(3)]

    def added(projected, up_ref):
        change = jnp.concatenate(
            [
                nn(ranks[0], up_ref[:, :qcols]),
                nn(ranks[1], up_ref[:, qcols : qcols + halfway]),
                nn(ranks[2], up_ref[:, qcols + halfway : both]),
            ],
            axis=1,
        )
        return projected[:, :both] + change.astype(BF16).astype(F32)

    mine = added(mine, small_ref)
    theirs = added(theirs, small_other_ref)
    combined = jnp.concatenate([mine[:, :qcols], theirs[:, :qcols]], axis=1)
    cosine, sine = cosine_ref[...], sine_ref[...]

    def rotate(part):
        return part * cosine + pltpu.roll(part, halfway, 1) * sine

    queries = [
        rotate(combined[:, h * HEAD_SIZE : (h + 1) * HEAD_SIZE]).astype(BF16) for h in range(heads)
    ]
    kv_mine = mine[:, qcols:]
    kv_theirs = theirs[:, qcols:]
    leading = jnp.where(core == 0, kv_mine, kv_theirs)
    trailing = jnp.where(core == 0, kv_theirs, kv_mine)
    first = iota((slots, LANES), 1) < halfway
    own_keys = rotate(jnp.where(first, leading, pltpu.roll(trailing, halfway, 1))).astype(BF16)
    own_values = jnp.where(first, pltpu.roll(leading, halfway, 1), trailing).astype(BF16)

    cached = k_ref.shape[0] * GROUP // slots
    rows = heads * GROUP
    shrink = math.sqrt(HEAD_SIZE)
    column = iota((rows, cached), 1)
    same = column % GROUP == iota((rows, cached), 0) % GROUP
    position = column // GROUP
    own = iota((rows, GROUP), 1) == iota((rows, GROUP), 0) % GROUP
    for g in range(slots // GROUP):
        members = slice(g * GROUP, (g + 1) * GROUP)
        held = slice(g * cached, (g + 1) * cached)
        query = jnp.concatenate([part[members] for part in queries], axis=0)
        length = jnp.concatenate([length_ref[members, 0:1]] * heads, axis=0).astype(jnp.int32)
        scores = jnp.where(
            same & (position < length), nt(query, k_ref[held, :]) / shrink, -jnp.inf
        )
        own_scores = jnp.where(own, nt(query, own_keys[members]) / shrink, -jnp.inf)
        highest = jnp.maximum(
            jnp.max(scores, axis=1, keepdims=True), jnp.max(own_scores, axis=1, keepdims=True)
        )
        raised = jnp.exp(scores - highest)
        own_raised = jnp.exp(own_scores - highest)
        total = jnp.sum(raised, axis=1, keepdims=True) + jnp.sum(own_raised, axis=1, keepdims=True)
        weights = (raised / total).astype(BF16)
        own_weights = (own_raised / total).astype(BF16)
        attended = (nn(weights, v_ref[held, :]) + nn(own_weights, own_values[members])).astype(BF16)
        for h in range(heads):
            out_ref[members, h * HEAD_SIZE : (h + 1) * HEAD_SIZE] = attended[
                h * GROUP : (h + 1) * GROUP
            ]


def output_kernel(capacity, owners, mine_ref, theirs_ref, wo_ref, wo_other_ref, small_ref, small_other_ref, up_ref, out_ref):
    core = lax.axis_index("tensor")
    slots, cols = mine_ref.shape
    hcols = cols // 2
    half = out_ref.shape[1]
    rows = owners * capacity
    theirs = theirs_ref[...]
    rows_in = jnp.concatenate(
        [mine_ref[...], jnp.concatenate([theirs[:, hcols:], theirs[:, :hcols]], axis=1)], axis=0
    )
    count = owners // 2
    per_owner = slots // count
    out_row = iota((rows, 2 * slots), 0)
    ahead = lax.axis_index("adapter") - core * count - out_row // capacity
    ahead = jnp.where(ahead < -owners, ahead + 2 * owners, jnp.where(ahead < 0, ahead + owners, ahead))
    source = jnp.where(ahead < count, ahead * per_owner, slots + (ahead - count) * per_owner)
    source = source + out_row % capacity
    arrange = ones_where(iota((rows, 2 * slots), 1) == source)
    attended = nn(arrange, rows_in).astype(BF16)
    left, right = attended[:, :hcols], attended[:, hcols:]
    down = slice(small_ref.shape[1] - hcols, small_ref.shape[1])
    ranks = (nt(left, small_ref[:, down]) + nt(right, small_other_ref[:, down])).astype(BF16)
    step = 512
    for c in range(0, half, step):
        delta = nn(ranks, up_ref[:, c : c + step]).astype(BF16).astype(F32)
        columns = pl.ds(pl.multiple_of(core * half + c, step), step)
        terms = nn(left, wo_ref[:, columns]) + nn(right, wo_other_ref[:, columns])
        out_ref[:, c : c + step] = (terms + delta).astype(BF16)


def pick_kernel(capacity, back_ref, named_ref, table_ref, out_ref):
    rows, half = back_ref.shape
    requests = out_ref.shape[0]
    owner, standing = owner_and_standing(named_ref[...], table_ref[...])
    place = ones_where(iota((rows, requests), 0) == owner * capacity + standing)
    step = 512
    for c in range(0, half, step):
        out_ref[:, c : c + step] = lax.dot_general(
            place,
            back_ref[:, c : c + step],
            (((0,), (0,)), ((), ())),
            preferred_element_type=F32,
        ).astype(BF16)


OUTSIDE = pl.BlockSpec(memory_space=pltpu.HBM)
INSIDE = pl.BlockSpec(memory_space=pltpu.VMEM)


def call(kernel, outs, scratch=(), vmem=8, outside=(), out_spec=INSIDE, moved=0):
    many = isinstance(outs, (list, tuple))
    return lambda *args: pl.pallas_call(
        kernel,
        out_shape=outs,
        in_specs=[OUTSIDE if i in outside else INSIDE for i in range(len(args))],
        out_specs=[out_spec] * len(outs) if many else out_spec,
        scratch_shapes=list(scratch),
        compiler_params=pltpu.CompilerParams(vmem_limit_bytes=vmem * MIB),
        cost_estimate=pl.CostEstimate(flops=0, bytes_accessed=moved, transcendentals=0),
    )(
        *[
            pltpu.with_memory_space_constraint(arg, pltpu.HBM) if i in outside else arg
            for i, arg in enumerate(args)
        ]
    )


def body(
    layer_input,
    input_norm_gain,
    query_projection,
    key_projection,
    value_projection,
    output_projection,
    cached_key_rows,
    cached_value_rows,
    request_adapter,
    adapter_row_table,
    cached_length,
    projection_adapter_down,
    query_adapter_up,
    key_value_adapter_up,
    output_adapter_down,
    output_adapter_up,
):
    shape = jax.ShapeDtypeStruct
    requests, width = layer_input.shape
    owners = lax.axis_size("adapter")
    adapters = adapter_row_table.shape[0]
    positions = cached_key_rows.shape[1]
    half = width // 2
    capacity = max(2, 2 * ((requests + adapters - 1) // adapters))
    count = owners // 2
    kept = (capacity + 3) // 4 * 4
    slots = count * kept
    block = shape((2 * kept, width + LANES), BF16)
    named = request_adapter.reshape(1, requests)
    table = adapter_row_table.reshape(1, adapters)

    rank, qcols = query_adapter_up.shape[1:]
    hcols = key_value_adapter_up.shape[3]
    hrows = output_projection.shape[0]
    *packed, small = call(
        functools.partial(pack_kernel, capacity),
        [block] * count + [shape((rank, qcols + 2 * hcols + hrows), BF16)],
        [
            pltpu.VMEM((requests, width), BF16),
            pltpu.VMEM((1, width), F32),
            pltpu.VMEM((positions * requests, LANES), BF16),
            pltpu.VMEM((positions * requests, LANES), BF16),
            pltpu.VMEM((1, requests), jnp.int32),
            pltpu.VMEM((1, adapters), jnp.int32),
            pltpu.VMEM((1, requests), jnp.int32),
            pltpu.VMEM((2 * requests, width), BF16),
            pltpu.VMEM((positions * requests, LANES), F32),
            pltpu.VMEM((rank, qcols), BF16),
            pltpu.VMEM((2, rank, hcols), BF16),
            pltpu.VMEM((rank, hrows), BF16),
            pltpu.SemaphoreType.DMA((10,)),
        ],
        outside=range(10),
    )(
        layer_input,
        input_norm_gain.reshape(1, width),
        cached_key_rows.reshape(requests * positions, HEAD_SIZE),
        cached_value_rows.reshape(requests * positions, HEAD_SIZE),
        named,
        table,
        cached_length.reshape(1, requests),
        query_adapter_up[0],
        key_value_adapter_up[0],
        output_adapter_down[0].T,
    )
    down = projection_adapter_down[0].T
    wk, wv = key_projection.T, value_projection.T
    kvcols = 2 * wk.shape[0]
    *packed, query_projection, wk, wv, down, output_projection, output_adapter_up = (
        lax.optimization_barrier(
            (*packed, query_projection, wk, wv, down, output_projection, output_adapter_up)
        )
    )
    weights = call(
        stage_kernel,
        [
            shape(query_projection.shape, BF16),
            shape((kvcols, width), BF16),
            shape(down.shape, BF16),
        ],
        [pltpu.SemaphoreType.DMA((8,))],
        outside=range(4),
        moved=2 * (query_projection.size + kvcols * width + down.size),
    )(query_projection, wk, wv, down)

    def onward(n):
        return [
            (a * 2 + t, (a + t * count + n) % owners * 2 + t) for a in range(owners) for t in range(2)
        ]

    arrived = [
        lax.ppermute(one, ("adapter", "tensor"), onward(n)) for n, one in enumerate(packed)
    ]
    arrived[0], *weights = lax.optimization_barrier((arrived[0], *weights))
    passed = [lax.ppermute(one, "tensor", SWAP) for one in arrived]
    wo_other = lax.ppermute(output_projection, "tensor", SWAP)
    small_other = lax.ppermute(small, "tensor", SWAP)
    pcols = qcols + kvcols + (down.shape[0] + LANES - 1) // LANES * LANES
    mine, theirs = call(
        functools.partial(project_kernel, count),
        [shape((slots, pcols), F32), shape((slots, pcols), F32)],
        [pltpu.VMEM((pcols // LANES, 4 * slots, LANES), F32)],
        vmem=24,
    )(*arrived, *passed, *weights)
    theirs = lax.ppermute(theirs, "tensor", SWAP)
    keys, values, lengths, cosine, sine = call(
        functools.partial(unpack_kernel, count),
        [shape((slots * positions, HEAD_SIZE), BF16)] * 2 + [shape((slots, LANES), F32)] * 3,
    )(*arrived)
    attended = call(attend_kernel, shape((slots, 2 * qcols), BF16), vmem=16)(
        mine, theirs, small, small_other, keys, values, lengths, cosine, sine
    )
    attended_other = lax.ppermute(attended, "tensor", SWAP)
    finished = call(
        functools.partial(output_kernel, capacity, owners),
        shape((owners * capacity, half), BF16),
        vmem=16,
    )(
        attended,
        attended_other,
        output_projection,
        wo_other,
        small,
        small_other,
        output_adapter_up[0],
    )
    back = lax.all_to_all(
        finished.reshape(owners, capacity, half), "adapter", split_axis=0, concat_axis=0, tiled=True
    ).reshape(owners * capacity, half)
    return call(functools.partial(pick_kernel, capacity), shape((requests, half), BF16))(
        back, named, table
    )


def solution(mesh):
    placed = (
        P(("groups", "adapter"), None),
        P(),
        P(None, "tensor"),
        P(None, "tensor"),
        P(None, "tensor"),
        P("tensor", None),
        P(("groups", "adapter"), None, None),
        P(("groups", "adapter"), None, None),
        P(("groups", "adapter"), None),
        P(),
        P(("groups", "adapter")),
        P("adapter", "tensor", None),
        P("adapter", None, "tensor"),
        P("adapter", None, None, "tensor"),
        P("adapter", "tensor", None),
        P("adapter", None, "tensor"),
    )
    return jax.shard_map(
        body,
        mesh=mesh,
        in_specs=placed,
        out_specs=P(("groups", "adapter"), "tensor"),
        check_vma=False,
    )
```

```python
import functools
import math

import jax
import jax.numpy as jnp
from jax import lax
from jax.experimental import pallas as pl
from jax.experimental.pallas import tpu as pltpu
from jax.sharding import PartitionSpec as P

HEAD_SIZE = 128
LANES = 128
EPSILON = 1e-05
THETA = 500000.0
BF16 = jnp.bfloat16
F32 = jnp.float32
SWAP = [(0, 1), (1, 0)]
GROUP = 16
MIB = 1024 * 1024


def nn(a, b):
    return lax.dot_general(a, b, (((1,), (0,)), ((), ())), preferred_element_type=F32)


def nt(a, b):
    return lax.dot_general(a, b, (((1,), (1,)), ((), ())), preferred_element_type=F32)


def iota(shape, dim):
    return lax.broadcasted_iota(jnp.int32, shape, dim)


def ones_where(condition):
    return jnp.where(condition, 1.0, 0.0).astype(BF16)


def owner_and_standing(named, table):
    requests, adapters = named.shape[1], table.shape[1]
    table_column = jnp.sum(
        jnp.where(iota((adapters, adapters), 0) == iota((adapters, adapters), 1), table, 0),
        axis=1,
        keepdims=True,
    )
    owner = jnp.sum(
        jnp.where(iota((adapters, requests), 0) == named, table_column, 0), axis=0, keepdims=True
    )
    square = (requests, requests)
    owner_column = jnp.sum(
        jnp.where(iota(square, 0) == iota(square, 1), owner, 0), axis=1, keepdims=True
    )
    earlier = (owner_column == owner) & (iota(square, 0) < iota(square, 1))
    standing = jnp.sum(jnp.where(earlier, 1, 0), axis=0, keepdims=True)
    return owner, standing


def copy_all(pairs, sems):
    copies = [pltpu.make_async_copy(a, b, sems.at[i]) for i, (a, b) in enumerate(pairs)]
    for copy in copies:
        copy.start()
    return copies


def pack_kernel(capacity, x_hbm, gain_hbm, k_hbm, v_hbm, named_hbm, table_hbm, length_hbm, up_hbm, kv_up_hbm, out_down_hbm, *rest):
    up_ref, kv_up_ref, out_down_ref = rest[-4:-1]
    rest = rest[:-4] + rest[-1:]
    small_ref, x_ref, gain_ref, k_ref, v_ref, named_ref, table_ref, length_ref, flat_ref, spread_ref, sems = rest[-11:]
    blocks = rest[:-11]
    count = len(blocks)
    owners = 2 * count
    named_copy, table_copy, length_copy, x_copy, gain_copy, k_copy, v_copy, *up_copies = copy_all(
        [
            (named_hbm, named_ref),
            (table_hbm, table_ref),
            (length_hbm, length_ref),
            (x_hbm, x_ref),
            (gain_hbm, gain_ref),
            (k_hbm, k_ref),
            (v_hbm, v_ref),
            (up_hbm, up_ref),
            (kv_up_hbm, kv_up_ref),
            (out_down_hbm, out_down_ref),
        ],
        sems,
    )
    requests, width = x_ref.shape
    positions = k_ref.shape[0] // requests
    per_block = blocks[0].shape[0]
    rows = per_block * count
    first = lax.axis_index("adapter") + lax.axis_index("tensor") * count
    named_copy.wait()
    table_copy.wait()
    length_copy.wait()
    owner, standing = owner_and_standing(named_ref[...], table_ref[...])
    ahead = owner - first
    ahead = jnp.where(ahead < -owners, ahead + 2 * owners, jnp.where(ahead < 0, ahead + owners, ahead))
    row = jnp.where(ahead < count, ahead * per_block + 2 * standing, -2)
    order = iota((rows, requests), 0)
    put_x = ones_where(order == row)
    put_kv = ones_where(order == row + 1)
    put = jnp.concatenate([put_x, put_kv], axis=1)

    x_copy.wait()
    gain_copy.wait()
    floats = x_ref[...].astype(F32)
    scale = lax.rsqrt(jnp.mean(floats * floats, axis=1, keepdims=True) + EPSILON)
    flat_ref[0:requests, :] = (floats * scale * gain_ref[...]).astype(BF16)
    for n, (source, copy) in enumerate(((k_ref, k_copy), (v_ref, v_copy))):
        copy.wait()
        spread_ref[...] = source[...].astype(F32)
        for p in range(positions):
            to = slice((n * positions + p) * LANES, (n * positions + p + 1) * LANES)
            flat_ref[requests : 2 * requests, to] = spread_ref[
                pl.ds(p, requests, stride=positions), :
            ].astype(BF16)
    step = 512
    for c in range(0, width, step):
        placed = nn(put, flat_ref[:, c : c + step]).astype(BF16)
        for j, block in enumerate(blocks):
            block[:, c : c + step] = placed[j * per_block : (j + 1) * per_block]
    square = (requests, requests)
    length_column = jnp.sum(
        jnp.where(iota(square, 0) == iota(square, 1), length_ref[...], 0), axis=1, keepdims=True
    )
    lengths = jnp.broadcast_to(length_column.astype(F32), (requests, LANES)).astype(BF16)
    placed = nn(put_x, lengths).astype(BF16)
    for j, block in enumerate(blocks):
        block[:, width:] = placed[j * per_block : (j + 1) * per_block]
    for copy in up_copies:
        copy.wait()
    small_ref[...] = jnp.concatenate(
        [up_ref[...], kv_up_ref[0], kv_up_ref[1], out_down_ref[...]], axis=1
    )


def stacked(blocks, columns):
    return jnp.concatenate([block[:, columns] for block in blocks], axis=0)


def stage_kernel(wq_hbm, wk_hbm, wv_hbm, down_hbm, wq_ref, kv_ref, down_ref, sems):
    width = wq_hbm.shape[0]
    hcols = wk_hbm.shape[0]
    ranks = down_hbm.shape[0]
    pieces = 4
    pairs = [(wk_hbm, kv_ref.at[0:hcols, :]), (wv_hbm, kv_ref.at[hcols:, :])]
    for n in range(pieces):
        rows = pl.ds(n * (width // pieces), width // pieces)
        pairs.append((wq_hbm.at[rows, :], wq_ref.at[rows, :]))
    for n in range(2):
        rows = pl.ds(n * (ranks // 2), ranks // 2)
        pairs.append((down_hbm.at[rows, :], down_ref.at[rows, :]))
    for copy in copy_all(pairs, sems):
        copy.wait()


def project_kernel(count, *refs):
    blocks = refs[: 2 * count]
    wq_ref, kv_ref, down_ref, mine_ref, theirs_ref, sums_ref = refs[2 * count :]
    width = wq_ref.shape[0]
    half = down_ref.shape[1]
    slots = mine_ref.shape[0]
    rows = sums_ref.shape[1]
    x_all = stacked(blocks, slice(0, width))
    halves = [x_all[:, :half], x_all[:, half:]]
    x_half = jnp.where(lax.axis_index("tensor") == 0, halves[0], halves[1])
    ranks = nt(x_half, down_ref[...])
    spare = jnp.zeros((rows, -ranks.shape[1] % LANES), F32)
    sums = [nn(x_all, wq_ref[...]), nt(x_all, kv_ref[...]), jnp.concatenate([ranks, spare], axis=1)]
    tile = 0
    for part in sums:
        for c in range(0, part.shape[1], LANES):
            sums_ref[tile] = part[:, c : c + LANES]
            columns = slice(tile * LANES, (tile + 1) * LANES)
            mine_ref[:, columns] = sums_ref[tile, pl.ds(0, slots, stride=2), :]
            theirs_ref[:, columns] = sums_ref[tile, pl.ds(rows // 2, slots, stride=2), :]
            tile += 1


def unpack_kernel(count, *refs):
    blocks = refs[:count]
    k_ref, v_ref, length_ref, cosine_ref, sine_ref = refs[count:]
    slots = length_ref.shape[0]
    per_block = blocks[0].shape[0]
    positions = k_ref.shape[0] // slots
    width = 2 * positions * LANES
    together = GROUP // (per_block // 2)
    pick = iota((GROUP, 2 * GROUP), 1) - 2 * iota((GROUP, 2 * GROUP), 0)
    pick_x, pick_kv = ones_where(pick == 0), ones_where(pick == 1)
    step = 512
    for g in range(slots // GROUP):
        members = blocks[g * together : (g + 1) * together]
        for c in range(0, width, step):
            picked = nn(pick_kv, stacked(members, slice(c, c + step))).astype(BF16)
            for j in range(step // LANES):
                p = c // LANES + j
                target, p = (k_ref, p) if p < positions else (v_ref, p - positions)
                first = (g * positions + p) * GROUP
                target[first : first + GROUP, :] = picked[:, j * LANES : (j + 1) * LANES]
        length_ref[g * GROUP : (g + 1) * GROUP, :] = nn(
            pick_x, stacked(members, slice(width, width + LANES))
        )
    halfway = HEAD_SIZE // 2
    lane = iota((slots, LANES), 1)
    exponent = (lane % halfway).astype(F32) * (-math.log(THETA) / halfway)
    angle = length_ref[...] * jnp.exp(exponent)
    cosine_ref[...] = jnp.cos(angle)
    sine = jnp.sin(angle)
    sine_ref[...] = jnp.where(lane < halfway, -sine, sine)


def attend_kernel(mine_ref, theirs_ref, small_ref, small_other_ref, k_ref, v_ref, length_ref, cosine_ref, sine_ref, out_ref):
    core = lax.axis_index("tensor")
    slots = mine_ref.shape[0]
    rank = small_ref.shape[0]
    kvcols = LANES
    qcols = out_ref.shape[1] // 2
    heads = 2 * qcols // HEAD_SIZE
    halfway = HEAD_SIZE // 2
    both = qcols + kvcols
    mine = mine_ref[...]
    theirs = theirs_ref[...]
    ranks = (mine + theirs)[:, both : both + 3 * rank].astype(BF16)
    ranks = [ranks[:, n * rank : (n + 1) * rank] for n in range(3)]

    def added(projected, up_ref):
        change = jnp.concatenate(
            [
                nn(ranks[0], up_ref[:, :qcols]),
                nn(ranks[1], up_ref[:, qcols : qcols + halfway]),
                nn(ranks[2], up_ref[:, qcols + halfway : both]),
            ],
            axis=1,
        )
        return projected[:, :both] + change.astype(BF16).astype(F32)

    mine = added(mine, small_ref)
    theirs = added(theirs, small_other_ref)
    combined = jnp.concatenate([mine[:, :qcols], theirs[:, :qcols]], axis=1)
    cosine, sine = cosine_ref[...], sine_ref[...]

    def rotate(part):
        return part * cosine + pltpu.roll(part, halfway, 1) * sine

    queries = [
        rotate(combined[:, h * HEAD_SIZE : (h + 1) * HEAD_SIZE]).astype(BF16) for h in range(heads)
    ]
    kv_mine = mine[:, qcols:]
    kv_theirs = theirs[:, qcols:]
    leading = jnp.where(core == 0, kv_mine, kv_theirs)
    trailing = jnp.where(core == 0, kv_theirs, kv_mine)
    first = iota((slots, LANES), 1) < halfway
    own_keys = rotate(jnp.where(first, leading, pltpu.roll(trailing, halfway, 1))).astype(BF16)
    own_values = jnp.where(first, pltpu.roll(leading, halfway, 1), trailing).astype(BF16)

    cached = k_ref.shape[0] * GROUP // slots
    rows = heads * GROUP
    shrink = math.sqrt(HEAD_SIZE)
    column = iota((rows, cached), 1)
    same = column % GROUP == iota((rows, cached), 0) % GROUP
    position = column // GROUP
    own = iota((rows, GROUP), 1) == iota((rows, GROUP), 0) % GROUP
    for g in range(slots // GROUP):
        members = slice(g * GROUP, (g + 1) * GROUP)
        held = slice(g * cached, (g + 1) * cached)
        query = jnp.concatenate([part[members] for part in queries], axis=0)
        length = jnp.concatenate([length_ref[members, 0:1]] * heads, axis=0).astype(jnp.int32)
        scores = jnp.where(
            same & (position < length), nt(query, k_ref[held, :]) / shrink, -jnp.inf
        )
        own_scores = jnp.where(own, nt(query, own_keys[members]) / shrink, -jnp.inf)
        highest = jnp.maximum(
            jnp.max(scores, axis=1, keepdims=True), jnp.max(own_scores, axis=1, keepdims=True)
        )
        raised = jnp.exp(scores - highest)
        own_raised = jnp.exp(own_scores - highest)
        total = jnp.sum(raised, axis=1, keepdims=True) + jnp.sum(own_raised, axis=1, keepdims=True)
        weights = (raised / total).astype(BF16)
        own_weights = (own_raised / total).astype(BF16)
        attended = (nn(weights, v_ref[held, :]) + nn(own_weights, own_values[members])).astype(BF16)
        for h in range(heads):
            out_ref[members, h * HEAD_SIZE : (h + 1) * HEAD_SIZE] = attended[
                h * GROUP : (h + 1) * GROUP
            ]


def output_kernel(count, attended_ref, wo_ref, wo_other_ref, small_ref, small_other_ref, up_ref, up_other_ref, *blocks):
    core = lax.axis_index("tensor")
    slots, cols = attended_ref.shape
    hcols = cols // 2
    per_block, half = blocks[0].shape
    kept = per_block // 2
    rows = count * per_block
    slot = iota((rows, slots), 0)
    slot = slot // per_block * kept + slot % kept
    attended = nn(ones_where(iota((rows, slots), 1) == slot), attended_ref[...]).astype(BF16)
    left, right = attended[:, :hcols], attended[:, hcols:]
    down = slice(small_ref.shape[1] - hcols, small_ref.shape[1])
    ranks = (nt(left, small_ref[:, down]) + nt(right, small_other_ref[:, down])).astype(BF16)
    step = 512
    side = iota((rows, step), 0) % per_block // kept
    for c in range(0, half, step):
        near, far = slice(c, c + step), slice(half + c, half + c + step)
        terms = jnp.where(
            side == 0,
            nn(left, wo_ref[:, near]) + nn(right, wo_other_ref[:, near]),
            nn(left, wo_ref[:, far]) + nn(right, wo_other_ref[:, far]),
        )
        delta = jnp.where(side == core, nn(ranks, up_ref[:, near]), nn(ranks, up_other_ref[:, near]))
        done = (terms + delta.astype(BF16).astype(F32)).astype(BF16)
        for j, block in enumerate(blocks):
            block[:, near] = done[j * per_block : (j + 1) * per_block]


def pick_kernel(count, *refs):
    blocks = refs[: 2 * count]
    named_ref, table_ref, out_ref = refs[2 * count :]
    core = lax.axis_index("tensor")
    owners = 2 * count
    per_block, half = blocks[0].shape
    rows = owners * per_block
    requests = out_ref.shape[0]
    owner, standing = owner_and_standing(named_ref[...], table_ref[...])
    ahead = owner - lax.axis_index("adapter") - core * count
    ahead = jnp.where(ahead < -owners, ahead + 2 * owners, jnp.where(ahead < 0, ahead + owners, ahead))
    source = ahead * per_block + core * (per_block // 2) + standing
    place = ones_where(iota((rows, requests), 0) == source)
    step = 512
    for c in range(0, half, step):
        out_ref[:, c : c + step] = lax.dot_general(
            place,
            stacked(blocks, slice(c, c + step)),
            (((0,), (0,)), ((), ())),
            preferred_element_type=F32,
        ).astype(BF16)


OUTSIDE = pl.BlockSpec(memory_space=pltpu.HBM)
INSIDE = pl.BlockSpec(memory_space=pltpu.VMEM)


def call(kernel, outs, scratch=(), vmem=8, outside=(), out_spec=INSIDE, moved=0):
    many = isinstance(outs, (list, tuple))
    return lambda *args: pl.pallas_call(
        kernel,
        out_shape=outs,
        in_specs=[OUTSIDE if i in outside else INSIDE for i in range(len(args))],
        out_specs=[out_spec] * len(outs) if many else out_spec,
        scratch_shapes=list(scratch),
        compiler_params=pltpu.CompilerParams(vmem_limit_bytes=vmem * MIB),
        cost_estimate=pl.CostEstimate(flops=0, bytes_accessed=moved, transcendentals=0),
    )(
        *[
            pltpu.with_memory_space_constraint(arg, pltpu.HBM) if i in outside else arg
            for i, arg in enumerate(args)
        ]
    )


def body(
    layer_input,
    input_norm_gain,
    query_projection,
    key_projection,
    value_projection,
    output_projection,
    cached_key_rows,
    cached_value_rows,
    request_adapter,
    adapter_row_table,
    cached_length,
    projection_adapter_down,
    query_adapter_up,
    key_value_adapter_up,
    output_adapter_down,
    output_adapter_up,
):
    shape = jax.ShapeDtypeStruct
    requests, width = layer_input.shape
    owners = lax.axis_size("adapter")
    adapters = adapter_row_table.shape[0]
    positions = cached_key_rows.shape[1]
    half = width // 2
    capacity = max(2, 2 * ((requests + adapters - 1) // adapters))
    count = owners // 2
    kept = (capacity + 3) // 4 * 4
    slots = count * kept
    block = shape((2 * kept, width + LANES), BF16)
    named = request_adapter.reshape(1, requests)
    table = adapter_row_table.reshape(1, adapters)

    rank, qcols = query_adapter_up.shape[1:]
    hcols = key_value_adapter_up.shape[3]
    hrows = output_projection.shape[0]
    *packed, small = call(
        functools.partial(pack_kernel, capacity),
        [block] * count + [shape((rank, qcols + 2 * hcols + hrows), BF16)],
        [
            pltpu.VMEM((requests, width), BF16),
            pltpu.VMEM((1, width), F32),
            pltpu.VMEM((positions * requests, LANES), BF16),
            pltpu.VMEM((positions * requests, LANES), BF16),
            pltpu.VMEM((1, requests), jnp.int32),
            pltpu.VMEM((1, adapters), jnp.int32),
            pltpu.VMEM((1, requests), jnp.int32),
            pltpu.VMEM((2 * requests, width), BF16),
            pltpu.VMEM((positions * requests, LANES), F32),
            pltpu.VMEM((rank, qcols), BF16),
            pltpu.VMEM((2, rank, hcols), BF16),
            pltpu.VMEM((rank, hrows), BF16),
            pltpu.SemaphoreType.DMA((10,)),
        ],
        outside=range(10),
    )(
        layer_input,
        input_norm_gain.reshape(1, width),
        cached_key_rows.reshape(requests * positions, HEAD_SIZE),
        cached_value_rows.reshape(requests * positions, HEAD_SIZE),
        named,
        table,
        cached_length.reshape(1, requests),
        query_adapter_up[0],
        key_value_adapter_up[0],
        output_adapter_down[0].T,
    )
    down = projection_adapter_down[0].T
    wk, wv = key_projection.T, value_projection.T
    kvcols = 2 * wk.shape[0]
    *packed, query_projection, wk, wv, down, output_projection = lax.optimization_barrier(
        (*packed, query_projection, wk, wv, down, output_projection)
    )
    weights = call(
        stage_kernel,
        [
            shape(query_projection.shape, BF16),
            shape((kvcols, width), BF16),
            shape(down.shape, BF16),
        ],
        [pltpu.SemaphoreType.DMA((8,))],
        outside=range(4),
        moved=2 * (query_projection.size + kvcols * width + down.size),
    )(query_projection, wk, wv, down)

    def onward(n):
        return [
            (a * 2 + t, (a + t * count + n) % owners * 2 + t) for a in range(owners) for t in range(2)
        ]

    arrived = [
        lax.ppermute(one, ("adapter", "tensor"), onward(n)) for n, one in enumerate(packed)
    ]
    arrived[0], *weights = lax.optimization_barrier((arrived[0], *weights))
    passed = [lax.ppermute(one, "tensor", SWAP) for one in arrived]
    wo_other = lax.ppermute(output_projection, "tensor", SWAP)
    pcols = qcols + kvcols + (down.shape[0] + LANES - 1) // LANES * LANES
    mine, theirs = call(
        functools.partial(project_kernel, count),
        [shape((slots, pcols), F32), shape((slots, pcols), F32)],
        [pltpu.VMEM((pcols // LANES, 4 * slots, LANES), F32)],
        vmem=24,
    )(*arrived, *passed, *weights)
    theirs, mine, small, out_up = lax.optimization_barrier(
        (theirs, mine, small, output_adapter_up[0])
    )
    theirs = lax.ppermute(theirs, "tensor", SWAP)
    small_other = lax.ppermute(small, "tensor", SWAP)
    out_up_other = lax.ppermute(out_up, "tensor", SWAP)
    keys, values, lengths, cosine, sine = call(
        functools.partial(unpack_kernel, count),
        [shape((slots * positions, HEAD_SIZE), BF16)] * 2 + [shape((slots, LANES), F32)] * 3,
    )(*arrived)
    attended = call(attend_kernel, shape((slots, 2 * qcols), BF16), vmem=16)(
        mine, theirs, small, small_other, keys, values, lengths, cosine, sine
    )
    finished = call(
        functools.partial(output_kernel, count),
        [shape((2 * kept, half), BF16)] * count,
        vmem=16,
    )(attended, output_projection, wo_other, small, small_other, out_up, out_up_other)
    returned = [
        lax.ppermute(one, ("adapter", "tensor"), [(b, a) for a, b in onward(n)])
        for n, one in enumerate(finished)
    ]
    returned += [lax.ppermute(one, "tensor", SWAP) for one in returned]
    return call(functools.partial(pick_kernel, count), shape((requests, half), BF16))(
        *returned, named, table
    )


def solution(mesh):
    placed = (
        P(("groups", "adapter"), None),
        P(),
        P(None, "tensor"),
        P(None, "tensor"),
        P(None, "tensor"),
        P("tensor", None),
        P(("groups", "adapter"), None, None),
        P(("groups", "adapter"), None, None),
        P(("groups", "adapter"), None),
        P(),
        P(("groups", "adapter")),
        P("adapter", "tensor", None),
        P("adapter", None, "tensor"),
        P("adapter", None, None, "tensor"),
        P("adapter", "tensor", None),
        P("adapter", None, "tensor"),
    )
    return jax.shard_map(
        body,
        mesh=mesh,
        in_specs=placed,
        out_specs=P(("groups", "adapter"), "tensor"),
        check_vma=False,
    )
```

```python
import functools
import math

import jax
import jax.numpy as jnp
from jax import lax
from jax.experimental import pallas as pl
from jax.experimental.pallas import tpu as pltpu
from jax.sharding import PartitionSpec as P

HEAD_SIZE = 128
LANES = 128
EPSILON = 1e-05
THETA = 500000.0
BF16 = jnp.bfloat16
F32 = jnp.float32
SWAP = [(0, 1), (1, 0)]
GROUP = 16
MIB = 1024 * 1024


def nn(a, b):
    return lax.dot_general(a, b, (((1,), (0,)), ((), ())), preferred_element_type=F32)


def nt(a, b):
    return lax.dot_general(a, b, (((1,), (1,)), ((), ())), preferred_element_type=F32)


def iota(shape, dim):
    return lax.broadcasted_iota(jnp.int32, shape, dim)


def ones_where(condition):
    return jnp.where(condition, 1.0, 0.0).astype(BF16)


def owner_and_standing(named, table):
    requests, adapters = named.shape[1], table.shape[1]
    table_column = jnp.sum(
        jnp.where(iota((adapters, adapters), 0) == iota((adapters, adapters), 1), table, 0),
        axis=1,
        keepdims=True,
    )
    owner = jnp.sum(
        jnp.where(iota((adapters, requests), 0) == named, table_column, 0), axis=0, keepdims=True
    )
    square = (requests, requests)
    owner_column = jnp.sum(
        jnp.where(iota(square, 0) == iota(square, 1), owner, 0), axis=1, keepdims=True
    )
    earlier = (owner_column == owner) & (iota(square, 0) < iota(square, 1))
    standing = jnp.sum(jnp.where(earlier, 1, 0), axis=0, keepdims=True)
    return owner, standing


def copy_all(pairs, sems):
    copies = [pltpu.make_async_copy(a, b, sems.at[i]) for i, (a, b) in enumerate(pairs)]
    for copy in copies:
        copy.start()
    return copies


def block_of(ahead, core, count):
    ahead = jnp.where(ahead < 0, ahead + 2 * count, ahead)
    return jnp.where(ahead // count == core, jnp.where(core == 0, count - 1 - ahead, ahead - count), -1)


def pack_kernel(capacity, x_hbm, gain_hbm, k_hbm, v_hbm, named_hbm, table_hbm, length_hbm, up_hbm, kv_up_hbm, out_down_hbm, *rest):
    up_ref, kv_up_ref, out_down_ref = rest[-4:-1]
    rest = rest[:-4] + rest[-1:]
    small_ref, x_ref, gain_ref, k_ref, v_ref, named_ref, table_ref, length_ref, flat_ref, spread_ref, sems = rest[-11:]
    blocks = rest[:-11]
    count = len(blocks)
    owners = 2 * count
    named_copy, table_copy, length_copy, x_copy, gain_copy, k_copy, v_copy, *up_copies = copy_all(
        [
            (named_hbm, named_ref),
            (table_hbm, table_ref),
            (length_hbm, length_ref),
            (x_hbm, x_ref),
            (gain_hbm, gain_ref),
            (k_hbm, k_ref),
            (v_hbm, v_ref),
            (up_hbm, up_ref),
            (kv_up_hbm, kv_up_ref),
            (out_down_hbm, out_down_ref),
        ],
        sems,
    )
    requests, width = x_ref.shape
    positions = k_ref.shape[0] // requests
    per_block = blocks[0].shape[0]
    rows = per_block * count
    named_copy.wait()
    table_copy.wait()
    length_copy.wait()
    owner, standing = owner_and_standing(named_ref[...], table_ref[...])
    block = block_of(owner - lax.axis_index("adapter"), lax.axis_index("tensor"), count)
    row = jnp.where(block < 0, -2, block * per_block + 2 * standing)
    order = iota((rows, requests), 0)
    put_x = ones_where(order == row)
    put_kv = ones_where(order == row + 1)
    put = jnp.concatenate([put_x, put_kv], axis=1)

    x_copy.wait()
    gain_copy.wait()
    floats = x_ref[...].astype(F32)
    scale = lax.rsqrt(jnp.mean(floats * floats, axis=1, keepdims=True) + EPSILON)
    flat_ref[0:requests, :] = (floats * scale * gain_ref[...]).astype(BF16)
    for n, (source, copy) in enumerate(((k_ref, k_copy), (v_ref, v_copy))):
        copy.wait()
        spread_ref[...] = source[...].astype(F32)
        for p in range(positions):
            to = slice((n * positions + p) * LANES, (n * positions + p + 1) * LANES)
            flat_ref[requests : 2 * requests, to] = spread_ref[
                pl.ds(p, requests, stride=positions), :
            ].astype(BF16)
    step = 512
    for c in range(0, width, step):
        placed = nn(put, flat_ref[:, c : c + step]).astype(BF16)
        for j, block in enumerate(blocks):
            block[:, c : c + step] = placed[j * per_block : (j + 1) * per_block]
    square = (requests, requests)
    length_column = jnp.sum(
        jnp.where(iota(square, 0) == iota(square, 1), length_ref[...], 0), axis=1, keepdims=True
    )
    lengths = jnp.broadcast_to(length_column.astype(F32), (requests, LANES)).astype(BF16)
    placed = nn(put_x, lengths).astype(BF16)
    for j, block in enumerate(blocks):
        block[:, width:] = placed[j * per_block : (j + 1) * per_block]
    for copy in up_copies:
        copy.wait()
    small_ref[...] = jnp.concatenate(
        [up_ref[...], kv_up_ref[0], kv_up_ref[1], out_down_ref[...]], axis=1
    )


def stacked(blocks, columns):
    return jnp.concatenate([block[:, columns] for block in blocks], axis=0)


def stage_kernel(wq_hbm, wk_hbm, wv_hbm, down_hbm, wq_ref, kv_ref, down_ref, sems):
    width = wq_hbm.shape[0]
    hcols = wk_hbm.shape[0]
    ranks = down_hbm.shape[0]
    pieces = 4
    pairs = [(wk_hbm, kv_ref.at[0:hcols, :]), (wv_hbm, kv_ref.at[hcols:, :])]
    for n in range(pieces):
        rows = pl.ds(n * (width // pieces), width // pieces)
        pairs.append((wq_hbm.at[rows, :], wq_ref.at[rows, :]))
    for n in range(2):
        rows = pl.ds(n * (ranks // 2), ranks // 2)
        pairs.append((down_hbm.at[rows, :], down_ref.at[rows, :]))
    for copy in copy_all(pairs, sems):
        copy.wait()


def project_kernel(count, *refs):
    blocks = refs[: 2 * count]
    wq_ref, kv_ref, down_ref, mine_ref, theirs_ref, sums_ref = refs[2 * count :]
    width = wq_ref.shape[0]
    half = down_ref.shape[1]
    slots = mine_ref.shape[0]
    rows = sums_ref.shape[1]
    x_all = stacked(blocks, slice(0, width))
    halves = [x_all[:, :half], x_all[:, half:]]
    x_half = jnp.where(lax.axis_index("tensor") == 0, halves[0], halves[1])
    ranks = nt(x_half, down_ref[...])
    spare = jnp.zeros((rows, -ranks.shape[1] % LANES), F32)
    sums = [nn(x_all, wq_ref[...]), nt(x_all, kv_ref[...]), jnp.concatenate([ranks, spare], axis=1)]
    tile = 0
    for part in sums:
        for c in range(0, part.shape[1], LANES):
            sums_ref[tile] = part[:, c : c + LANES]
            columns = slice(tile * LANES, (tile + 1) * LANES)
            mine_ref[:, columns] = sums_ref[tile, pl.ds(0, slots, stride=2), :]
            theirs_ref[:, columns] = sums_ref[tile, pl.ds(rows // 2, slots, stride=2), :]
            tile += 1


def unpack_kernel(count, *refs):
    blocks = refs[:count]
    k_ref, v_ref, length_ref, cosine_ref, sine_ref = refs[count:]
    slots = length_ref.shape[0]
    per_block = blocks[0].shape[0]
    positions = k_ref.shape[0] // slots
    width = 2 * positions * LANES
    together = GROUP // (per_block // 2)
    pick = iota((GROUP, 2 * GROUP), 1) - 2 * iota((GROUP, 2 * GROUP), 0)
    pick_x, pick_kv = ones_where(pick == 0), ones_where(pick == 1)
    step = 512
    for g in range(slots // GROUP):
        members = blocks[g * together : (g + 1) * together]
        for c in range(0, width, step):
            picked = nn(pick_kv, stacked(members, slice(c, c + step))).astype(BF16)
            for j in range(step // LANES):
                p = c // LANES + j
                target, p = (k_ref, p) if p < positions else (v_ref, p - positions)
                first = (g * positions + p) * GROUP
                target[first : first + GROUP, :] = picked[:, j * LANES : (j + 1) * LANES]
        length_ref[g * GROUP : (g + 1) * GROUP, :] = nn(
            pick_x, stacked(members, slice(width, width + LANES))
        )
    halfway = HEAD_SIZE // 2
    lane = iota((slots, LANES), 1)
    exponent = (lane % halfway).astype(F32) * (-math.log(THETA) / halfway)
    angle = length_ref[...] * jnp.exp(exponent)
    cosine_ref[...] = jnp.cos(angle)
    sine = jnp.sin(angle)
    sine_ref[...] = jnp.where(lane < halfway, -sine, sine)


def attend_kernel(mine_ref, theirs_ref, small_ref, small_other_ref, k_ref, v_ref, length_ref, cosine_ref, sine_ref, out_ref):
    core = lax.axis_index("tensor")
    slots = mine_ref.shape[0]
    rank = small_ref.shape[0]
    kvcols = LANES
    qcols = out_ref.shape[1] // 2
    heads = 2 * qcols // HEAD_SIZE
    halfway = HEAD_SIZE // 2
    both = qcols + kvcols
    mine = mine_ref[...]
    theirs = theirs_ref[...]
    ranks = (mine + theirs)[:, both : both + 3 * rank].astype(BF16)
    ranks = [ranks[:, n * rank : (n + 1) * rank] for n in range(3)]

    def added(projected, up_ref):
        change = jnp.concatenate(
            [
                nn(ranks[0], up_ref[:, :qcols]),
                nn(ranks[1], up_ref[:, qcols : qcols + halfway]),
                nn(ranks[2], up_ref[:, qcols + halfway : both]),
            ],
            axis=1,
        )
        return projected[:, :both] + change.astype(BF16).astype(F32)

    mine = added(mine, small_ref)
    theirs = added(theirs, small_other_ref)
    combined = jnp.concatenate([mine[:, :qcols], theirs[:, :qcols]], axis=1)
    cosine, sine = cosine_ref[...], sine_ref[...]

    def rotate(part):
        return part * cosine + pltpu.roll(part, halfway, 1) * sine

    queries = [
        rotate(combined[:, h * HEAD_SIZE : (h + 1) * HEAD_SIZE]).astype(BF16) for h in range(heads)
    ]
    kv_mine = mine[:, qcols:]
    kv_theirs = theirs[:, qcols:]
    leading = jnp.where(core == 0, kv_mine, kv_theirs)
    trailing = jnp.where(core == 0, kv_theirs, kv_mine)
    first = iota((slots, LANES), 1) < halfway
    own_keys = rotate(jnp.where(first, leading, pltpu.roll(trailing, halfway, 1))).astype(BF16)
    own_values = jnp.where(first, pltpu.roll(leading, halfway, 1), trailing).astype(BF16)

    cached = k_ref.shape[0] * GROUP // slots
    rows = heads * GROUP
    shrink = math.sqrt(HEAD_SIZE)
    column = iota((rows, cached), 1)
    same = column % GROUP == iota((rows, cached), 0) % GROUP
    position = column // GROUP
    own = iota((rows, GROUP), 1) == iota((rows, GROUP), 0) % GROUP
    for g in range(slots // GROUP):
        members = slice(g * GROUP, (g + 1) * GROUP)
        held = slice(g * cached, (g + 1) * cached)
        query = jnp.concatenate([part[members] for part in queries], axis=0)
        length = jnp.concatenate([length_ref[members, 0:1]] * heads, axis=0).astype(jnp.int32)
        scores = jnp.where(
            same & (position < length), nt(query, k_ref[held, :]) / shrink, -jnp.inf
        )
        own_scores = jnp.where(own, nt(query, own_keys[members]) / shrink, -jnp.inf)
        highest = jnp.maximum(
            jnp.max(scores, axis=1, keepdims=True), jnp.max(own_scores, axis=1, keepdims=True)
        )
        raised = jnp.exp(scores - highest)
        own_raised = jnp.exp(own_scores - highest)
        total = jnp.sum(raised, axis=1, keepdims=True) + jnp.sum(own_raised, axis=1, keepdims=True)
        weights = (raised / total).astype(BF16)
        own_weights = (own_raised / total).astype(BF16)
        attended = (nn(weights, v_ref[held, :]) + nn(own_weights, own_values[members])).astype(BF16)
        for h in range(heads):
            out_ref[members, h * HEAD_SIZE : (h + 1) * HEAD_SIZE] = attended[
                h * GROUP : (h + 1) * GROUP
            ]


def output_kernel(count, attended_ref, wo_ref, wo_other_ref, small_ref, small_other_ref, up_ref, up_other_ref, *blocks):
    core = lax.axis_index("tensor")
    slots, cols = attended_ref.shape
    hcols = cols // 2
    per_block, half = blocks[0].shape
    kept = per_block // 2
    rows = count * per_block
    slot = iota((rows, slots), 0)
    slot = slot // per_block * kept + slot % kept
    attended = nn(ones_where(iota((rows, slots), 1) == slot), attended_ref[...]).astype(BF16)
    left, right = attended[:, :hcols], attended[:, hcols:]
    down = slice(small_ref.shape[1] - hcols, small_ref.shape[1])
    ranks = (nt(left, small_ref[:, down]) + nt(right, small_other_ref[:, down])).astype(BF16)
    step = 512
    side = iota((rows, step), 0) % per_block // kept
    for c in range(0, half, step):
        near, far = slice(c, c + step), slice(half + c, half + c + step)
        terms = jnp.where(
            side == 0,
            nn(left, wo_ref[:, near]) + nn(right, wo_other_ref[:, near]),
            nn(left, wo_ref[:, far]) + nn(right, wo_other_ref[:, far]),
        )
        delta = jnp.where(side == core, nn(ranks, up_ref[:, near]), nn(ranks, up_other_ref[:, near]))
        done = (terms + delta.astype(BF16).astype(F32)).astype(BF16)
        for j, block in enumerate(blocks):
            block[:, near] = done[j * per_block : (j + 1) * per_block]


def pick_kernel(count, *refs):
    blocks = refs[: 2 * count]
    named_ref, table_ref, out_ref = refs[2 * count :]
    core = lax.axis_index("tensor")
    owners = 2 * count
    per_block, half = blocks[0].shape
    rows = owners * per_block
    requests = out_ref.shape[0]
    owner, standing = owner_and_standing(named_ref[...], table_ref[...])
    ahead = owner - lax.axis_index("adapter")
    mine, theirs = block_of(ahead, core, count), block_of(ahead, 1 - core, count)
    source = jnp.where(mine < 0, count + theirs, mine) * per_block
    source = source + core * (per_block // 2) + standing
    place = ones_where(iota((rows, requests), 0) == source)
    step = 512
    for c in range(0, half, step):
        out_ref[:, c : c + step] = lax.dot_general(
            place,
            stacked(blocks, slice(c, c + step)),
            (((0,), (0,)), ((), ())),
            preferred_element_type=F32,
        ).astype(BF16)


OUTSIDE = pl.BlockSpec(memory_space=pltpu.HBM)
INSIDE = pl.BlockSpec(memory_space=pltpu.VMEM)


def call(kernel, outs, scratch=(), vmem=8, outside=(), out_spec=INSIDE, moved=0):
    many = isinstance(outs, (list, tuple))
    return lambda *args: pl.pallas_call(
        kernel,
        out_shape=outs,
        in_specs=[OUTSIDE if i in outside else INSIDE for i in range(len(args))],
        out_specs=[out_spec] * len(outs) if many else out_spec,
        scratch_shapes=list(scratch),
        compiler_params=pltpu.CompilerParams(vmem_limit_bytes=vmem * MIB),
        cost_estimate=pl.CostEstimate(flops=0, bytes_accessed=moved, transcendentals=0),
    )(
        *[
            pltpu.with_memory_space_constraint(arg, pltpu.HBM) if i in outside else arg
            for i, arg in enumerate(args)
        ]
    )


def body(
    layer_input,
    input_norm_gain,
    query_projection,
    key_projection,
    value_projection,
    output_projection,
    cached_key_rows,
    cached_value_rows,
    request_adapter,
    adapter_row_table,
    cached_length,
    projection_adapter_down,
    query_adapter_up,
    key_value_adapter_up,
    output_adapter_down,
    output_adapter_up,
):
    shape = jax.ShapeDtypeStruct
    requests, width = layer_input.shape
    owners = lax.axis_size("adapter")
    adapters = adapter_row_table.shape[0]
    positions = cached_key_rows.shape[1]
    half = width // 2
    capacity = max(2, 2 * ((requests + adapters - 1) // adapters))
    count = owners // 2
    kept = (capacity + 3) // 4 * 4
    slots = count * kept
    block = shape((2 * kept, width + LANES), BF16)
    named = request_adapter.reshape(1, requests)
    table = adapter_row_table.reshape(1, adapters)

    rank, qcols = query_adapter_up.shape[1:]
    hcols = key_value_adapter_up.shape[3]
    hrows = output_projection.shape[0]
    *packed, small = call(
        functools.partial(pack_kernel, capacity),
        [block] * count + [shape((rank, qcols + 2 * hcols + hrows), BF16)],
        [
            pltpu.VMEM((requests, width), BF16),
            pltpu.VMEM((1, width), F32),
            pltpu.VMEM((positions * requests, LANES), BF16),
            pltpu.VMEM((positions * requests, LANES), BF16),
            pltpu.VMEM((1, requests), jnp.int32),
            pltpu.VMEM((1, adapters), jnp.int32),
            pltpu.VMEM((1, requests), jnp.int32),
            pltpu.VMEM((2 * requests, width), BF16),
            pltpu.VMEM((positions * requests, LANES), F32),
            pltpu.VMEM((rank, qcols), BF16),
            pltpu.VMEM((2, rank, hcols), BF16),
            pltpu.VMEM((rank, hrows), BF16),
            pltpu.SemaphoreType.DMA((10,)),
        ],
        outside=range(10),
    )(
        layer_input,
        input_norm_gain.reshape(1, width),
        cached_key_rows.reshape(requests * positions, HEAD_SIZE),
        cached_value_rows.reshape(requests * positions, HEAD_SIZE),
        named,
        table,
        cached_length.reshape(1, requests),
        query_adapter_up[0],
        key_value_adapter_up[0],
        output_adapter_down[0].T,
    )
    down = projection_adapter_down[0].T
    wk, wv = key_projection.T, value_projection.T
    kvcols = 2 * wk.shape[0]
    *packed, query_projection, wk, wv, down, output_projection = lax.optimization_barrier(
        (*packed, query_projection, wk, wv, down, output_projection)
    )
    weights = call(
        stage_kernel,
        [
            shape(query_projection.shape, BF16),
            shape((kvcols, width), BF16),
            shape(down.shape, BF16),
        ],
        [pltpu.SemaphoreType.DMA((8,))],
        outside=range(4),
        moved=2 * (query_projection.size + kvcols * width + down.size),
    )(query_projection, wk, wv, down)

    def onward(n):
        shifts = (count - 1 - n, count + n)
        return [
            (a * 2 + t, (a + shifts[t]) % owners * 2 + t) for a in range(owners) for t in range(2)
        ]

    arrived = [
        lax.ppermute(one, ("adapter", "tensor"), onward(n)) for n, one in enumerate(packed)
    ]
    arrived[0], *weights = lax.optimization_barrier((arrived[0], *weights))
    passed = [lax.ppermute(one, "tensor", SWAP) for one in arrived]
    wo_other = lax.ppermute(output_projection, "tensor", SWAP)
    pcols = qcols + kvcols + (down.shape[0] + LANES - 1) // LANES * LANES
    mine, theirs = call(
        functools.partial(project_kernel, count),
        [shape((slots, pcols), F32), shape((slots, pcols), F32)],
        [pltpu.VMEM((pcols // LANES, 4 * slots, LANES), F32)],
        vmem=24,
    )(*arrived, *passed, *weights)
    theirs, mine, small, out_up = lax.optimization_barrier(
        (theirs, mine, small, output_adapter_up[0])
    )
    theirs = lax.ppermute(theirs, "tensor", SWAP)
    small_other = lax.ppermute(small, "tensor", SWAP)
    out_up_other = lax.ppermute(out_up, "tensor", SWAP)
    keys, values, lengths, cosine, sine = call(
        functools.partial(unpack_kernel, count),
        [shape((slots * positions, HEAD_SIZE), BF16)] * 2 + [shape((slots, LANES), F32)] * 3,
    )(*arrived)
    attended = call(attend_kernel, shape((slots, 2 * qcols), BF16), vmem=16)(
        mine, theirs, small, small_other, keys, values, lengths, cosine, sine
    )
    finished = call(
        functools.partial(output_kernel, count),
        [shape((2 * kept, half), BF16)] * count,
        vmem=16,
    )(attended, output_projection, wo_other, small, small_other, out_up, out_up_other)
    returned = [
        lax.ppermute(one, ("adapter", "tensor"), [(b, a) for a, b in onward(n)])
        for n, one in enumerate(finished)
    ]
    returned += [lax.ppermute(one, "tensor", SWAP) for one in returned]
    return call(functools.partial(pick_kernel, count), shape((requests, half), BF16))(
        *returned, named, table
    )


def solution(mesh):
    placed = (
        P(("groups", "adapter"), None),
        P(),
        P(None, "tensor"),
        P(None, "tensor"),
        P(None, "tensor"),
        P("tensor", None),
        P(("groups", "adapter"), None, None),
        P(("groups", "adapter"), None, None),
        P(("groups", "adapter"), None),
        P(),
        P(("groups", "adapter")),
        P("adapter", "tensor", None),
        P("adapter", None, "tensor"),
        P("adapter", None, None, "tensor"),
        P("adapter", "tensor", None),
        P("adapter", None, "tensor"),
    )
    return jax.shard_map(
        body,
        mesh=mesh,
        in_specs=placed,
        out_specs=P(("groups", "adapter"), "tensor"),
        check_vma=False,
    )
```

```python
import functools
import math

import jax
import jax.numpy as jnp
from jax import lax
from jax.experimental import pallas as pl
from jax.experimental.pallas import tpu as pltpu
from jax.sharding import PartitionSpec as P

HEAD_SIZE = 128
LANES = 128
EPSILON = 1e-05
THETA = 500000.0
BF16 = jnp.bfloat16
F32 = jnp.float32
SWAP = [(0, 1), (1, 0)]
GROUP = 16
MIB = 1024 * 1024


def nn(a, b):
    return lax.dot_general(a, b, (((1,), (0,)), ((), ())), preferred_element_type=F32)


def nt(a, b):
    return lax.dot_general(a, b, (((1,), (1,)), ((), ())), preferred_element_type=F32)


def iota(shape, dim):
    return lax.broadcasted_iota(jnp.int32, shape, dim)


def ones_where(condition):
    return jnp.where(condition, 1.0, 0.0).astype(BF16)


def owner_and_standing(named, table):
    requests, adapters = named.shape[1], table.shape[1]
    table_column = jnp.sum(
        jnp.where(iota((adapters, adapters), 0) == iota((adapters, adapters), 1), table, 0),
        axis=1,
        keepdims=True,
    )
    owner = jnp.sum(
        jnp.where(iota((adapters, requests), 0) == named, table_column, 0), axis=0, keepdims=True
    )
    square = (requests, requests)
    owner_column = jnp.sum(
        jnp.where(iota(square, 0) == iota(square, 1), owner, 0), axis=1, keepdims=True
    )
    earlier = (owner_column == owner) & (iota(square, 0) < iota(square, 1))
    standing = jnp.sum(jnp.where(earlier, 1, 0), axis=0, keepdims=True)
    return owner, standing


def copy_all(pairs, sems):
    copies = [pltpu.make_async_copy(a, b, sems.at[i]) for i, (a, b) in enumerate(pairs)]
    for copy in copies:
        copy.start()
    return copies


def block_of(ahead, core, count):
    ahead = jnp.where(ahead < 0, ahead + 2 * count, ahead)
    return jnp.where(ahead // count == core, jnp.where(core == 0, count - 1 - ahead, ahead - count), -1)


def pack_kernel(capacity, x_hbm, gain_hbm, k_hbm, v_hbm, named_hbm, table_hbm, length_hbm, *rest):
    x_ref, gain_ref, k_ref, v_ref, named_ref, table_ref, length_ref, flat_ref, spread_ref, sems = rest[-10:]
    blocks = rest[:-10]
    count = len(blocks)
    owners = 2 * count
    named_copy, table_copy, length_copy, x_copy, gain_copy, k_copy, v_copy = copy_all(
        [
            (named_hbm, named_ref),
            (table_hbm, table_ref),
            (length_hbm, length_ref),
            (x_hbm, x_ref),
            (gain_hbm, gain_ref),
            (k_hbm, k_ref),
            (v_hbm, v_ref),
        ],
        sems,
    )
    requests, width = x_ref.shape
    positions = k_ref.shape[0] // requests
    per_block = blocks[0].shape[0]
    rows = per_block * count
    named_copy.wait()
    table_copy.wait()
    length_copy.wait()
    owner, standing = owner_and_standing(named_ref[...], table_ref[...])
    block = block_of(owner - lax.axis_index("adapter"), lax.axis_index("tensor"), count)
    row = jnp.where(block < 0, -2, block * per_block + 2 * standing)
    order = iota((rows, requests), 0)
    put_x = ones_where(order == row)
    put_kv = ones_where(order == row + 1)
    put = jnp.concatenate([put_x, put_kv], axis=1)

    x_copy.wait()
    gain_copy.wait()
    floats = x_ref[...].astype(F32)
    scale = lax.rsqrt(jnp.mean(floats * floats, axis=1, keepdims=True) + EPSILON)
    flat_ref[0:requests, :] = (floats * scale * gain_ref[...]).astype(BF16)
    for n, (source, copy) in enumerate(((k_ref, k_copy), (v_ref, v_copy))):
        copy.wait()
        spread_ref[...] = source[...].astype(F32)
        for p in range(positions):
            to = slice((n * positions + p) * LANES, (n * positions + p + 1) * LANES)
            flat_ref[requests : 2 * requests, to] = spread_ref[
                pl.ds(p, requests, stride=positions), :
            ].astype(BF16)
    step = 512
    for c in range(0, width, step):
        placed = nn(put, flat_ref[:, c : c + step]).astype(BF16)
        for j, block in enumerate(blocks):
            block[:, c : c + step] = placed[j * per_block : (j + 1) * per_block]
    square = (requests, requests)
    length_column = jnp.sum(
        jnp.where(iota(square, 0) == iota(square, 1), length_ref[...], 0), axis=1, keepdims=True
    )
    lengths = jnp.broadcast_to(length_column.astype(F32), (requests, LANES)).astype(BF16)
    placed = nn(put_x, lengths).astype(BF16)
    for j, block in enumerate(blocks):
        block[:, width:] = placed[j * per_block : (j + 1) * per_block]


def stacked(blocks, columns):
    return jnp.concatenate([block[:, columns] for block in blocks], axis=0)


def stage_kernel(wq_hbm, wk_hbm, wv_hbm, down_hbm, up_hbm, kv_up_hbm, out_down_hbm, out_up_hbm, wq_ref, kv_ref, down_ref, small_ref, up_ref, kv_up_ref, out_down_ref, sems):
    width = wq_hbm.shape[0]
    hcols = wk_hbm.shape[0]
    ranks = down_hbm.shape[0]
    pieces = 4
    pairs = [
        (up_hbm, up_ref),
        (kv_up_hbm, kv_up_ref),
        (out_down_hbm, out_down_ref),
        (wk_hbm, kv_ref.at[0:hcols, :]),
        (wv_hbm, kv_ref.at[hcols:, :]),
        (out_up_hbm, small_ref.at[:, 0 : out_up_hbm.shape[1]]),
    ]
    for n in range(pieces):
        rows = pl.ds(n * (width // pieces), width // pieces)
        pairs.append((wq_hbm.at[rows, :], wq_ref.at[rows, :]))
    for n in range(2):
        rows = pl.ds(n * (ranks // 2), ranks // 2)
        pairs.append((down_hbm.at[rows, :], down_ref.at[rows, :]))
    copies = copy_all(pairs, sems)
    for copy in copies[:3]:
        copy.wait()
    small_ref[:, out_up_hbm.shape[1] :] = jnp.concatenate(
        [up_ref[...], kv_up_ref[0], kv_up_ref[1], out_down_ref[...]], axis=1
    )
    for copy in copies[3:]:
        copy.wait()


def project_kernel(count, *refs):
    blocks = refs[: 2 * count]
    wq_ref, kv_ref, down_ref, mine_ref, theirs_ref, sums_ref = refs[2 * count :]
    width = wq_ref.shape[0]
    half = down_ref.shape[1]
    slots = mine_ref.shape[0]
    rows = sums_ref.shape[1]
    x_all = stacked(blocks, slice(0, width))
    halves = [x_all[:, :half], x_all[:, half:]]
    x_half = jnp.where(lax.axis_index("tensor") == 0, halves[0], halves[1])
    ranks = nt(x_half, down_ref[...])
    spare = jnp.zeros((rows, -ranks.shape[1] % LANES), F32)
    sums = [nn(x_all, wq_ref[...]), nt(x_all, kv_ref[...]), jnp.concatenate([ranks, spare], axis=1)]
    tile = 0
    for part in sums:
        for c in range(0, part.shape[1], LANES):
            sums_ref[tile] = part[:, c : c + LANES]
            columns = slice(tile * LANES, (tile + 1) * LANES)
            mine_ref[:, columns] = sums_ref[tile, pl.ds(0, slots, stride=2), :]
            theirs_ref[:, columns] = sums_ref[tile, pl.ds(rows // 2, slots, stride=2), :]
            tile += 1


def unpack_kernel(count, *refs):
    blocks = refs[:count]
    named_ref, table_ref, k_ref, v_ref, length_ref, cosine_ref, sine_ref, place_ref = refs[count:]
    requests, rows = place_ref.shape
    core = lax.axis_index("tensor")
    owner, standing = owner_and_standing(named_ref[...], table_ref[...])
    ahead = owner - lax.axis_index("adapter")
    near, far = block_of(ahead, core, count), block_of(ahead, 1 - core, count)
    back = rows // (2 * count)
    source = jnp.where(near < 0, count + far, near) * back + core * (back // 2) + standing
    square = (requests, requests)
    source = jnp.sum(
        jnp.where(iota(square, 0) == iota(square, 1), source, 0), axis=1, keepdims=True
    )
    place_ref[...] = ones_where(iota((requests, rows), 1) == source)
    slots = length_ref.shape[0]
    per_block = blocks[0].shape[0]
    positions = k_ref.shape[0] // slots
    width = 2 * positions * LANES
    together = GROUP // (per_block // 2)
    pick = iota((GROUP, 2 * GROUP), 1) - 2 * iota((GROUP, 2 * GROUP), 0)
    pick_x, pick_kv = ones_where(pick == 0), ones_where(pick == 1)
    step = 512
    for g in range(slots // GROUP):
        members = blocks[g * together : (g + 1) * together]
        for c in range(0, width, step):
            picked = nn(pick_kv, stacked(members, slice(c, c + step))).astype(BF16)
            for j in range(step // LANES):
                p = c // LANES + j
                target, p = (k_ref, p) if p < positions else (v_ref, p - positions)
                first = (g * positions + p) * GROUP
                target[first : first + GROUP, :] = picked[:, j * LANES : (j + 1) * LANES]
        length_ref[g * GROUP : (g + 1) * GROUP, :] = nn(
            pick_x, stacked(members, slice(width, width + LANES))
        )
    halfway = HEAD_SIZE // 2
    lane = iota((slots, LANES), 1)
    exponent = (lane % halfway).astype(F32) * (-math.log(THETA) / halfway)
    angle = length_ref[...] * jnp.exp(exponent)
    cosine_ref[...] = jnp.cos(angle)
    sine = jnp.sin(angle)
    sine_ref[...] = jnp.where(lane < halfway, -sine, sine)


def attend_kernel(mine_ref, theirs_ref, small_ref, small_other_ref, k_ref, v_ref, length_ref, cosine_ref, sine_ref, out_ref):
    core = lax.axis_index("tensor")
    slots = mine_ref.shape[0]
    rank = small_ref.shape[0]
    kvcols = LANES
    qcols = out_ref.shape[1] // 2
    heads = 2 * qcols // HEAD_SIZE
    halfway = HEAD_SIZE // 2
    both = qcols + kvcols
    base = small_ref.shape[1] - both - qcols
    mine = mine_ref[...]
    theirs = theirs_ref[...]
    ranks = (mine + theirs)[:, both : both + 3 * rank].astype(BF16)
    ranks = [ranks[:, n * rank : (n + 1) * rank] for n in range(3)]

    def added(projected, up_ref):
        change = jnp.concatenate(
            [
                nn(ranks[0], up_ref[:, base : base + qcols]),
                nn(ranks[1], up_ref[:, base + qcols : base + qcols + halfway]),
                nn(ranks[2], up_ref[:, base + qcols + halfway : base + both]),
            ],
            axis=1,
        )
        return projected[:, :both] + change.astype(BF16).astype(F32)

    mine = added(mine, small_ref)
    theirs = added(theirs, small_other_ref)
    combined = jnp.concatenate([mine[:, :qcols], theirs[:, :qcols]], axis=1)
    cosine, sine = cosine_ref[...], sine_ref[...]

    def rotate(part):
        return part * cosine + pltpu.roll(part, halfway, 1) * sine

    queries = [
        rotate(combined[:, h * HEAD_SIZE : (h + 1) * HEAD_SIZE]).astype(BF16) for h in range(heads)
    ]
    kv_mine = mine[:, qcols:]
    kv_theirs = theirs[:, qcols:]
    leading = jnp.where(core == 0, kv_mine, kv_theirs)
    trailing = jnp.where(core == 0, kv_theirs, kv_mine)
    first = iota((slots, LANES), 1) < halfway
    own_keys = rotate(jnp.where(first, leading, pltpu.roll(trailing, halfway, 1))).astype(BF16)
    own_values = jnp.where(first, pltpu.roll(leading, halfway, 1), trailing).astype(BF16)

    cached = k_ref.shape[0] * GROUP // slots
    rows = heads * GROUP
    shrink = math.sqrt(HEAD_SIZE)
    column = iota((rows, cached), 1)
    same = column % GROUP == iota((rows, cached), 0) % GROUP
    position = column // GROUP
    own = iota((rows, GROUP), 1) == iota((rows, GROUP), 0) % GROUP
    for g in range(slots // GROUP):
        members = slice(g * GROUP, (g + 1) * GROUP)
        held = slice(g * cached, (g + 1) * cached)
        query = jnp.concatenate([part[members] for part in queries], axis=0)
        length = jnp.concatenate([length_ref[members, 0:1]] * heads, axis=0).astype(jnp.int32)
        scores = jnp.where(
            same & (position < length), nt(query, k_ref[held, :]) / shrink, -jnp.inf
        )
        own_scores = jnp.where(own, nt(query, own_keys[members]) / shrink, -jnp.inf)
        highest = jnp.maximum(
            jnp.max(scores, axis=1, keepdims=True), jnp.max(own_scores, axis=1, keepdims=True)
        )
        raised = jnp.exp(scores - highest)
        own_raised = jnp.exp(own_scores - highest)
        total = jnp.sum(raised, axis=1, keepdims=True) + jnp.sum(own_raised, axis=1, keepdims=True)
        weights = (raised / total).astype(BF16)
        own_weights = (own_raised / total).astype(BF16)
        attended = (nn(weights, v_ref[held, :]) + nn(own_weights, own_values[members])).astype(BF16)
        for h in range(heads):
            out_ref[members, h * HEAD_SIZE : (h + 1) * HEAD_SIZE] = attended[
                h * GROUP : (h + 1) * GROUP
            ]


def output_kernel(count, attended_ref, wo_ref, wo_other_ref, small_ref, small_other_ref, *blocks):
    core = lax.axis_index("tensor")
    slots, cols = attended_ref.shape
    hcols = cols // 2
    per_block, half = blocks[0].shape
    kept = per_block // 2
    rows = count * per_block
    slot = iota((rows, slots), 0)
    slot = slot // per_block * kept + slot % kept
    attended = nn(ones_where(iota((rows, slots), 1) == slot), attended_ref[...]).astype(BF16)
    left, right = attended[:, :hcols], attended[:, hcols:]
    down = slice(small_ref.shape[1] - hcols, small_ref.shape[1])
    ranks = (nt(left, small_ref[:, down]) + nt(right, small_other_ref[:, down])).astype(BF16)
    step = 512
    side = iota((rows, step), 0) % per_block // kept
    for c in range(0, half, step):
        near, far = slice(c, c + step), slice(half + c, half + c + step)
        terms = jnp.where(
            side == 0,
            nn(left, wo_ref[:, near]) + nn(right, wo_other_ref[:, near]),
            nn(left, wo_ref[:, far]) + nn(right, wo_other_ref[:, far]),
        )
        delta = jnp.where(side == core, nn(ranks, small_ref[:, near]), nn(ranks, small_other_ref[:, near]))
        done = (terms + delta.astype(BF16).astype(F32)).astype(BF16)
        for j, block in enumerate(blocks):
            block[:, near] = done[j * per_block : (j + 1) * per_block]


def pick_kernel(place_ref, *refs):
    blocks, out_ref = refs[:-1], refs[-1]
    step = 512
    for c in range(0, out_ref.shape[1], step):
        out_ref[:, c : c + step] = nn(place_ref[...], stacked(blocks, slice(c, c + step))).astype(BF16)


OUTSIDE = pl.BlockSpec(memory_space=pltpu.HBM)
INSIDE = pl.BlockSpec(memory_space=pltpu.VMEM)


def call(kernel, outs, scratch=(), vmem=8, outside=(), out_spec=INSIDE, moved=0):
    many = isinstance(outs, (list, tuple))
    return lambda *args: pl.pallas_call(
        kernel,
        out_shape=outs,
        in_specs=[OUTSIDE if i in outside else INSIDE for i in range(len(args))],
        out_specs=[out_spec] * len(outs) if many else out_spec,
        scratch_shapes=list(scratch),
        compiler_params=pltpu.CompilerParams(vmem_limit_bytes=vmem * MIB),
        cost_estimate=pl.CostEstimate(flops=0, bytes_accessed=moved, transcendentals=0),
    )(
        *[
            pltpu.with_memory_space_constraint(arg, pltpu.HBM) if i in outside else arg
            for i, arg in enumerate(args)
        ]
    )


def body(
    layer_input,
    input_norm_gain,
    query_projection,
    key_projection,
    value_projection,
    output_projection,
    cached_key_rows,
    cached_value_rows,
    request_adapter,
    adapter_row_table,
    cached_length,
    projection_adapter_down,
    query_adapter_up,
    key_value_adapter_up,
    output_adapter_down,
    output_adapter_up,
):
    shape = jax.ShapeDtypeStruct
    requests, width = layer_input.shape
    owners = lax.axis_size("adapter")
    adapters = adapter_row_table.shape[0]
    positions = cached_key_rows.shape[1]
    half = width // 2
    capacity = max(2, 2 * ((requests + adapters - 1) // adapters))
    count = owners // 2
    kept = (capacity + 3) // 4 * 4
    slots = count * kept
    block = shape((2 * kept, width + LANES), BF16)
    named = request_adapter.reshape(1, requests)
    table = adapter_row_table.reshape(1, adapters)

    rank, qcols = query_adapter_up.shape[1:]
    hcols = key_value_adapter_up.shape[3]
    hrows = output_projection.shape[0]
    packed = call(
        functools.partial(pack_kernel, capacity),
        [block] * count,
        [
            pltpu.VMEM((requests, width), BF16),
            pltpu.VMEM((1, width), F32),
            pltpu.VMEM((positions * requests, LANES), BF16),
            pltpu.VMEM((positions * requests, LANES), BF16),
            pltpu.VMEM((1, requests), jnp.int32),
            pltpu.VMEM((1, adapters), jnp.int32),
            pltpu.VMEM((1, requests), jnp.int32),
            pltpu.VMEM((2 * requests, width), BF16),
            pltpu.VMEM((positions * requests, LANES), F32),
            pltpu.SemaphoreType.DMA((7,)),
        ],
        outside=range(7),
    )(
        layer_input,
        input_norm_gain.reshape(1, width),
        cached_key_rows.reshape(requests * positions, HEAD_SIZE),
        cached_value_rows.reshape(requests * positions, HEAD_SIZE),
        named,
        table,
        cached_length.reshape(1, requests),
    )
    down = projection_adapter_down[0].T
    wk, wv = key_projection.T, value_projection.T
    kvcols = 2 * wk.shape[0]
    *packed, query_projection, wk, wv, down, output_projection = lax.optimization_barrier(
        (*packed, query_projection, wk, wv, down, output_projection)
    )
    *weights, small = call(
        stage_kernel,
        [
            shape(query_projection.shape, BF16),
            shape((kvcols, width), BF16),
            shape(down.shape, BF16),
            shape((rank, half + qcols + 2 * hcols + hrows), BF16),
        ],
        [
            pltpu.VMEM((rank, qcols), BF16),
            pltpu.VMEM((2, rank, hcols), BF16),
            pltpu.VMEM((rank, hrows), BF16),
            pltpu.SemaphoreType.DMA((12,)),
        ],
        outside=range(8),
        moved=2 * (query_projection.size + kvcols * width + down.size),
    )(
        query_projection,
        wk,
        wv,
        down,
        query_adapter_up[0],
        key_value_adapter_up[0],
        output_adapter_down[0].T,
        output_adapter_up[0],
    )

    def onward(n):
        shifts = (count - 1 - n, count + n)
        return [
            (a * 2 + t, (a + shifts[t]) % owners * 2 + t) for a in range(owners) for t in range(2)
        ]

    arrived = [
        lax.ppermute(one, ("adapter", "tensor"), onward(n)) for n, one in enumerate(packed)
    ]
    arrived[0], *weights = lax.optimization_barrier((arrived[0], *weights))
    passed = [lax.ppermute(one, "tensor", SWAP) for one in arrived]
    wo_other = lax.ppermute(output_projection, "tensor", SWAP)
    pcols = qcols + kvcols + (down.shape[0] + LANES - 1) // LANES * LANES
    mine, theirs = call(
        functools.partial(project_kernel, count),
        [shape((slots, pcols), F32), shape((slots, pcols), F32)],
        [pltpu.VMEM((pcols // LANES, 4 * slots, LANES), F32)],
        vmem=24,
    )(*arrived, *passed, *weights)
    theirs, mine, small = lax.optimization_barrier((theirs, mine, small))
    theirs = lax.ppermute(theirs, "tensor", SWAP)
    small_other = lax.ppermute(small, "tensor", SWAP)
    keys, values, lengths, cosine, sine, place = call(
        functools.partial(unpack_kernel, count),
        [shape((slots * positions, HEAD_SIZE), BF16)] * 2
        + [shape((slots, LANES), F32)] * 3
        + [shape((requests, 4 * slots), BF16)],
    )(*arrived, named, table)
    attended = call(attend_kernel, shape((slots, 2 * qcols), BF16), vmem=16)(
        mine, theirs, small, small_other, keys, values, lengths, cosine, sine
    )
    finished = call(
        functools.partial(output_kernel, count),
        [shape((2 * kept, half), BF16)] * count,
        vmem=16,
    )(attended, output_projection, wo_other, small, small_other)
    returned = [
        lax.ppermute(one, ("adapter", "tensor"), [(b, a) for a, b in onward(n)])
        for n, one in enumerate(finished)
    ]
    returned += [lax.ppermute(one, "tensor", SWAP) for one in returned]
    return call(pick_kernel, shape((requests, half), BF16))(place, *returned)


def solution(mesh):
    placed = (
        P(("groups", "adapter"), None),
        P(),
        P(None, "tensor"),
        P(None, "tensor"),
        P(None, "tensor"),
        P("tensor", None),
        P(("groups", "adapter"), None, None),
        P(("groups", "adapter"), None, None),
        P(("groups", "adapter"), None),
        P(),
        P(("groups", "adapter")),
        P("adapter", "tensor", None),
        P("adapter", None, "tensor"),
        P("adapter", None, None, "tensor"),
        P("adapter", "tensor", None),
        P("adapter", None, "tensor"),
    )
    return jax.shard_map(
        body,
        mesh=mesh,
        in_specs=placed,
        out_specs=P(("groups", "adapter"), "tensor"),
        check_vma=False,
    )
```

```python
import functools
import math

import jax
import jax.numpy as jnp
from jax import lax
from jax.experimental import pallas as pl
from jax.experimental.pallas import tpu as pltpu
from jax.sharding import PartitionSpec as P

HEAD_SIZE = 128
LANES = 128
EPSILON = 1e-05
THETA = 500000.0
BF16 = jnp.bfloat16
F32 = jnp.float32
SWAP = [(0, 1), (1, 0)]
GROUP = 16
MIB = 1024 * 1024


def nn(a, b):
    return lax.dot_general(a, b, (((1,), (0,)), ((), ())), preferred_element_type=F32)


def nt(a, b):
    return lax.dot_general(a, b, (((1,), (1,)), ((), ())), preferred_element_type=F32)


def iota(shape, dim):
    return lax.broadcasted_iota(jnp.int32, shape, dim)


def ones_where(condition):
    return jnp.where(condition, 1.0, 0.0).astype(BF16)


def owner_and_standing(named, table):
    requests, adapters = named.shape[1], table.shape[1]
    table_column = jnp.sum(
        jnp.where(iota((adapters, adapters), 0) == iota((adapters, adapters), 1), table, 0),
        axis=1,
        keepdims=True,
    )
    owner = jnp.sum(
        jnp.where(iota((adapters, requests), 0) == named, table_column, 0), axis=0, keepdims=True
    )
    square = (requests, requests)
    owner_column = jnp.sum(
        jnp.where(iota(square, 0) == iota(square, 1), owner, 0), axis=1, keepdims=True
    )
    earlier = (owner_column == owner) & (iota(square, 0) < iota(square, 1))
    standing = jnp.sum(jnp.where(earlier, 1, 0), axis=0, keepdims=True)
    return owner, standing


def copy_all(pairs, sems):
    copies = [pltpu.make_async_copy(a, b, sems.at[i]) for i, (a, b) in enumerate(pairs)]
    for copy in copies:
        copy.start()
    return copies


def block_of(ahead, core, count):
    ahead = jnp.where(ahead < 0, ahead + 2 * count, ahead)
    return jnp.where(ahead // count == core, jnp.where(core == 0, count - 1 - ahead, ahead - count), -1)


def pack_kernel(capacity, x_hbm, gain_hbm, k_hbm, v_hbm, named_hbm, table_hbm, length_hbm, *rest):
    x_ref, gain_ref, k_ref, v_ref, named_ref, table_ref, length_ref, flat_ref, spread_ref, sems = rest[-10:]
    blocks = rest[:-10]
    count = len(blocks)
    owners = 2 * count
    named_copy, table_copy, length_copy, x_copy, gain_copy, k_copy, v_copy = copy_all(
        [
            (named_hbm, named_ref),
            (table_hbm, table_ref),
            (length_hbm, length_ref),
            (x_hbm, x_ref),
            (gain_hbm, gain_ref),
            (k_hbm, k_ref),
            (v_hbm, v_ref),
        ],
        sems,
    )
    requests, width = x_ref.shape
    positions = k_ref.shape[0] // requests
    per_block = blocks[0].shape[0]
    rows = per_block * count
    named_copy.wait()
    table_copy.wait()
    length_copy.wait()
    owner, standing = owner_and_standing(named_ref[...], table_ref[...])
    block = block_of(owner - lax.axis_index("adapter"), lax.axis_index("tensor"), count)
    row = jnp.where(block < 0, -2, block * per_block + 2 * standing)
    order = iota((rows, requests), 0)
    put_x = ones_where(order == row)
    put_kv = ones_where(order == row + 1)
    put = jnp.concatenate([put_x, put_kv], axis=1)

    x_copy.wait()
    gain_copy.wait()
    floats = x_ref[...].astype(F32)
    scale = lax.rsqrt(jnp.mean(floats * floats, axis=1, keepdims=True) + EPSILON)
    flat_ref[0:requests, :] = (floats * scale * gain_ref[...]).astype(BF16)
    for n, (source, copy) in enumerate(((k_ref, k_copy), (v_ref, v_copy))):
        copy.wait()
        spread_ref[...] = source[...].astype(F32)
        for p in range(positions):
            to = slice((n * positions + p) * LANES, (n * positions + p + 1) * LANES)
            flat_ref[requests : 2 * requests, to] = spread_ref[
                pl.ds(p, requests, stride=positions), :
            ].astype(BF16)
    step = 512
    for c in range(0, width, step):
        placed = nn(put, flat_ref[:, c : c + step]).astype(BF16)
        for j, block in enumerate(blocks):
            block[:, c : c + step] = placed[j * per_block : (j + 1) * per_block]
    square = (requests, requests)
    length_column = jnp.sum(
        jnp.where(iota(square, 0) == iota(square, 1), length_ref[...], 0), axis=1, keepdims=True
    )
    lengths = jnp.broadcast_to(length_column.astype(F32), (requests, LANES)).astype(BF16)
    placed = nn(put_x, lengths).astype(BF16)
    for j, block in enumerate(blocks):
        block[:, width:] = placed[j * per_block : (j + 1) * per_block]


def stacked(blocks, columns):
    return jnp.concatenate([block[:, columns] for block in blocks], axis=0)


def stage_kernel(wq_hbm, wk_hbm, wv_hbm, down_hbm, up_hbm, kv_up_hbm, out_down_hbm, out_up_hbm, wq_ref, narrow_ref, small_ref, up_ref, kv_up_ref, out_down_ref, sems):
    width = wq_hbm.shape[0]
    hcols = wk_hbm.shape[0]
    ranks = down_hbm.shape[0]
    pieces = 4
    pairs = [
        (up_hbm, up_ref),
        (kv_up_hbm, kv_up_ref),
        (out_down_hbm, out_down_ref),
        (out_up_hbm, small_ref.at[:, 0 : out_up_hbm.shape[1]]),
    ]
    for n in range(pieces):
        rows = pl.ds(n * (width // pieces), width // pieces)
        pairs.append((wq_hbm.at[rows, :], wq_ref.at[rows, :]))
    for n in range(2):
        rows = pl.ds(n * (ranks // 2), ranks // 2)
        pairs.append((down_hbm.at[rows, :], narrow_ref.at[pl.ds(4 * hcols + n * (ranks // 2), ranks // 2), :]))
        columns = pl.ds(n * (width // 2), width // 2)
        for m, source in enumerate((wk_hbm, wv_hbm)):
            target = narrow_ref.at[pl.ds((2 * n + m) * hcols, hcols), :]
            pairs.append((source.at[:, columns], target))
    copies = copy_all(pairs, sems)
    for copy in copies[:3]:
        copy.wait()
    small_ref[:, out_up_hbm.shape[1] :] = jnp.concatenate(
        [up_ref[...], kv_up_ref[0], kv_up_ref[1], out_down_ref[...]], axis=1
    )
    for copy in copies[3:]:
        copy.wait()


def project_kernel(count, *refs):
    blocks = refs[: 2 * count]
    wq_ref, narrow_ref, mine_ref, theirs_ref, sums_ref = refs[2 * count :]
    width = wq_ref.shape[0]
    half = narrow_ref.shape[1]
    slots = mine_ref.shape[0]
    rows = sums_ref.shape[1]
    kvcols = LANES
    x_all = stacked(blocks, slice(0, width))
    narrow = nt(jnp.concatenate([x_all[:, :half], x_all[:, half:]], axis=0), narrow_ref[...])
    early, late = narrow[:rows], narrow[rows:]
    ranks = jnp.where(lax.axis_index("tensor") == 0, early[:, 2 * kvcols :], late[:, 2 * kvcols :])
    spare = jnp.zeros((rows, -ranks.shape[1] % LANES), F32)
    sums = [
        nn(x_all, wq_ref[...]),
        early[:, :kvcols] + late[:, kvcols : 2 * kvcols],
        jnp.concatenate([ranks, spare], axis=1),
    ]
    tile = 0
    for part in sums:
        for c in range(0, part.shape[1], LANES):
            sums_ref[tile] = part[:, c : c + LANES]
            columns = slice(tile * LANES, (tile + 1) * LANES)
            mine_ref[:, columns] = sums_ref[tile, pl.ds(0, slots, stride=2), :]
            theirs_ref[:, columns] = sums_ref[tile, pl.ds(rows // 2, slots, stride=2), :]
            tile += 1


def unpack_kernel(count, *refs):
    blocks = refs[:count]
    named_ref, table_ref, k_ref, v_ref, length_ref, cosine_ref, sine_ref, place_ref = refs[count:]
    requests, rows = place_ref.shape
    core = lax.axis_index("tensor")
    owner, standing = owner_and_standing(named_ref[...], table_ref[...])
    ahead = owner - lax.axis_index("adapter")
    near, far = block_of(ahead, core, count), block_of(ahead, 1 - core, count)
    back = rows // (2 * count)
    source = jnp.where(near < 0, count + far, near) * back + core * (back // 2) + standing
    square = (requests, requests)
    source = jnp.sum(
        jnp.where(iota(square, 0) == iota(square, 1), source, 0), axis=1, keepdims=True
    )
    place_ref[...] = ones_where(iota((requests, rows), 1) == source)
    slots = length_ref.shape[0]
    per_block = blocks[0].shape[0]
    positions = k_ref.shape[0] // slots
    width = 2 * positions * LANES
    together = GROUP // (per_block // 2)
    pick = iota((GROUP, 2 * GROUP), 1) - 2 * iota((GROUP, 2 * GROUP), 0)
    pick_x, pick_kv = ones_where(pick == 0), ones_where(pick == 1)
    step = 512
    for g in range(slots // GROUP):
        members = blocks[g * together : (g + 1) * together]
        for c in range(0, width, step):
            picked = nn(pick_kv, stacked(members, slice(c, c + step))).astype(BF16)
            for j in range(step // LANES):
                p = c // LANES + j
                target, p = (k_ref, p) if p < positions else (v_ref, p - positions)
                first = (g * positions + p) * GROUP
                target[first : first + GROUP, :] = picked[:, j * LANES : (j + 1) * LANES]
        length_ref[g * GROUP : (g + 1) * GROUP, :] = nn(
            pick_x, stacked(members, slice(width, width + LANES))
        )
    halfway = HEAD_SIZE // 2
    lane = iota((slots, LANES), 1)
    exponent = (lane % halfway).astype(F32) * (-math.log(THETA) / halfway)
    angle = length_ref[...] * jnp.exp(exponent)
    cosine_ref[...] = jnp.cos(angle)
    sine = jnp.sin(angle)
    sine_ref[...] = jnp.where(lane < halfway, -sine, sine)


def attend_kernel(mine_ref, theirs_ref, small_ref, small_other_ref, k_ref, v_ref, length_ref, cosine_ref, sine_ref, out_ref):
    core = lax.axis_index("tensor")
    slots = mine_ref.shape[0]
    rank = small_ref.shape[0]
    kvcols = LANES
    qcols = out_ref.shape[1] // 2
    heads = 2 * qcols // HEAD_SIZE
    halfway = HEAD_SIZE // 2
    both = qcols + kvcols
    base = small_ref.shape[1] - both - qcols
    mine = mine_ref[...]
    theirs = theirs_ref[...]
    ranks = (mine + theirs)[:, both : both + 3 * rank].astype(BF16)
    ranks = [ranks[:, n * rank : (n + 1) * rank] for n in range(3)]

    def added(projected, up_ref):
        change = jnp.concatenate(
            [
                nn(ranks[0], up_ref[:, base : base + qcols]),
                nn(ranks[1], up_ref[:, base + qcols : base + qcols + halfway]),
                nn(ranks[2], up_ref[:, base + qcols + halfway : base + both]),
            ],
            axis=1,
        )
        return projected[:, :both] + change.astype(BF16).astype(F32)

    mine = added(mine, small_ref)
    theirs = added(theirs, small_other_ref)
    combined = jnp.concatenate([mine[:, :qcols], theirs[:, :qcols]], axis=1)
    cosine, sine = cosine_ref[...], sine_ref[...]

    def rotate(part):
        return part * cosine + pltpu.roll(part, halfway, 1) * sine

    queries = [
        rotate(combined[:, h * HEAD_SIZE : (h + 1) * HEAD_SIZE]).astype(BF16) for h in range(heads)
    ]
    kv_mine = mine[:, qcols:]
    kv_theirs = theirs[:, qcols:]
    leading = jnp.where(core == 0, kv_mine, kv_theirs)
    trailing = jnp.where(core == 0, kv_theirs, kv_mine)
    first = iota((slots, LANES), 1) < halfway
    own_keys = rotate(jnp.where(first, leading, pltpu.roll(trailing, halfway, 1))).astype(BF16)
    own_values = jnp.where(first, pltpu.roll(leading, halfway, 1), trailing).astype(BF16)

    cached = k_ref.shape[0] * GROUP // slots
    rows = heads * GROUP
    shrink = math.sqrt(HEAD_SIZE)
    column = iota((rows, cached), 1)
    same = column % GROUP == iota((rows, cached), 0) % GROUP
    position = column // GROUP
    own = iota((rows, GROUP), 1) == iota((rows, GROUP), 0) % GROUP
    for g in range(slots // GROUP):
        members = slice(g * GROUP, (g + 1) * GROUP)
        held = slice(g * cached, (g + 1) * cached)
        query = jnp.concatenate([part[members] for part in queries], axis=0)
        length = jnp.concatenate([length_ref[members, 0:1]] * heads, axis=0).astype(jnp.int32)
        scores = jnp.where(
            same & (position < length), nt(query, k_ref[held, :]) / shrink, -jnp.inf
        )
        own_scores = jnp.where(own, nt(query, own_keys[members]) / shrink, -jnp.inf)
        highest = jnp.maximum(
            jnp.max(scores, axis=1, keepdims=True), jnp.max(own_scores, axis=1, keepdims=True)
        )
        raised = jnp.exp(scores - highest)
        own_raised = jnp.exp(own_scores - highest)
        total = jnp.sum(raised, axis=1, keepdims=True) + jnp.sum(own_raised, axis=1, keepdims=True)
        weights = (raised / total).astype(BF16)
        own_weights = (own_raised / total).astype(BF16)
        attended = (nn(weights, v_ref[held, :]) + nn(own_weights, own_values[members])).astype(BF16)
        for h in range(heads):
            out_ref[members, h * HEAD_SIZE : (h + 1) * HEAD_SIZE] = attended[
                h * GROUP : (h + 1) * GROUP
            ]


def output_kernel(count, attended_ref, wo_ref, wo_other_ref, small_ref, small_other_ref, *blocks):
    core = lax.axis_index("tensor")
    slots, cols = attended_ref.shape
    hcols = cols // 2
    per_block, half = blocks[0].shape
    kept = per_block // 2
    rows = count * per_block
    slot = iota((rows, slots), 0)
    slot = slot // per_block * kept + slot % kept
    attended = nn(ones_where(iota((rows, slots), 1) == slot), attended_ref[...]).astype(BF16)
    left, right = attended[:, :hcols], attended[:, hcols:]
    down = slice(small_ref.shape[1] - hcols, small_ref.shape[1])
    ranks = (nt(left, small_ref[:, down]) + nt(right, small_other_ref[:, down])).astype(BF16)
    step = 512
    side = iota((rows, step), 0) % per_block // kept
    for c in range(0, half, step):
        near, far = slice(c, c + step), slice(half + c, half + c + step)
        terms = jnp.where(
            side == 0,
            nn(left, wo_ref[:, near]) + nn(right, wo_other_ref[:, near]),
            nn(left, wo_ref[:, far]) + nn(right, wo_other_ref[:, far]),
        )
        delta = jnp.where(side == core, nn(ranks, small_ref[:, near]), nn(ranks, small_other_ref[:, near]))
        done = (terms + delta.astype(BF16).astype(F32)).astype(BF16)
        for j, block in enumerate(blocks):
            block[:, near] = done[j * per_block : (j + 1) * per_block]


def pick_kernel(place_ref, *refs):
    blocks, out_ref = refs[:-1], refs[-1]
    step = 512
    for c in range(0, out_ref.shape[1], step):
        out_ref[:, c : c + step] = nn(place_ref[...], stacked(blocks, slice(c, c + step))).astype(BF16)


OUTSIDE = pl.BlockSpec(memory_space=pltpu.HBM)
INSIDE = pl.BlockSpec(memory_space=pltpu.VMEM)


def call(kernel, outs, scratch=(), vmem=8, outside=(), out_spec=INSIDE, moved=0):
    many = isinstance(outs, (list, tuple))
    return lambda *args: pl.pallas_call(
        kernel,
        out_shape=outs,
        in_specs=[OUTSIDE if i in outside else INSIDE for i in range(len(args))],
        out_specs=[out_spec] * len(outs) if many else out_spec,
        scratch_shapes=list(scratch),
        compiler_params=pltpu.CompilerParams(vmem_limit_bytes=vmem * MIB),
        cost_estimate=pl.CostEstimate(flops=0, bytes_accessed=moved, transcendentals=0),
    )(
        *[
            pltpu.with_memory_space_constraint(arg, pltpu.HBM) if i in outside else arg
            for i, arg in enumerate(args)
        ]
    )


def body(
    layer_input,
    input_norm_gain,
    query_projection,
    key_projection,
    value_projection,
    output_projection,
    cached_key_rows,
    cached_value_rows,
    request_adapter,
    adapter_row_table,
    cached_length,
    projection_adapter_down,
    query_adapter_up,
    key_value_adapter_up,
    output_adapter_down,
    output_adapter_up,
):
    shape = jax.ShapeDtypeStruct
    requests, width = layer_input.shape
    owners = lax.axis_size("adapter")
    adapters = adapter_row_table.shape[0]
    positions = cached_key_rows.shape[1]
    half = width // 2
    capacity = max(2, 2 * ((requests + adapters - 1) // adapters))
    count = owners // 2
    kept = (capacity + 3) // 4 * 4
    slots = count * kept
    block = shape((2 * kept, width + LANES), BF16)
    named = request_adapter.reshape(1, requests)
    table = adapter_row_table.reshape(1, adapters)

    rank, qcols = query_adapter_up.shape[1:]
    hcols = key_value_adapter_up.shape[3]
    hrows = output_projection.shape[0]
    packed = call(
        functools.partial(pack_kernel, capacity),
        [block] * count,
        [
            pltpu.VMEM((requests, width), BF16),
            pltpu.VMEM((1, width), F32),
            pltpu.VMEM((positions * requests, LANES), BF16),
            pltpu.VMEM((positions * requests, LANES), BF16),
            pltpu.VMEM((1, requests), jnp.int32),
            pltpu.VMEM((1, adapters), jnp.int32),
            pltpu.VMEM((1, requests), jnp.int32),
            pltpu.VMEM((2 * requests, width), BF16),
            pltpu.VMEM((positions * requests, LANES), F32),
            pltpu.SemaphoreType.DMA((7,)),
        ],
        outside=range(7),
    )(
        layer_input,
        input_norm_gain.reshape(1, width),
        cached_key_rows.reshape(requests * positions, HEAD_SIZE),
        cached_value_rows.reshape(requests * positions, HEAD_SIZE),
        named,
        table,
        cached_length.reshape(1, requests),
    )
    down = projection_adapter_down[0].T
    wk, wv = key_projection.T, value_projection.T
    kvcols = 2 * wk.shape[0]
    *packed, query_projection, wk, wv, down, output_projection = lax.optimization_barrier(
        (*packed, query_projection, wk, wv, down, output_projection)
    )
    *weights, small = call(
        stage_kernel,
        [
            shape(query_projection.shape, BF16),
            shape((2 * kvcols + down.shape[0], half), BF16),
            shape((rank, half + qcols + 2 * hcols + hrows), BF16),
        ],
        [
            pltpu.VMEM((rank, qcols), BF16),
            pltpu.VMEM((2, rank, hcols), BF16),
            pltpu.VMEM((rank, hrows), BF16),
            pltpu.SemaphoreType.DMA((14,)),
        ],
        outside=range(8),
        moved=2 * (query_projection.size + kvcols * width + down.size),
    )(
        query_projection,
        wk,
        wv,
        down,
        query_adapter_up[0],
        key_value_adapter_up[0],
        output_adapter_down[0].T,
        output_adapter_up[0],
    )

    def onward(n):
        shifts = (count - 1 - n, count + n)
        return [
            (a * 2 + t, (a + shifts[t]) % owners * 2 + t) for a in range(owners) for t in range(2)
        ]

    arrived = [
        lax.ppermute(one, ("adapter", "tensor"), onward(n)) for n, one in enumerate(packed)
    ]
    arrived[0], *weights = lax.optimization_barrier((arrived[0], *weights))
    passed = [lax.ppermute(one, "tensor", SWAP) for one in arrived]
    wo_other = lax.ppermute(output_projection, "tensor", SWAP)
    pcols = qcols + kvcols + (down.shape[0] + LANES - 1) // LANES * LANES
    mine, theirs = call(
        functools.partial(project_kernel, count),
        [shape((slots, pcols), F32), shape((slots, pcols), F32)],
        [pltpu.VMEM((pcols // LANES, 4 * slots, LANES), F32)],
        vmem=24,
    )(*arrived, *passed, *weights)
    theirs, mine, small = lax.optimization_barrier((theirs, mine, small))
    theirs = lax.ppermute(theirs, "tensor", SWAP)
    small_other = lax.ppermute(small, "tensor", SWAP)
    keys, values, lengths, cosine, sine, place = call(
        functools.partial(unpack_kernel, count),
        [shape((slots * positions, HEAD_SIZE), BF16)] * 2
        + [shape((slots, LANES), F32)] * 3
        + [shape((requests, 4 * slots), BF16)],
    )(*arrived, named, table)
    attended = call(attend_kernel, shape((slots, 2 * qcols), BF16), vmem=16)(
        mine, theirs, small, small_other, keys, values, lengths, cosine, sine
    )
    finished = call(
        functools.partial(output_kernel, count),
        [shape((2 * kept, half), BF16)] * count,
        vmem=16,
    )(attended, output_projection, wo_other, small, small_other)
    returned = [
        lax.ppermute(one, ("adapter", "tensor"), [(b, a) for a, b in onward(n)])
        for n, one in enumerate(finished)
    ]
    waited = list(returned)
    for n in reversed(range(count - 1)):
        waited[n] = lax.optimization_barrier((returned[n], returned[n + 1]))[0]
    returned += [lax.ppermute(one, "tensor", SWAP) for one in waited]
    return call(pick_kernel, shape((requests, half), BF16))(place, *returned)


def solution(mesh):
    placed = (
        P(("groups", "adapter"), None),
        P(),
        P(None, "tensor"),
        P(None, "tensor"),
        P(None, "tensor"),
        P("tensor", None),
        P(("groups", "adapter"), None, None),
        P(("groups", "adapter"), None, None),
        P(("groups", "adapter"), None),
        P(),
        P(("groups", "adapter")),
        P("adapter", "tensor", None),
        P("adapter", None, "tensor"),
        P("adapter", None, None, "tensor"),
        P("adapter", "tensor", None),
        P("adapter", None, "tensor"),
    )
    return jax.shard_map(
        body,
        mesh=mesh,
        in_specs=placed,
        out_specs=P(("groups", "adapter"), "tensor"),
        check_vma=False,
    )
```

```python
import functools
import math

import jax
import jax.numpy as jnp
from jax import lax
from jax.experimental import pallas as pl
from jax.experimental.pallas import tpu as pltpu
from jax.sharding import PartitionSpec as P

HEAD_SIZE = 128
LANES = 128
EPSILON = 1e-05
THETA = 500000.0
BF16 = jnp.bfloat16
F32 = jnp.float32
SWAP = [(0, 1), (1, 0)]
GROUP = 16
MIB = 1024 * 1024


def nn(a, b):
    return lax.dot_general(a, b, (((1,), (0,)), ((), ())), preferred_element_type=F32)


def nt(a, b):
    return lax.dot_general(a, b, (((1,), (1,)), ((), ())), preferred_element_type=F32)


def iota(shape, dim):
    return lax.broadcasted_iota(jnp.int32, shape, dim)


def ones_where(condition):
    return jnp.where(condition, 1.0, 0.0).astype(BF16)


def owner_and_standing(named, table):
    requests, adapters = named.shape[1], table.shape[1]
    table_column = jnp.sum(
        jnp.where(iota((adapters, adapters), 0) == iota((adapters, adapters), 1), table, 0),
        axis=1,
        keepdims=True,
    )
    owner = jnp.sum(
        jnp.where(iota((adapters, requests), 0) == named, table_column, 0), axis=0, keepdims=True
    )
    square = (requests, requests)
    owner_column = jnp.sum(
        jnp.where(iota(square, 0) == iota(square, 1), owner, 0), axis=1, keepdims=True
    )
    earlier = (owner_column == owner) & (iota(square, 0) < iota(square, 1))
    standing = jnp.sum(jnp.where(earlier, 1, 0), axis=0, keepdims=True)
    return owner, standing


def copy_all(pairs, sems):
    copies = [pltpu.make_async_copy(a, b, sems.at[i]) for i, (a, b) in enumerate(pairs)]
    for copy in copies:
        copy.start()
    return copies


TURNS = ((1, 0, 2, 3), (0, 1, 2, 3))


def turn_of(distance, turns):
    turn = distance
    for n, one in enumerate(turns):
        turn = jnp.where(distance == one, n, turn)
    return turn


def block_of(ahead, core, count):
    ahead = jnp.where(ahead < 0, ahead + 2 * count, ahead)
    return jnp.where(ahead // count == core,
        jnp.where(
            core == 0,
            turn_of(count - 1 - ahead, TURNS[0]),
            turn_of(ahead - count, TURNS[1]),
        ), -1)


def pack_kernel(capacity, x_hbm, gain_hbm, k_hbm, v_hbm, named_hbm, table_hbm, length_hbm, *rest):
    x_ref, gain_ref, k_ref, v_ref, named_ref, table_ref, length_ref, flat_ref, spread_ref, sems = rest[-10:]
    blocks = rest[:-10]
    count = len(blocks)
    owners = 2 * count
    named_copy, table_copy, length_copy, x_copy, gain_copy, k_copy, v_copy = copy_all(
        [
            (named_hbm, named_ref),
            (table_hbm, table_ref),
            (length_hbm, length_ref),
            (x_hbm, x_ref),
            (gain_hbm, gain_ref),
            (k_hbm, k_ref),
            (v_hbm, v_ref),
        ],
        sems,
    )
    requests, width = x_ref.shape
    positions = k_ref.shape[0] // requests
    per_block = blocks[0].shape[0]
    rows = per_block * count
    named_copy.wait()
    table_copy.wait()
    length_copy.wait()
    owner, standing = owner_and_standing(named_ref[...], table_ref[...])
    block = block_of(owner - lax.axis_index("adapter"), lax.axis_index("tensor"), count)
    row = jnp.where(block < 0, -2, block * per_block + 2 * standing)
    order = iota((rows, requests), 0)
    put_x = ones_where(order == row)
    put_kv = ones_where(order == row + 1)
    put = jnp.concatenate([put_x, put_kv], axis=1)

    x_copy.wait()
    gain_copy.wait()
    floats = x_ref[...].astype(F32)
    scale = lax.rsqrt(jnp.mean(floats * floats, axis=1, keepdims=True) + EPSILON)
    flat_ref[0:requests, :] = (floats * scale * gain_ref[...]).astype(BF16)
    for n, (source, copy) in enumerate(((k_ref, k_copy), (v_ref, v_copy))):
        copy.wait()
        spread_ref[...] = source[...].astype(F32)
        for p in range(positions):
            to = slice((n * positions + p) * LANES, (n * positions + p + 1) * LANES)
            flat_ref[requests : 2 * requests, to] = spread_ref[
                pl.ds(p, requests, stride=positions), :
            ].astype(BF16)
    step = 512
    for c in range(0, width, step):
        placed = nn(put, flat_ref[:, c : c + step]).astype(BF16)
        for j, block in enumerate(blocks):
            block[:, c : c + step] = placed[j * per_block : (j + 1) * per_block]
    square = (requests, requests)
    length_column = jnp.sum(
        jnp.where(iota(square, 0) == iota(square, 1), length_ref[...], 0), axis=1, keepdims=True
    )
    lengths = jnp.broadcast_to(length_column.astype(F32), (requests, LANES)).astype(BF16)
    placed = nn(put_x, lengths).astype(BF16)
    for j, block in enumerate(blocks):
        block[:, width:] = placed[j * per_block : (j + 1) * per_block]


def stacked(blocks, columns):
    return jnp.concatenate([block[:, columns] for block in blocks], axis=0)


def stage_kernel(wq_hbm, wk_hbm, wv_hbm, down_hbm, up_hbm, kv_up_hbm, out_down_hbm, out_up_hbm, wq_ref, narrow_ref, small_ref, up_ref, kv_up_ref, out_down_ref, sems):
    width = wq_hbm.shape[0]
    hcols = wk_hbm.shape[0]
    ranks = down_hbm.shape[0]
    pieces = 4
    pairs = [
        (up_hbm, up_ref),
        (kv_up_hbm, kv_up_ref),
        (out_down_hbm, out_down_ref),
        (out_up_hbm, small_ref.at[:, 0 : out_up_hbm.shape[1]]),
    ]
    for n in range(pieces):
        rows = pl.ds(n * (width // pieces), width // pieces)
        pairs.append((wq_hbm.at[rows, :], wq_ref.at[rows, :]))
    for n in range(2):
        rows = pl.ds(n * (ranks // 2), ranks // 2)
        pairs.append((down_hbm.at[rows, :], narrow_ref.at[pl.ds(4 * hcols + n * (ranks // 2), ranks // 2), :]))
        columns = pl.ds(n * (width // 2), width // 2)
        for m, source in enumerate((wk_hbm, wv_hbm)):
            target = narrow_ref.at[pl.ds((2 * n + m) * hcols, hcols), :]
            pairs.append((source.at[:, columns], target))
    copies = copy_all(pairs, sems)
    for copy in copies[:3]:
        copy.wait()
    small_ref[:, out_up_hbm.shape[1] :] = jnp.concatenate(
        [up_ref[...], kv_up_ref[0], kv_up_ref[1], out_down_ref[...]], axis=1
    )
    for copy in copies[3:]:
        copy.wait()


def project_kernel(count, *refs):
    blocks = refs[: 2 * count]
    wq_ref, narrow_ref, mine_ref, theirs_ref, sums_ref = refs[2 * count :]
    width = wq_ref.shape[0]
    half = narrow_ref.shape[1]
    slots = mine_ref.shape[0]
    rows = sums_ref.shape[1]
    kvcols = LANES
    x_all = stacked(blocks, slice(0, width))
    narrow = nt(jnp.concatenate([x_all[:, :half], x_all[:, half:]], axis=0), narrow_ref[...])
    early, late = narrow[:rows], narrow[rows:]
    ranks = jnp.where(lax.axis_index("tensor") == 0, early[:, 2 * kvcols :], late[:, 2 * kvcols :])
    spare = jnp.zeros((rows, -ranks.shape[1] % LANES), F32)
    sums = [
        nn(x_all, wq_ref[...]),
        early[:, :kvcols] + late[:, kvcols : 2 * kvcols],
        jnp.concatenate([ranks, spare], axis=1),
    ]
    tile = 0
    for part in sums:
        for c in range(0, part.shape[1], LANES):
            sums_ref[tile] = part[:, c : c + LANES]
            columns = slice(tile * LANES, (tile + 1) * LANES)
            mine_ref[:, columns] = sums_ref[tile, pl.ds(0, slots, stride=2), :]
            theirs_ref[:, columns] = sums_ref[tile, pl.ds(rows // 2, slots, stride=2), :]
            tile += 1


def unpack_kernel(count, *refs):
    blocks = refs[:count]
    named_ref, table_ref, k_ref, v_ref, length_ref, cosine_ref, sine_ref, place_ref = refs[count:]
    requests, rows = place_ref.shape
    core = lax.axis_index("tensor")
    owner, standing = owner_and_standing(named_ref[...], table_ref[...])
    ahead = owner - lax.axis_index("adapter")
    near, far = block_of(ahead, core, count), block_of(ahead, 1 - core, count)
    back = rows // (2 * count)
    source = jnp.where(near < 0, count + far, near) * back + core * (back // 2) + standing
    square = (requests, requests)
    source = jnp.sum(
        jnp.where(iota(square, 0) == iota(square, 1), source, 0), axis=1, keepdims=True
    )
    place_ref[...] = ones_where(iota((requests, rows), 1) == source)
    slots = length_ref.shape[0]
    per_block = blocks[0].shape[0]
    positions = k_ref.shape[0] // slots
    width = 2 * positions * LANES
    together = GROUP // (per_block // 2)
    pick = iota((GROUP, 2 * GROUP), 1) - 2 * iota((GROUP, 2 * GROUP), 0)
    pick_x, pick_kv = ones_where(pick == 0), ones_where(pick == 1)
    step = 512
    for g in range(slots // GROUP):
        members = blocks[g * together : (g + 1) * together]
        for c in range(0, width, step):
            picked = nn(pick_kv, stacked(members, slice(c, c + step))).astype(BF16)
            for j in range(step // LANES):
                p = c // LANES + j
                target, p = (k_ref, p) if p < positions else (v_ref, p - positions)
                first = (g * positions + p) * GROUP
                target[first : first + GROUP, :] = picked[:, j * LANES : (j + 1) * LANES]
        length_ref[g * GROUP : (g + 1) * GROUP, :] = nn(
            pick_x, stacked(members, slice(width, width + LANES))
        )
    halfway = HEAD_SIZE // 2
    lane = iota((slots, LANES), 1)
    exponent = (lane % halfway).astype(F32) * (-math.log(THETA) / halfway)
    angle = length_ref[...] * jnp.exp(exponent)
    cosine_ref[...] = jnp.cos(angle)
    sine = jnp.sin(angle)
    sine_ref[...] = jnp.where(lane < halfway, -sine, sine)


def attend_kernel(mine_ref, theirs_ref, small_ref, small_other_ref, k_ref, v_ref, length_ref, cosine_ref, sine_ref, out_ref):
    core = lax.axis_index("tensor")
    slots = mine_ref.shape[0]
    rank = small_ref.shape[0]
    kvcols = LANES
    qcols = out_ref.shape[1] // 2
    heads = 2 * qcols // HEAD_SIZE
    halfway = HEAD_SIZE // 2
    both = qcols + kvcols
    base = small_ref.shape[1] - both - qcols
    mine = mine_ref[...]
    theirs = theirs_ref[...]
    ranks = (mine + theirs)[:, both : both + 3 * rank].astype(BF16)
    ranks = [ranks[:, n * rank : (n + 1) * rank] for n in range(3)]

    def added(projected, up_ref):
        change = jnp.concatenate(
            [
                nn(ranks[0], up_ref[:, base : base + qcols]),
                nn(ranks[1], up_ref[:, base + qcols : base + qcols + halfway]),
                nn(ranks[2], up_ref[:, base + qcols + halfway : base + both]),
            ],
            axis=1,
        )
        return projected[:, :both] + change.astype(BF16).astype(F32)

    mine = added(mine, small_ref)
    theirs = added(theirs, small_other_ref)
    combined = jnp.concatenate([mine[:, :qcols], theirs[:, :qcols]], axis=1)
    cosine, sine = cosine_ref[...], sine_ref[...]

    def rotate(part):
        return part * cosine + pltpu.roll(part, halfway, 1) * sine

    queries = [
        rotate(combined[:, h * HEAD_SIZE : (h + 1) * HEAD_SIZE]).astype(BF16) for h in range(heads)
    ]
    kv_mine = mine[:, qcols:]
    kv_theirs = theirs[:, qcols:]
    leading = jnp.where(core == 0, kv_mine, kv_theirs)
    trailing = jnp.where(core == 0, kv_theirs, kv_mine)
    first = iota((slots, LANES), 1) < halfway
    own_keys = rotate(jnp.where(first, leading, pltpu.roll(trailing, halfway, 1))).astype(BF16)
    own_values = jnp.where(first, pltpu.roll(leading, halfway, 1), trailing).astype(BF16)

    cached = k_ref.shape[0] * GROUP // slots
    rows = heads * GROUP
    shrink = math.sqrt(HEAD_SIZE)
    column = iota((rows, cached), 1)
    same = column % GROUP == iota((rows, cached), 0) % GROUP
    position = column // GROUP
    own = iota((rows, GROUP), 1) == iota((rows, GROUP), 0) % GROUP
    for g in range(slots // GROUP):
        members = slice(g * GROUP, (g + 1) * GROUP)
        held = slice(g * cached, (g + 1) * cached)
        query = jnp.concatenate([part[members] for part in queries], axis=0)
        length = jnp.concatenate([length_ref[members, 0:1]] * heads, axis=0).astype(jnp.int32)
        scores = jnp.where(
            same & (position < length), nt(query, k_ref[held, :]) / shrink, -jnp.inf
        )
        own_scores = jnp.where(own, nt(query, own_keys[members]) / shrink, -jnp.inf)
        highest = jnp.maximum(
            jnp.max(scores, axis=1, keepdims=True), jnp.max(own_scores, axis=1, keepdims=True)
        )
        raised = jnp.exp(scores - highest)
        own_raised = jnp.exp(own_scores - highest)
        total = jnp.sum(raised, axis=1, keepdims=True) + jnp.sum(own_raised, axis=1, keepdims=True)
        weights = (raised / total).astype(BF16)
        own_weights = (own_raised / total).astype(BF16)
        attended = (nn(weights, v_ref[held, :]) + nn(own_weights, own_values[members])).astype(BF16)
        for h in range(heads):
            out_ref[members, h * HEAD_SIZE : (h + 1) * HEAD_SIZE] = attended[
                h * GROUP : (h + 1) * GROUP
            ]


def output_kernel(count, attended_ref, wo_ref, wo_other_ref, small_ref, small_other_ref, *blocks):
    core = lax.axis_index("tensor")
    slots, cols = attended_ref.shape
    hcols = cols // 2
    per_block, half = blocks[0].shape
    kept = per_block // 2
    rows = count * per_block
    slot = iota((rows, slots), 0)
    slot = slot // per_block * kept + slot % kept
    attended = nn(ones_where(iota((rows, slots), 1) == slot), attended_ref[...]).astype(BF16)
    left, right = attended[:, :hcols], attended[:, hcols:]
    down = slice(small_ref.shape[1] - hcols, small_ref.shape[1])
    ranks = (nt(left, small_ref[:, down]) + nt(right, small_other_ref[:, down])).astype(BF16)
    step = 512
    side = iota((rows, step), 0) % per_block // kept
    for c in range(0, half, step):
        near, far = slice(c, c + step), slice(half + c, half + c + step)
        terms = jnp.where(
            side == 0,
            nn(left, wo_ref[:, near]) + nn(right, wo_other_ref[:, near]),
            nn(left, wo_ref[:, far]) + nn(right, wo_other_ref[:, far]),
        )
        delta = jnp.where(side == core, nn(ranks, small_ref[:, near]), nn(ranks, small_other_ref[:, near]))
        done = (terms + delta.astype(BF16).astype(F32)).astype(BF16)
        for j, block in enumerate(blocks):
            block[:, near] = done[j * per_block : (j + 1) * per_block]


def pick_kernel(place_ref, *refs):
    blocks, out_ref = refs[:-1], refs[-1]
    step = 512
    for c in range(0, out_ref.shape[1], step):
        out_ref[:, c : c + step] = nn(place_ref[...], stacked(blocks, slice(c, c + step))).astype(BF16)


OUTSIDE = pl.BlockSpec(memory_space=pltpu.HBM)
INSIDE = pl.BlockSpec(memory_space=pltpu.VMEM)


def call(kernel, outs, scratch=(), vmem=8, outside=(), out_spec=INSIDE, moved=0):
    many = isinstance(outs, (list, tuple))
    return lambda *args: pl.pallas_call(
        kernel,
        out_shape=outs,
        in_specs=[OUTSIDE if i in outside else INSIDE for i in range(len(args))],
        out_specs=[out_spec] * len(outs) if many else out_spec,
        scratch_shapes=list(scratch),
        compiler_params=pltpu.CompilerParams(vmem_limit_bytes=vmem * MIB),
        cost_estimate=pl.CostEstimate(flops=0, bytes_accessed=moved, transcendentals=0),
    )(
        *[
            pltpu.with_memory_space_constraint(arg, pltpu.HBM) if i in outside else arg
            for i, arg in enumerate(args)
        ]
    )


def body(
    layer_input,
    input_norm_gain,
    query_projection,
    key_projection,
    value_projection,
    output_projection,
    cached_key_rows,
    cached_value_rows,
    request_adapter,
    adapter_row_table,
    cached_length,
    projection_adapter_down,
    query_adapter_up,
    key_value_adapter_up,
    output_adapter_down,
    output_adapter_up,
):
    shape = jax.ShapeDtypeStruct
    requests, width = layer_input.shape
    owners = lax.axis_size("adapter")
    adapters = adapter_row_table.shape[0]
    positions = cached_key_rows.shape[1]
    half = width // 2
    capacity = max(2, 2 * ((requests + adapters - 1) // adapters))
    count = owners // 2
    kept = (capacity + 3) // 4 * 4
    slots = count * kept
    block = shape((2 * kept, width + LANES), BF16)
    named = request_adapter.reshape(1, requests)
    table = adapter_row_table.reshape(1, adapters)

    rank, qcols = query_adapter_up.shape[1:]
    hcols = key_value_adapter_up.shape[3]
    hrows = output_projection.shape[0]
    packed = call(
        functools.partial(pack_kernel, capacity),
        [block] * count,
        [
            pltpu.VMEM((requests, width), BF16),
            pltpu.VMEM((1, width), F32),
            pltpu.VMEM((positions * requests, LANES), BF16),
            pltpu.VMEM((positions * requests, LANES), BF16),
            pltpu.VMEM((1, requests), jnp.int32),
            pltpu.VMEM((1, adapters), jnp.int32),
            pltpu.VMEM((1, requests), jnp.int32),
            pltpu.VMEM((2 * requests, width), BF16),
            pltpu.VMEM((positions * requests, LANES), F32),
            pltpu.SemaphoreType.DMA((7,)),
        ],
        outside=range(7),
    )(
        layer_input,
        input_norm_gain.reshape(1, width),
        cached_key_rows.reshape(requests * positions, HEAD_SIZE),
        cached_value_rows.reshape(requests * positions, HEAD_SIZE),
        named,
        table,
        cached_length.reshape(1, requests),
    )
    down = projection_adapter_down[0].T
    wk, wv = key_projection.T, value_projection.T
    kvcols = 2 * wk.shape[0]
    *packed, query_projection, wk, wv, down, output_projection = lax.optimization_barrier(
        (*packed, query_projection, wk, wv, down, output_projection)
    )
    *weights, small = call(
        stage_kernel,
        [
            shape(query_projection.shape, BF16),
            shape((2 * kvcols + down.shape[0], half), BF16),
            shape((rank, half + qcols + 2 * hcols + hrows), BF16),
        ],
        [
            pltpu.VMEM((rank, qcols), BF16),
            pltpu.VMEM((2, rank, hcols), BF16),
            pltpu.VMEM((rank, hrows), BF16),
            pltpu.SemaphoreType.DMA((14,)),
        ],
        outside=range(8),
        moved=2 * (query_projection.size + kvcols * width + down.size),
    )(
        query_projection,
        wk,
        wv,
        down,
        query_adapter_up[0],
        key_value_adapter_up[0],
        output_adapter_down[0].T,
        output_adapter_up[0],
    )

    def onward(n):
        near, far = [turns[n] if n < len(turns) else n for turns in TURNS]
        shifts = (count - 1 - near, count + far)
        return [
            (a * 2 + t, (a + shifts[t]) % owners * 2 + t) for a in range(owners) for t in range(2)
        ]

    arrived = [
        lax.ppermute(one, ("adapter", "tensor"), onward(n)) for n, one in enumerate(packed)
    ]
    arrived[0], *weights = lax.optimization_barrier((arrived[0], *weights))
    passed = [lax.ppermute(one, "tensor", SWAP) for one in arrived]
    wo_other = lax.ppermute(output_projection, "tensor", SWAP)
    pcols = qcols + kvcols + (down.shape[0] + LANES - 1) // LANES * LANES
    mine, theirs = call(
        functools.partial(project_kernel, count),
        [shape((slots, pcols), F32), shape((slots, pcols), F32)],
        [pltpu.VMEM((pcols // LANES, 4 * slots, LANES), F32)],
        vmem=24,
    )(*arrived, *passed, *weights)
    theirs, mine, small = lax.optimization_barrier((theirs, mine, small))
    theirs = lax.ppermute(theirs, "tensor", SWAP)
    small_other = lax.ppermute(small, "tensor", SWAP)
    keys, values, lengths, cosine, sine, place = call(
        functools.partial(unpack_kernel, count),
        [shape((slots * positions, HEAD_SIZE), BF16)] * 2
        + [shape((slots, LANES), F32)] * 3
        + [shape((requests, 4 * slots), BF16)],
    )(*arrived, named, table)
    attended = call(attend_kernel, shape((slots, 2 * qcols), BF16), vmem=16)(
        mine, theirs, small, small_other, keys, values, lengths, cosine, sine
    )
    finished = call(
        functools.partial(output_kernel, count),
        [shape((2 * kept, half), BF16)] * count,
        vmem=16,
    )(attended, output_projection, wo_other, small, small_other)
    returned = [
        lax.ppermute(one, ("adapter", "tensor"), [(b, a) for a, b in onward(n)])
        for n, one in enumerate(finished)
    ]
    waited = list(returned)
    for n in reversed(range(count - 1)):
        waited[n] = lax.optimization_barrier((returned[n], returned[n + 1]))[0]
    returned += [lax.ppermute(one, "tensor", SWAP) for one in waited]
    return call(pick_kernel, shape((requests, half), BF16))(place, *returned)


def solution(mesh):
    placed = (
        P(("groups", "adapter"), None),
        P(),
        P(None, "tensor"),
        P(None, "tensor"),
        P(None, "tensor"),
        P("tensor", None),
        P(("groups", "adapter"), None, None),
        P(("groups", "adapter"), None, None),
        P(("groups", "adapter"), None),
        P(),
        P(("groups", "adapter")),
        P("adapter", "tensor", None),
        P("adapter", None, "tensor"),
        P("adapter", None, None, "tensor"),
        P("adapter", "tensor", None),
        P("adapter", None, "tensor"),
    )
    return jax.shard_map(
        body,
        mesh=mesh,
        in_specs=placed,
        out_specs=P(("groups", "adapter"), "tensor"),
        check_vma=False,
    )
```

```python
import functools
import math

import jax
import jax.numpy as jnp
from jax import lax
from jax.experimental import pallas as pl
from jax.experimental.pallas import tpu as pltpu
from jax.sharding import PartitionSpec as P

HEAD_SIZE = 128
LANES = 128
EPSILON = 1e-05
THETA = 500000.0
BF16 = jnp.bfloat16
F32 = jnp.float32
SWAP = [(0, 1), (1, 0)]
GROUP = 16
MIB = 1024 * 1024


def nn(a, b):
    return lax.dot_general(a, b, (((1,), (0,)), ((), ())), preferred_element_type=F32)


def nt(a, b):
    return lax.dot_general(a, b, (((1,), (1,)), ((), ())), preferred_element_type=F32)


def iota(shape, dim):
    return lax.broadcasted_iota(jnp.int32, shape, dim)


def ones_where(condition):
    return jnp.where(condition, 1.0, 0.0).astype(BF16)


def owner_and_standing(named, table):
    requests, adapters = named.shape[1], table.shape[1]
    table_column = jnp.sum(
        jnp.where(iota((adapters, adapters), 0) == iota((adapters, adapters), 1), table, 0),
        axis=1,
        keepdims=True,
    )
    owner = jnp.sum(
        jnp.where(iota((adapters, requests), 0) == named, table_column, 0), axis=0, keepdims=True
    )
    square = (requests, requests)
    owner_column = jnp.sum(
        jnp.where(iota(square, 0) == iota(square, 1), owner, 0), axis=1, keepdims=True
    )
    earlier = (owner_column == owner) & (iota(square, 0) < iota(square, 1))
    standing = jnp.sum(jnp.where(earlier, 1, 0), axis=0, keepdims=True)
    return owner, standing


def copy_all(pairs, sems):
    copies = [pltpu.make_async_copy(a, b, sems.at[i]) for i, (a, b) in enumerate(pairs)]
    for copy in copies:
        copy.start()
    return copies


TURNS = ((1, 0, 2, 3), (0, 1, 2, 3))


def turn_of(distance, turns):
    turn = distance
    for n, one in enumerate(turns):
        turn = jnp.where(distance == one, n, turn)
    return turn


def block_of(ahead, core, count):
    ahead = jnp.where(ahead < 0, ahead + 2 * count, ahead)
    return jnp.where(ahead // count == core,
        jnp.where(
            core == 0,
            turn_of(count - 1 - ahead, TURNS[0]),
            turn_of(ahead - count, TURNS[1]),
        ), -1)


def pack_kernel(capacity, x_hbm, gain_hbm, k_hbm, v_hbm, named_hbm, table_hbm, length_hbm, *rest):
    x_ref, gain_ref, k_ref, v_ref, named_ref, table_ref, length_ref, flat_ref, spread_ref, sems = rest[-10:]
    blocks = rest[:-10]
    count = len(blocks)
    owners = 2 * count
    named_copy, table_copy, length_copy, x_copy, gain_copy, k_copy, v_copy = copy_all(
        [
            (named_hbm, named_ref),
            (table_hbm, table_ref),
            (length_hbm, length_ref),
            (x_hbm, x_ref),
            (gain_hbm, gain_ref),
            (k_hbm, k_ref),
            (v_hbm, v_ref),
        ],
        sems,
    )
    requests, width = x_ref.shape
    positions = k_ref.shape[0] // requests
    per_block = blocks[0].shape[0]
    rows = per_block * count
    named_copy.wait()
    table_copy.wait()
    length_copy.wait()
    owner, standing = owner_and_standing(named_ref[...], table_ref[...])
    block = block_of(owner - lax.axis_index("adapter"), lax.axis_index("tensor"), count)
    row = jnp.where(block < 0, -2, block * per_block + 2 * standing)
    order = iota((rows, requests), 0)
    put_x = ones_where(order == row)
    put_kv = ones_where(order == row + 1)
    put = jnp.concatenate([put_x, put_kv], axis=1)

    x_copy.wait()
    gain_copy.wait()
    floats = x_ref[...].astype(F32)
    scale = lax.rsqrt(jnp.mean(floats * floats, axis=1, keepdims=True) + EPSILON)
    flat_ref[0:requests, :] = (floats * scale * gain_ref[...]).astype(BF16)
    for n, (source, copy) in enumerate(((k_ref, k_copy), (v_ref, v_copy))):
        copy.wait()
        spread_ref[...] = source[...].astype(F32)
        for p in range(positions):
            to = slice((n * positions + p) * LANES, (n * positions + p + 1) * LANES)
            flat_ref[requests : 2 * requests, to] = spread_ref[
                pl.ds(p, requests, stride=positions), :
            ].astype(BF16)
    step = 1024
    for c in range(0, width, step):
        placed = nn(put, flat_ref[:, c : c + step]).astype(BF16)
        for j, block in enumerate(blocks):
            block[:, c : c + step] = placed[j * per_block : (j + 1) * per_block]
    square = (requests, requests)
    length_column = jnp.sum(
        jnp.where(iota(square, 0) == iota(square, 1), length_ref[...], 0), axis=1, keepdims=True
    )
    lengths = jnp.broadcast_to(length_column.astype(F32), (requests, LANES)).astype(BF16)
    placed = nn(put_x, lengths).astype(BF16)
    for j, block in enumerate(blocks):
        block[:, width:] = placed[j * per_block : (j + 1) * per_block]


def stacked(blocks, columns):
    return jnp.concatenate([block[:, columns] for block in blocks], axis=0)


def stage_kernel(wq_hbm, wk_hbm, wv_hbm, down_hbm, up_hbm, kv_up_hbm, out_down_hbm, out_up_hbm, wq_ref, narrow_ref, small_ref, up_ref, kv_up_ref, out_down_ref, sems):
    width = wq_hbm.shape[0]
    hcols = wk_hbm.shape[0]
    ranks = down_hbm.shape[0]
    pieces = 4
    pairs = [
        (up_hbm, up_ref),
        (kv_up_hbm, kv_up_ref),
        (out_down_hbm, out_down_ref),
        (out_up_hbm, small_ref.at[:, 0 : out_up_hbm.shape[1]]),
    ]
    for n in range(pieces):
        rows = pl.ds(n * (width // pieces), width // pieces)
        pairs.append((wq_hbm.at[rows, :], wq_ref.at[rows, :]))
    for n in range(2):
        rows = pl.ds(n * (ranks // 2), ranks // 2)
        pairs.append((down_hbm.at[rows, :], narrow_ref.at[pl.ds(4 * hcols + n * (ranks // 2), ranks // 2), :]))
        columns = pl.ds(n * (width // 2), width // 2)
        for m, source in enumerate((wk_hbm, wv_hbm)):
            target = narrow_ref.at[pl.ds((2 * n + m) * hcols, hcols), :]
            pairs.append((source.at[:, columns], target))
    copies = copy_all(pairs, sems)
    for copy in copies[:3]:
        copy.wait()
    small_ref[:, out_up_hbm.shape[1] :] = jnp.concatenate(
        [up_ref[...], kv_up_ref[0], kv_up_ref[1], out_down_ref[...]], axis=1
    )
    for copy in copies[3:]:
        copy.wait()


def project_kernel(count, *refs):
    blocks = refs[: 2 * count]
    wq_ref, narrow_ref, mine_ref, theirs_ref, sums_ref = refs[2 * count :]
    width = wq_ref.shape[0]
    half = narrow_ref.shape[1]
    slots = mine_ref.shape[0]
    rows = sums_ref.shape[1]
    kvcols = LANES
    x_all = stacked(blocks, slice(0, width))
    narrow = nt(jnp.concatenate([x_all[:, :half], x_all[:, half:]], axis=0), narrow_ref[...])
    early, late = narrow[:rows], narrow[rows:]
    ranks = jnp.where(lax.axis_index("tensor") == 0, early[:, 2 * kvcols :], late[:, 2 * kvcols :])
    spare = jnp.zeros((rows, -ranks.shape[1] % LANES), F32)
    sums = [
        nn(x_all, wq_ref[...]),
        early[:, :kvcols] + late[:, kvcols : 2 * kvcols],
        jnp.concatenate([ranks, spare], axis=1),
    ]
    tile = 0
    for part in sums:
        for c in range(0, part.shape[1], LANES):
            sums_ref[tile] = part[:, c : c + LANES]
            columns = slice(tile * LANES, (tile + 1) * LANES)
            mine_ref[:, columns] = sums_ref[tile, pl.ds(0, slots, stride=2), :]
            theirs_ref[:, columns] = sums_ref[tile, pl.ds(rows // 2, slots, stride=2), :]
            tile += 1


def unpack_kernel(count, *refs):
    blocks = refs[:count]
    named_ref, table_ref, k_ref, v_ref, length_ref, cosine_ref, sine_ref, place_ref = refs[count:]
    requests, rows = place_ref.shape
    core = lax.axis_index("tensor")
    owner, standing = owner_and_standing(named_ref[...], table_ref[...])
    ahead = owner - lax.axis_index("adapter")
    near, far = block_of(ahead, core, count), block_of(ahead, 1 - core, count)
    back = rows // (2 * count)
    source = jnp.where(near < 0, count + far, near) * back + core * (back // 2) + standing
    square = (requests, requests)
    source = jnp.sum(
        jnp.where(iota(square, 0) == iota(square, 1), source, 0), axis=1, keepdims=True
    )
    place_ref[...] = ones_where(iota((requests, rows), 1) == source)
    slots = length_ref.shape[0]
    per_block = blocks[0].shape[0]
    positions = k_ref.shape[0] // slots
    width = 2 * positions * LANES
    together = GROUP // (per_block // 2)
    pick = iota((GROUP, 2 * GROUP), 1) - 2 * iota((GROUP, 2 * GROUP), 0)
    pick_x, pick_kv = ones_where(pick == 0), ones_where(pick == 1)
    step = 1024
    for g in range(slots // GROUP):
        members = blocks[g * together : (g + 1) * together]
        for c in range(0, width, step):
            picked = nn(pick_kv, stacked(members, slice(c, c + step))).astype(BF16)
            for j in range(step // LANES):
                p = c // LANES + j
                target, p = (k_ref, p) if p < positions else (v_ref, p - positions)
                first = (g * positions + p) * GROUP
                target[first : first + GROUP, :] = picked[:, j * LANES : (j + 1) * LANES]
        length_ref[g * GROUP : (g + 1) * GROUP, :] = nn(
            pick_x, stacked(members, slice(width, width + LANES))
        )
    halfway = HEAD_SIZE // 2
    lane = iota((slots, LANES), 1)
    exponent = (lane % halfway).astype(F32) * (-math.log(THETA) / halfway)
    angle = length_ref[...] * jnp.exp(exponent)
    cosine_ref[...] = jnp.cos(angle)
    sine = jnp.sin(angle)
    sine_ref[...] = jnp.where(lane < halfway, -sine, sine)


def attend_kernel(mine_ref, theirs_ref, small_ref, small_other_ref, k_ref, v_ref, length_ref, cosine_ref, sine_ref, out_ref):
    core = lax.axis_index("tensor")
    slots = mine_ref.shape[0]
    rank = small_ref.shape[0]
    kvcols = LANES
    qcols = out_ref.shape[1] // 2
    heads = 2 * qcols // HEAD_SIZE
    halfway = HEAD_SIZE // 2
    both = qcols + kvcols
    base = small_ref.shape[1] - both - qcols
    mine = mine_ref[...]
    theirs = theirs_ref[...]
    ranks = (mine + theirs)[:, both : both + 3 * rank].astype(BF16)
    ranks = [ranks[:, n * rank : (n + 1) * rank] for n in range(3)]

    def added(projected, up_ref):
        change = jnp.concatenate(
            [
                nn(ranks[0], up_ref[:, base : base + qcols]),
                nn(ranks[1], up_ref[:, base + qcols : base + qcols + halfway]),
                nn(ranks[2], up_ref[:, base + qcols + halfway : base + both]),
            ],
            axis=1,
        )
        return projected[:, :both] + change.astype(BF16).astype(F32)

    mine = added(mine, small_ref)
    theirs = added(theirs, small_other_ref)
    combined = jnp.concatenate([mine[:, :qcols], theirs[:, :qcols]], axis=1)
    cosine, sine = cosine_ref[...], sine_ref[...]

    def rotate(part):
        return part * cosine + pltpu.roll(part, halfway, 1) * sine

    queries = [
        rotate(combined[:, h * HEAD_SIZE : (h + 1) * HEAD_SIZE]).astype(BF16) for h in range(heads)
    ]
    kv_mine = mine[:, qcols:]
    kv_theirs = theirs[:, qcols:]
    leading = jnp.where(core == 0, kv_mine, kv_theirs)
    trailing = jnp.where(core == 0, kv_theirs, kv_mine)
    first = iota((slots, LANES), 1) < halfway
    own_keys = rotate(jnp.where(first, leading, pltpu.roll(trailing, halfway, 1))).astype(BF16)
    own_values = jnp.where(first, pltpu.roll(leading, halfway, 1), trailing).astype(BF16)

    cached = k_ref.shape[0] * GROUP // slots
    rows = heads * GROUP
    shrink = math.sqrt(HEAD_SIZE)
    column = iota((rows, cached), 1)
    same = column % GROUP == iota((rows, cached), 0) % GROUP
    position = column // GROUP
    own = iota((rows, GROUP), 1) == iota((rows, GROUP), 0) % GROUP
    for g in range(slots // GROUP):
        members = slice(g * GROUP, (g + 1) * GROUP)
        held = slice(g * cached, (g + 1) * cached)
        query = jnp.concatenate([part[members] for part in queries], axis=0)
        length = jnp.concatenate([length_ref[members, 0:1]] * heads, axis=0).astype(jnp.int32)
        scores = jnp.where(
            same & (position < length), nt(query, k_ref[held, :]) / shrink, -jnp.inf
        )
        own_scores = jnp.where(own, nt(query, own_keys[members]) / shrink, -jnp.inf)
        highest = jnp.maximum(
            jnp.max(scores, axis=1, keepdims=True), jnp.max(own_scores, axis=1, keepdims=True)
        )
        raised = jnp.exp(scores - highest)
        own_raised = jnp.exp(own_scores - highest)
        total = jnp.sum(raised, axis=1, keepdims=True) + jnp.sum(own_raised, axis=1, keepdims=True)
        weights = (raised / total).astype(BF16)
        own_weights = (own_raised / total).astype(BF16)
        attended = (nn(weights, v_ref[held, :]) + nn(own_weights, own_values[members])).astype(BF16)
        for h in range(heads):
            out_ref[members, h * HEAD_SIZE : (h + 1) * HEAD_SIZE] = attended[
                h * GROUP : (h + 1) * GROUP
            ]


def output_kernel(count, attended_ref, wo_ref, wo_other_ref, small_ref, small_other_ref, *blocks):
    core = lax.axis_index("tensor")
    slots, cols = attended_ref.shape
    hcols = cols // 2
    per_block, half = blocks[0].shape
    kept = per_block // 2
    rows = count * per_block
    slot = iota((rows, slots), 0)
    slot = slot // per_block * kept + slot % kept
    attended = nn(ones_where(iota((rows, slots), 1) == slot), attended_ref[...]).astype(BF16)
    left, right = attended[:, :hcols], attended[:, hcols:]
    down = slice(small_ref.shape[1] - hcols, small_ref.shape[1])
    ranks = (nt(left, small_ref[:, down]) + nt(right, small_other_ref[:, down])).astype(BF16)
    step = 1024
    side = iota((rows, step), 0) % per_block // kept
    for c in range(0, half, step):
        near, far = slice(c, c + step), slice(half + c, half + c + step)
        terms = jnp.where(
            side == 0,
            nn(left, wo_ref[:, near]) + nn(right, wo_other_ref[:, near]),
            nn(left, wo_ref[:, far]) + nn(right, wo_other_ref[:, far]),
        )
        delta = jnp.where(side == core, nn(ranks, small_ref[:, near]), nn(ranks, small_other_ref[:, near]))
        done = (terms + delta.astype(BF16).astype(F32)).astype(BF16)
        for j, block in enumerate(blocks):
            block[:, near] = done[j * per_block : (j + 1) * per_block]


def pick_kernel(place_ref, *refs):
    blocks, out_ref = refs[:-1], refs[-1]
    step = 1024
    for c in range(0, out_ref.shape[1], step):
        out_ref[:, c : c + step] = nn(place_ref[...], stacked(blocks, slice(c, c + step))).astype(BF16)


OUTSIDE = pl.BlockSpec(memory_space=pltpu.HBM)
INSIDE = pl.BlockSpec(memory_space=pltpu.VMEM)


def call(kernel, outs, scratch=(), vmem=8, outside=(), out_spec=INSIDE, moved=0):
    many = isinstance(outs, (list, tuple))
    return lambda *args: pl.pallas_call(
        kernel,
        out_shape=outs,
        in_specs=[OUTSIDE if i in outside else INSIDE for i in range(len(args))],
        out_specs=[out_spec] * len(outs) if many else out_spec,
        scratch_shapes=list(scratch),
        compiler_params=pltpu.CompilerParams(vmem_limit_bytes=vmem * MIB),
        cost_estimate=pl.CostEstimate(flops=0, bytes_accessed=moved, transcendentals=0),
    )(
        *[
            pltpu.with_memory_space_constraint(arg, pltpu.HBM) if i in outside else arg
            for i, arg in enumerate(args)
        ]
    )


def body(
    layer_input,
    input_norm_gain,
    query_projection,
    key_projection,
    value_projection,
    output_projection,
    cached_key_rows,
    cached_value_rows,
    request_adapter,
    adapter_row_table,
    cached_length,
    projection_adapter_down,
    query_adapter_up,
    key_value_adapter_up,
    output_adapter_down,
    output_adapter_up,
):
    shape = jax.ShapeDtypeStruct
    requests, width = layer_input.shape
    owners = lax.axis_size("adapter")
    adapters = adapter_row_table.shape[0]
    positions = cached_key_rows.shape[1]
    half = width // 2
    capacity = max(2, 2 * ((requests + adapters - 1) // adapters))
    count = owners // 2
    kept = (capacity + 3) // 4 * 4
    slots = count * kept
    block = shape((2 * kept, width + LANES), BF16)
    named = request_adapter.reshape(1, requests)
    table = adapter_row_table.reshape(1, adapters)

    rank, qcols = query_adapter_up.shape[1:]
    hcols = key_value_adapter_up.shape[3]
    hrows = output_projection.shape[0]
    packed = call(
        functools.partial(pack_kernel, capacity),
        [block] * count,
        [
            pltpu.VMEM((requests, width), BF16),
            pltpu.VMEM((1, width), F32),
            pltpu.VMEM((positions * requests, LANES), BF16),
            pltpu.VMEM((positions * requests, LANES), BF16),
            pltpu.VMEM((1, requests), jnp.int32),
            pltpu.VMEM((1, adapters), jnp.int32),
            pltpu.VMEM((1, requests), jnp.int32),
            pltpu.VMEM((2 * requests, width), BF16),
            pltpu.VMEM((positions * requests, LANES), F32),
            pltpu.SemaphoreType.DMA((7,)),
        ],
        outside=range(7),
    )(
        layer_input,
        input_norm_gain.reshape(1, width),
        cached_key_rows.reshape(requests * positions, HEAD_SIZE),
        cached_value_rows.reshape(requests * positions, HEAD_SIZE),
        named,
        table,
        cached_length.reshape(1, requests),
    )
    down = projection_adapter_down[0].T
    wk, wv = key_projection.T, value_projection.T
    kvcols = 2 * wk.shape[0]
    *packed, query_projection, wk, wv, down = lax.optimization_barrier(
        (*packed, query_projection, wk, wv, down)
    )
    *weights, small = call(
        stage_kernel,
        [
            shape(query_projection.shape, BF16),
            shape((2 * kvcols + down.shape[0], half), BF16),
            shape((rank, half + qcols + 2 * hcols + hrows), BF16),
        ],
        [
            pltpu.VMEM((rank, qcols), BF16),
            pltpu.VMEM((2, rank, hcols), BF16),
            pltpu.VMEM((rank, hrows), BF16),
            pltpu.SemaphoreType.DMA((14,)),
        ],
        outside=range(8),
        moved=2 * (query_projection.size + kvcols * width + down.size),
    )(
        query_projection,
        wk,
        wv,
        down,
        query_adapter_up[0],
        key_value_adapter_up[0],
        output_adapter_down[0].T,
        output_adapter_up[0],
    )

    def onward(n):
        near, far = [turns[n] if n < len(turns) else n for turns in TURNS]
        shifts = (count - 1 - near, count + far)
        return [
            (a * 2 + t, (a + shifts[t]) % owners * 2 + t) for a in range(owners) for t in range(2)
        ]

    arrived = [
        lax.ppermute(one, ("adapter", "tensor"), onward(n)) for n, one in enumerate(packed)
    ]
    arrived[0], *weights = lax.optimization_barrier((arrived[0], *weights))
    passed = [lax.ppermute(one, "tensor", SWAP) for one in arrived]
    wo_other = lax.ppermute(output_projection, "tensor", SWAP)
    pcols = qcols + kvcols + (down.shape[0] + LANES - 1) // LANES * LANES
    mine, theirs = call(
        functools.partial(project_kernel, count),
        [shape((slots, pcols), F32), shape((slots, pcols), F32)],
        [pltpu.VMEM((pcols // LANES, 4 * slots, LANES), F32)],
        vmem=24,
    )(*arrived, *passed, *weights)
    theirs, mine, small = lax.optimization_barrier((theirs, mine, small))
    theirs = lax.ppermute(theirs, "tensor", SWAP)
    small_other = lax.ppermute(small, "tensor", SWAP)
    keys, values, lengths, cosine, sine, place = call(
        functools.partial(unpack_kernel, count),
        [shape((slots * positions, HEAD_SIZE), BF16)] * 2
        + [shape((slots, LANES), F32)] * 3
        + [shape((requests, 4 * slots), BF16)],
    )(*arrived, named, table)
    attended = call(attend_kernel, shape((slots, 2 * qcols), BF16), vmem=16)(
        mine, theirs, small, small_other, keys, values, lengths, cosine, sine
    )
    finished = call(
        functools.partial(output_kernel, count),
        [shape((2 * kept, half), BF16)] * count,
        vmem=16,
    )(attended, output_projection, wo_other, small, small_other)
    returned = [
        lax.ppermute(one, ("adapter", "tensor"), [(b, a) for a, b in onward(n)])
        for n, one in enumerate(finished)
    ]
    waited = list(returned)
    for n in reversed(range(count - 1)):
        waited[n] = lax.optimization_barrier((returned[n], returned[n + 1]))[0]
    returned += [lax.ppermute(one, "tensor", SWAP) for one in waited]
    return call(pick_kernel, shape((requests, half), BF16))(place, *returned)


def solution(mesh):
    placed = (
        P(("groups", "adapter"), None),
        P(),
        P(None, "tensor"),
        P(None, "tensor"),
        P(None, "tensor"),
        P("tensor", None),
        P(("groups", "adapter"), None, None),
        P(("groups", "adapter"), None, None),
        P(("groups", "adapter"), None),
        P(),
        P(("groups", "adapter")),
        P("adapter", "tensor", None),
        P("adapter", None, "tensor"),
        P("adapter", None, None, "tensor"),
        P("adapter", "tensor", None),
        P("adapter", None, "tensor"),
    )
    return jax.shard_map(
        body,
        mesh=mesh,
        in_specs=placed,
        out_specs=P(("groups", "adapter"), "tensor"),
        check_vma=False,
    )
```

```python
import functools
import math

import jax
import jax.numpy as jnp
from jax import lax
from jax.experimental import pallas as pl
from jax.experimental.pallas import tpu as pltpu
from jax.sharding import PartitionSpec as P

HEAD_SIZE = 128
LANES = 128
EPSILON = 1e-05
THETA = 500000.0
BF16 = jnp.bfloat16
F32 = jnp.float32
SWAP = [(0, 1), (1, 0)]
GROUP = 16
MIB = 1024 * 1024


def nn(a, b):
    return lax.dot_general(a, b, (((1,), (0,)), ((), ())), preferred_element_type=F32)


def nt(a, b):
    return lax.dot_general(a, b, (((1,), (1,)), ((), ())), preferred_element_type=F32)


def iota(shape, dim):
    return lax.broadcasted_iota(jnp.int32, shape, dim)


def ones_where(condition):
    return jnp.where(condition, 1.0, 0.0).astype(BF16)


def owner_and_standing(named, table):
    requests, adapters = named.shape[1], table.shape[1]
    table_column = jnp.sum(
        jnp.where(iota((adapters, adapters), 0) == iota((adapters, adapters), 1), table, 0),
        axis=1,
        keepdims=True,
    )
    owner = jnp.sum(
        jnp.where(iota((adapters, requests), 0) == named, table_column, 0), axis=0, keepdims=True
    )
    square = (requests, requests)
    owner_column = jnp.sum(
        jnp.where(iota(square, 0) == iota(square, 1), owner, 0), axis=1, keepdims=True
    )
    earlier = (owner_column == owner) & (iota(square, 0) < iota(square, 1))
    standing = jnp.sum(jnp.where(earlier, 1, 0), axis=0, keepdims=True)
    return owner, standing


def copy_all(pairs, sems):
    copies = [pltpu.make_async_copy(a, b, sems.at[i]) for i, (a, b) in enumerate(pairs)]
    for copy in copies:
        copy.start()
    return copies


TURNS = ((1, 0, 2, 3), (0, 1, 3, 2))


def turn_of(distance, turns):
    turn = distance
    for n, one in enumerate(turns):
        turn = jnp.where(distance == one, n, turn)
    return turn


def block_of(ahead, core, count):
    ahead = jnp.where(ahead < 0, ahead + 2 * count, ahead)
    return jnp.where(ahead // count == core,
        jnp.where(
            core == 0,
            turn_of(count - 1 - ahead, TURNS[0]),
            turn_of(ahead - count, TURNS[1]),
        ), -1)


def pack_kernel(capacity, x_hbm, gain_hbm, k_hbm, v_hbm, named_hbm, table_hbm, length_hbm, *rest):
    x_ref, gain_ref, k_ref, v_ref, named_ref, table_ref, length_ref, flat_ref, spread_ref, sems = rest[-10:]
    blocks = rest[:-10]
    count = len(blocks)
    owners = 2 * count
    named_copy, table_copy, length_copy, x_copy, gain_copy, k_copy, v_copy = copy_all(
        [
            (named_hbm, named_ref),
            (table_hbm, table_ref),
            (length_hbm, length_ref),
            (x_hbm, x_ref),
            (gain_hbm, gain_ref),
            (k_hbm, k_ref),
            (v_hbm, v_ref),
        ],
        sems,
    )
    requests, width = x_ref.shape
    positions = k_ref.shape[0] // requests
    per_block = blocks[0].shape[0]
    rows = per_block * count
    named_copy.wait()
    table_copy.wait()
    length_copy.wait()
    owner, standing = owner_and_standing(named_ref[...], table_ref[...])
    block = block_of(owner - lax.axis_index("adapter"), lax.axis_index("tensor"), count)
    row = jnp.where(block < 0, -2, block * per_block + 2 * standing)
    order = iota((rows, requests), 0)
    put_x = ones_where(order == row)
    put_kv = ones_where(order == row + 1)
    put = jnp.concatenate([put_x, put_kv], axis=1)

    x_copy.wait()
    gain_copy.wait()
    floats = x_ref[...].astype(F32)
    scale = lax.rsqrt(jnp.mean(floats * floats, axis=1, keepdims=True) + EPSILON)
    flat_ref[0:requests, :] = (floats * scale * gain_ref[...]).astype(BF16)
    for n, (source, copy) in enumerate(((k_ref, k_copy), (v_ref, v_copy))):
        copy.wait()
        spread_ref[...] = source[...].astype(F32)
        for p in range(positions):
            to = slice((n * positions + p) * LANES, (n * positions + p + 1) * LANES)
            flat_ref[requests : 2 * requests, to] = spread_ref[
                pl.ds(p, requests, stride=positions), :
            ].astype(BF16)
    step = 2048
    for c in range(0, width, step):
        placed = nn(put, flat_ref[:, c : c + step]).astype(BF16)
        for j, block in enumerate(blocks):
            block[:, c : c + step] = placed[j * per_block : (j + 1) * per_block]
    square = (requests, requests)
    length_column = jnp.sum(
        jnp.where(iota(square, 0) == iota(square, 1), length_ref[...], 0), axis=1, keepdims=True
    )
    lengths = jnp.broadcast_to(length_column.astype(F32), (requests, LANES)).astype(BF16)
    placed = nn(put_x, lengths).astype(BF16)
    for j, block in enumerate(blocks):
        block[:, width:] = placed[j * per_block : (j + 1) * per_block]


def stacked(blocks, columns):
    return jnp.concatenate([block[:, columns] for block in blocks], axis=0)


def stage_kernel(wq_hbm, wk_hbm, wv_hbm, down_hbm, up_hbm, kv_up_hbm, out_down_hbm, out_up_hbm, wq_ref, narrow_ref, small_ref, up_ref, kv_up_ref, out_down_ref, sems):
    width = wq_hbm.shape[0]
    hcols = wk_hbm.shape[0]
    ranks = down_hbm.shape[0]
    pieces = 4
    pairs = [
        (up_hbm, up_ref),
        (kv_up_hbm, kv_up_ref),
        (out_down_hbm, out_down_ref),
        (out_up_hbm, small_ref.at[:, 0 : out_up_hbm.shape[1]]),
    ]
    for n in range(pieces):
        rows = pl.ds(n * (width // pieces), width // pieces)
        pairs.append((wq_hbm.at[rows, :], wq_ref.at[rows, :]))
    for n in range(2):
        rows = pl.ds(n * (ranks // 2), ranks // 2)
        pairs.append((down_hbm.at[rows, :], narrow_ref.at[pl.ds(4 * hcols + n * (ranks // 2), ranks // 2), :]))
        columns = pl.ds(n * (width // 2), width // 2)
        for m, source in enumerate((wk_hbm, wv_hbm)):
            target = narrow_ref.at[pl.ds((2 * n + m) * hcols, hcols), :]
            pairs.append((source.at[:, columns], target))
    copies = copy_all(pairs, sems)
    for copy in copies[:3]:
        copy.wait()
    small_ref[:, out_up_hbm.shape[1] :] = jnp.concatenate(
        [up_ref[...], kv_up_ref[0], kv_up_ref[1], out_down_ref[...]], axis=1
    )
    for copy in copies[3:]:
        copy.wait()


def project_kernel(count, *refs):
    blocks = refs[: 2 * count]
    wq_ref, narrow_ref, mine_ref, theirs_ref, sums_ref = refs[2 * count :]
    width = wq_ref.shape[0]
    half = narrow_ref.shape[1]
    slots = mine_ref.shape[0]
    rows = sums_ref.shape[1]
    kvcols = LANES
    x_all = stacked(blocks, slice(0, width))
    narrow = nt(jnp.concatenate([x_all[:, :half], x_all[:, half:]], axis=0), narrow_ref[...])
    early, late = narrow[:rows], narrow[rows:]
    ranks = jnp.where(lax.axis_index("tensor") == 0, early[:, 2 * kvcols :], late[:, 2 * kvcols :])
    spare = jnp.zeros((rows, -ranks.shape[1] % LANES), F32)
    sums = [
        nn(x_all, wq_ref[...]),
        early[:, :kvcols] + late[:, kvcols : 2 * kvcols],
        jnp.concatenate([ranks, spare], axis=1),
    ]
    tile = 0
    for part in sums:
        for c in range(0, part.shape[1], LANES):
            sums_ref[tile] = part[:, c : c + LANES]
            columns = slice(tile * LANES, (tile + 1) * LANES)
            mine_ref[:, columns] = sums_ref[tile, pl.ds(0, slots, stride=2), :]
            theirs_ref[:, columns] = sums_ref[tile, pl.ds(rows // 2, slots, stride=2), :]
            tile += 1


def unpack_kernel(count, *refs):
    blocks = refs[:count]
    named_ref, table_ref, k_ref, v_ref, length_ref, cosine_ref, sine_ref, place_ref = refs[count:]
    requests, rows = place_ref.shape
    core = lax.axis_index("tensor")
    owner, standing = owner_and_standing(named_ref[...], table_ref[...])
    ahead = owner - lax.axis_index("adapter")
    near, far = block_of(ahead, core, count), block_of(ahead, 1 - core, count)
    back = rows // (2 * count)
    source = jnp.where(near < 0, count + far, near) * back + core * (back // 2) + standing
    square = (requests, requests)
    source = jnp.sum(
        jnp.where(iota(square, 0) == iota(square, 1), source, 0), axis=1, keepdims=True
    )
    place_ref[...] = ones_where(iota((requests, rows), 1) == source)
    slots = length_ref.shape[0]
    per_block = blocks[0].shape[0]
    positions = k_ref.shape[0] // slots
    width = 2 * positions * LANES
    together = GROUP // (per_block // 2)
    pick = iota((GROUP, 2 * GROUP), 1) - 2 * iota((GROUP, 2 * GROUP), 0)
    pick_x, pick_kv = ones_where(pick == 0), ones_where(pick == 1)
    step = 2048
    for g in range(slots // GROUP):
        members = blocks[g * together : (g + 1) * together]
        for c in range(0, width, step):
            picked = nn(pick_kv, stacked(members, slice(c, c + step))).astype(BF16)
            for j in range(step // LANES):
                p = c // LANES + j
                target, p = (k_ref, p) if p < positions else (v_ref, p - positions)
                first = (g * positions + p) * GROUP
                target[first : first + GROUP, :] = picked[:, j * LANES : (j + 1) * LANES]
        length_ref[g * GROUP : (g + 1) * GROUP, :] = nn(
            pick_x, stacked(members, slice(width, width + LANES))
        )
    halfway = HEAD_SIZE // 2
    lane = iota((slots, LANES), 1)
    exponent = (lane % halfway).astype(F32) * (-math.log(THETA) / halfway)
    angle = length_ref[...] * jnp.exp(exponent)
    cosine_ref[...] = jnp.cos(angle)
    sine = jnp.sin(angle)
    sine_ref[...] = jnp.where(lane < halfway, -sine, sine)


def attend_kernel(mine_ref, theirs_ref, small_ref, small_other_ref, k_ref, v_ref, length_ref, cosine_ref, sine_ref, out_ref):
    core = lax.axis_index("tensor")
    slots = mine_ref.shape[0]
    rank = small_ref.shape[0]
    kvcols = LANES
    qcols = out_ref.shape[1] // 2
    heads = 2 * qcols // HEAD_SIZE
    halfway = HEAD_SIZE // 2
    both = qcols + kvcols
    base = small_ref.shape[1] - both - qcols
    mine = mine_ref[...]
    theirs = theirs_ref[...]
    ranks = (mine + theirs)[:, both : both + 3 * rank].astype(BF16)
    ranks = [ranks[:, n * rank : (n + 1) * rank] for n in range(3)]

    def added(projected, up_ref):
        change = jnp.concatenate(
            [
                nn(ranks[0], up_ref[:, base : base + qcols]),
                nn(ranks[1], up_ref[:, base + qcols : base + qcols + halfway]),
                nn(ranks[2], up_ref[:, base + qcols + halfway : base + both]),
            ],
            axis=1,
        )
        return projected[:, :both] + change.astype(BF16).astype(F32)

    mine = added(mine, small_ref)
    theirs = added(theirs, small_other_ref)
    combined = jnp.concatenate([mine[:, :qcols], theirs[:, :qcols]], axis=1)
    cosine, sine = cosine_ref[...], sine_ref[...]

    def rotate(part):
        return part * cosine + pltpu.roll(part, halfway, 1) * sine

    queries = [
        rotate(combined[:, h * HEAD_SIZE : (h + 1) * HEAD_SIZE]).astype(BF16) for h in range(heads)
    ]
    kv_mine = mine[:, qcols:]
    kv_theirs = theirs[:, qcols:]
    leading = jnp.where(core == 0, kv_mine, kv_theirs)
    trailing = jnp.where(core == 0, kv_theirs, kv_mine)
    first = iota((slots, LANES), 1) < halfway
    own_keys = rotate(jnp.where(first, leading, pltpu.roll(trailing, halfway, 1))).astype(BF16)
    own_values = jnp.where(first, pltpu.roll(leading, halfway, 1), trailing).astype(BF16)

    cached = k_ref.shape[0] * GROUP // slots
    rows = heads * GROUP
    shrink = math.sqrt(HEAD_SIZE)
    column = iota((rows, cached), 1)
    same = column % GROUP == iota((rows, cached), 0) % GROUP
    position = column // GROUP
    own = iota((rows, GROUP), 1) == iota((rows, GROUP), 0) % GROUP
    for g in range(slots // GROUP):
        members = slice(g * GROUP, (g + 1) * GROUP)
        held = slice(g * cached, (g + 1) * cached)
        query = jnp.concatenate([part[members] for part in queries], axis=0)
        length = jnp.concatenate([length_ref[members, 0:1]] * heads, axis=0).astype(jnp.int32)
        scores = jnp.where(
            same & (position < length), nt(query, k_ref[held, :]) / shrink, -jnp.inf
        )
        own_scores = jnp.where(own, nt(query, own_keys[members]) / shrink, -jnp.inf)
        highest = jnp.maximum(
            jnp.max(scores, axis=1, keepdims=True), jnp.max(own_scores, axis=1, keepdims=True)
        )
        raised = jnp.exp(scores - highest)
        own_raised = jnp.exp(own_scores - highest)
        total = jnp.sum(raised, axis=1, keepdims=True) + jnp.sum(own_raised, axis=1, keepdims=True)
        weights = (raised / total).astype(BF16)
        own_weights = (own_raised / total).astype(BF16)
        attended = (nn(weights, v_ref[held, :]) + nn(own_weights, own_values[members])).astype(BF16)
        for h in range(heads):
            out_ref[members, h * HEAD_SIZE : (h + 1) * HEAD_SIZE] = attended[
                h * GROUP : (h + 1) * GROUP
            ]


def output_kernel(count, attended_ref, wo_ref, wo_other_ref, small_ref, small_other_ref, *blocks):
    core = lax.axis_index("tensor")
    slots, cols = attended_ref.shape
    hcols = cols // 2
    per_block, half = blocks[0].shape
    kept = per_block // 2
    rows = count * per_block
    slot = iota((rows, slots), 0)
    slot = slot // per_block * kept + slot % kept
    attended = nn(ones_where(iota((rows, slots), 1) == slot), attended_ref[...]).astype(BF16)
    left, right = attended[:, :hcols], attended[:, hcols:]
    down = slice(small_ref.shape[1] - hcols, small_ref.shape[1])
    ranks = (nt(left, small_ref[:, down]) + nt(right, small_other_ref[:, down])).astype(BF16)
    step = 2048
    side = iota((rows, step), 0) % per_block // kept
    for c in range(0, half, step):
        near, far = slice(c, c + step), slice(half + c, half + c + step)
        terms = jnp.where(
            side == 0,
            nn(left, wo_ref[:, near]) + nn(right, wo_other_ref[:, near]),
            nn(left, wo_ref[:, far]) + nn(right, wo_other_ref[:, far]),
        )
        delta = jnp.where(side == core, nn(ranks, small_ref[:, near]), nn(ranks, small_other_ref[:, near]))
        done = (terms + delta.astype(BF16).astype(F32)).astype(BF16)
        for j, block in enumerate(blocks):
            block[:, near] = done[j * per_block : (j + 1) * per_block]


def pick_kernel(place_ref, *refs):
    blocks, out_ref = refs[:-1], refs[-1]
    step = 2048
    for c in range(0, out_ref.shape[1], step):
        out_ref[:, c : c + step] = nn(place_ref[...], stacked(blocks, slice(c, c + step))).astype(BF16)


OUTSIDE = pl.BlockSpec(memory_space=pltpu.HBM)
INSIDE = pl.BlockSpec(memory_space=pltpu.VMEM)


def call(kernel, outs, scratch=(), vmem=8, outside=(), out_spec=INSIDE, moved=0):
    many = isinstance(outs, (list, tuple))
    return lambda *args: pl.pallas_call(
        kernel,
        out_shape=outs,
        in_specs=[OUTSIDE if i in outside else INSIDE for i in range(len(args))],
        out_specs=[out_spec] * len(outs) if many else out_spec,
        scratch_shapes=list(scratch),
        compiler_params=pltpu.CompilerParams(vmem_limit_bytes=vmem * MIB),
        cost_estimate=pl.CostEstimate(flops=0, bytes_accessed=moved, transcendentals=0),
    )(
        *[
            pltpu.with_memory_space_constraint(arg, pltpu.HBM) if i in outside else arg
            for i, arg in enumerate(args)
        ]
    )


def body(
    layer_input,
    input_norm_gain,
    query_projection,
    key_projection,
    value_projection,
    output_projection,
    cached_key_rows,
    cached_value_rows,
    request_adapter,
    adapter_row_table,
    cached_length,
    projection_adapter_down,
    query_adapter_up,
    key_value_adapter_up,
    output_adapter_down,
    output_adapter_up,
):
    shape = jax.ShapeDtypeStruct
    requests, width = layer_input.shape
    owners = lax.axis_size("adapter")
    adapters = adapter_row_table.shape[0]
    positions = cached_key_rows.shape[1]
    half = width // 2
    capacity = max(2, 2 * ((requests + adapters - 1) // adapters))
    count = owners // 2
    kept = (capacity + 3) // 4 * 4
    slots = count * kept
    block = shape((2 * kept, width + LANES), BF16)
    named = request_adapter.reshape(1, requests)
    table = adapter_row_table.reshape(1, adapters)

    rank, qcols = query_adapter_up.shape[1:]
    hcols = key_value_adapter_up.shape[3]
    hrows = output_projection.shape[0]
    packed = call(
        functools.partial(pack_kernel, capacity),
        [block] * count,
        [
            pltpu.VMEM((requests, width), BF16),
            pltpu.VMEM((1, width), F32),
            pltpu.VMEM((positions * requests, LANES), BF16),
            pltpu.VMEM((positions * requests, LANES), BF16),
            pltpu.VMEM((1, requests), jnp.int32),
            pltpu.VMEM((1, adapters), jnp.int32),
            pltpu.VMEM((1, requests), jnp.int32),
            pltpu.VMEM((2 * requests, width), BF16),
            pltpu.VMEM((positions * requests, LANES), F32),
            pltpu.SemaphoreType.DMA((7,)),
        ],
        outside=range(7),
    )(
        layer_input,
        input_norm_gain.reshape(1, width),
        cached_key_rows.reshape(requests * positions, HEAD_SIZE),
        cached_value_rows.reshape(requests * positions, HEAD_SIZE),
        named,
        table,
        cached_length.reshape(1, requests),
    )
    down = projection_adapter_down[0].T
    wk, wv = key_projection.T, value_projection.T
    kvcols = 2 * wk.shape[0]
    *packed, query_projection, wk, wv, down = lax.optimization_barrier(
        (*packed, query_projection, wk, wv, down)
    )
    *weights, small = call(
        stage_kernel,
        [
            shape(query_projection.shape, BF16),
            shape((2 * kvcols + down.shape[0], half), BF16),
            shape((rank, half + qcols + 2 * hcols + hrows), BF16),
        ],
        [
            pltpu.VMEM((rank, qcols), BF16),
            pltpu.VMEM((2, rank, hcols), BF16),
            pltpu.VMEM((rank, hrows), BF16),
            pltpu.SemaphoreType.DMA((14,)),
        ],
        outside=range(8),
        moved=2 * (query_projection.size + kvcols * width + down.size),
    )(
        query_projection,
        wk,
        wv,
        down,
        query_adapter_up[0],
        key_value_adapter_up[0],
        output_adapter_down[0].T,
        output_adapter_up[0],
    )

    def onward(n):
        near, far = [turns[n] if n < len(turns) else n for turns in TURNS]
        shifts = (count - 1 - near, count + far)
        return [
            (a * 2 + t, (a + shifts[t]) % owners * 2 + t) for a in range(owners) for t in range(2)
        ]

    arrived = [
        lax.ppermute(one, ("adapter", "tensor"), onward(n)) for n, one in enumerate(packed)
    ]
    arrived[0], *weights = lax.optimization_barrier((arrived[0], *weights))
    passed = [lax.ppermute(one, "tensor", SWAP) for one in arrived]
    wo_other = lax.ppermute(output_projection, "tensor", SWAP)
    pcols = qcols + kvcols + (down.shape[0] + LANES - 1) // LANES * LANES
    mine, theirs = call(
        functools.partial(project_kernel, count),
        [shape((slots, pcols), F32), shape((slots, pcols), F32)],
        [pltpu.VMEM((pcols // LANES, 4 * slots, LANES), F32)],
        vmem=24,
    )(*arrived, *passed, *weights)
    theirs, mine, small = lax.optimization_barrier((theirs, mine, small))
    theirs = lax.ppermute(theirs, "tensor", SWAP)
    small_other = lax.ppermute(small, "tensor", SWAP)
    keys, values, lengths, cosine, sine, place = call(
        functools.partial(unpack_kernel, count),
        [shape((slots * positions, HEAD_SIZE), BF16)] * 2
        + [shape((slots, LANES), F32)] * 3
        + [shape((requests, 4 * slots), BF16)],
    )(*arrived, named, table)
    attended = call(attend_kernel, shape((slots, 2 * qcols), BF16), vmem=16)(
        mine, theirs, small, small_other, keys, values, lengths, cosine, sine
    )
    finished = call(
        functools.partial(output_kernel, count),
        [shape((2 * kept, half), BF16)] * count,
        vmem=16,
    )(attended, output_projection, wo_other, small, small_other)
    returned = [
        lax.ppermute(one, ("adapter", "tensor"), [(b, a) for a, b in onward(n)])
        for n, one in enumerate(finished)
    ]
    waited = list(returned)
    for n in reversed(range(count - 1)):
        waited[n] = lax.optimization_barrier((returned[n], returned[n + 1]))[0]
    returned += [lax.ppermute(one, "tensor", SWAP) for one in waited]
    return call(pick_kernel, shape((requests, half), BF16))(place, *returned)


def solution(mesh):
    placed = (
        P(("groups", "adapter"), None),
        P(),
        P(None, "tensor"),
        P(None, "tensor"),
        P(None, "tensor"),
        P("tensor", None),
        P(("groups", "adapter"), None, None),
        P(("groups", "adapter"), None, None),
        P(("groups", "adapter"), None),
        P(),
        P(("groups", "adapter")),
        P("adapter", "tensor", None),
        P("adapter", None, "tensor"),
        P("adapter", None, None, "tensor"),
        P("adapter", "tensor", None),
        P("adapter", None, "tensor"),
    )
    return jax.shard_map(
        body,
        mesh=mesh,
        in_specs=placed,
        out_specs=P(("groups", "adapter"), "tensor"),
        check_vma=False,
    )
```
